32 devices in a mesh: shard: 4 (over y, core), ctx: 2 (over x), tp: 4 (over z).
Axes of the slice: x: 2, y: 2, z: 4, core: 2. Of those that a mesh axis runs over, the one named last changes fastest.
Arguments:
- tokens: bfloat16 [2, 4, 2048, 768], P(None, 'shard', 'ctx'), may hold values from -6 to 6
- segments: int32 [2, 4, 2048], P(None, 'shard', 'ctx'), may hold values from 0 to 5, never falling along the last dimension, each value on 1 to 800 neighbouring positions
- query_weight: bfloat16 [768, 768], P(('shard', 'ctx'), 'tp'), may hold values from -0.21875 to 0.21875
- key_weight: bfloat16 [768, 768], P(('shard', 'ctx'), 'tp'), may hold values from -0.21875 to 0.21875
- value_weight: bfloat16 [768, 768], P(('shard', 'ctx'), 'tp'), may hold values from -0.21875 to 0.21875
- output_weight: bfloat16 [768, 768], P('tp', ('shard', 'ctx')), may hold values from -1.75 to 1.75
- attn_gain: bfloat16 [768], P(('shard', 'ctx')), may hold values from 0.5 to 1.5
- attn_shift: bfloat16 [768], P(('shard', 'ctx')), may hold values from -3 to 3
- inner_weight: bfloat16 [768, 3072], P(('shard', 'ctx'), 'tp'), may hold values from -0.21875 to 0.21875
- outer_weight: bfloat16 [3072, 768], P('tp', ('shard', 'ctx')), may hold values from -0.21875 to 0.21875
- ffn_gain: bfloat16 [768], P(('shard', 'ctx')), may hold values from 0.5 to 1.5
- ffn_shift: bfloat16 [768], P(('shard', 'ctx')), may hold values from -3 to 3
- proj_weight: bfloat16 [768, 128], P(('shard', 'ctx')), may hold values from -0.21875 to 0.21875
- grad_embed: bfloat16 [2, 4, 2048, 128], P(None, 'shard', 'ctx'), may hold values from -48 to 48
Outputs:
- embeddings: float32 [2, 4, 2048, 128], P(None, 'shard', ('ctx', 'tp'))
- grad_tokens: float32 [2, 4, 2048, 768], P(None, 'shard', 'ctx', 'tp')
- query_grad: float32 [768, 768], P(('shard', 'ctx'), 'tp')
- key_grad: float32 [768, 768], P(('shard', 'ctx'), 'tp')
- value_grad: float32 [768, 768], P(('shard', 'ctx'), 'tp')
- output_grad: float32 [768, 768], P('tp', ('shard', 'ctx'))
- attn_gain_grad: float32 [768], P(('shard', 'ctx'))
- attn_shift_grad: float32 [768], P(('shard', 'ctx'))
- inner_grad: float32 [768, 3072], P(('shard', 'ctx'), 'tp')
- outer_grad: float32 [3072, 768], P('tp', ('shard', 'ctx'))
- ffn_gain_grad: float32 [768], P(('shard', 'ctx'))
- ffn_shift_grad: float32 [768], P(('shard', 'ctx'))
- proj_grad: float32 [768, 128], P(('shard', 'ctx'))
The draws below stay inside these ranges and needn't reach their ends.
Inputs may be any that keep to these rules, and one draw needn't show every extreme that they name: `segments`: within each sequence the document numbers never fall; each of the 6 documents spans 1 to 800 tokens and one spans exactly 800.
All inputs are finite; a program needn't handle non-finite values.
Results may differ from the reference program's by a relative error of at most 0.02.
Values may be sent and summed in bfloat16 or wider, within the bound.
No kernel may reach another device: no remote copies, remote signals or barrier semaphores. Data moves between devices by JAX's collectives and lax.ppermute only.
A program may use at most 192 MiB of HBM per device.

```python
import math
import jax
import jax.numpy as jnp
import numpy as np
from jax import lax

D = 768
HEADS = 12
DH = 64
FF = 3072
P_SIZE = 128
SEQ = 2048
MICRO = 2
SEG_COUNT = 6
SEG_MOST = 800
BATCH = 4


def levels(key, extent, cuts, least, largest):
    factor_of, own = 1.0, jax.random.fold_in(key, 6)
    for dim, shards_of in cuts:
        steps = jnp.exp(jax.random.uniform(jax.random.fold_in(own, dim), (shards_of,), jnp.float32, least / len(cuts), largest / len(cuts)))
        factor_of = factor_of * jnp.repeat(steps, extent[dim] // shards_of).reshape([-1 if axis == dim else 1 for axis in range(len(extent))])
    return factor_of


def profile(number_of, total, most, slope):
    weights = [(1 << 20) // math.isqrt(standing ** slope) + 1 for standing in range(2, number_of + 1)]
    rest, given = total - most - (number_of - 1), [1] * (number_of - 1)
    while rest > 0:
        movable = [i for i in range(number_of - 1) if given[i] < most]
        pool, budget = sum([weights[i] for i in movable]), rest
        for i in movable:
            addition = min(most - given[i], max(1, budget * weights[i] // pool), rest)
            given[i] = given[i] + addition
            rest = rest - addition
    return np.array([most] + given)


def uneven_parts(stream_key, amount, total, most, slope):
    if amount == 2:
        one = jax.random.randint(stream_key, (), max(1, total - most), min(most, total - 1) + 1)
        return jnp.stack([one, total - one])
    sizes = jnp.asarray(profile(amount, total, most, slope), jnp.int32)
    twos = (amount - 1) // 2
    source_of, sink = sizes[1:1 + 2 * twos:2], sizes[2:2 + 2 * twos:2]
    margin = jnp.minimum(source_of - 1, most - sink)
    passed = jax.random.randint(jax.random.fold_in(stream_key, 1), (twos,), 0, 1 << 20) % (margin + 1)
    sizes = sizes.at[1:1 + 2 * twos:2].set(source_of - passed).at[2:2 + 2 * twos:2].set(sink + passed)
    return sizes[jax.random.permutation(jax.random.fold_in(stream_key, 2), amount)]


def noise(rng, extent, spread, reach, shards=(), dtype=jnp.bfloat16):
    result = jax.random.normal(rng, extent, jnp.float32) * spread
    if len(shards) > 0:
        result = levels(rng, extent, shards, -0.22, 0.18) * result
    return jnp.clip(result, min=-reach, max=reach).astype(dtype)


def setup_inputs(seed: int = 0) -> dict:
    streams_of = jax.random.split(jax.random.key(seed), 15)
    tokens = noise(streams_of[0], (MICRO, BATCH, SEQ, D), 1.0, 6.0, ((1, 4), (2, 2)))
    segments = jax.vmap(lambda own: jnp.searchsorted(jnp.cumsum(uneven_parts(own, SEG_COUNT, SEQ, SEG_MOST, 1)), jnp.arange(SEQ), side="right"))(jax.random.split(streams_of[1], MICRO * BATCH)).reshape((MICRO, BATCH, SEQ)).astype(jnp.int32)
    query_weight = noise(streams_of[2], (D, D), D ** -0.5, 0.21875, ((0, 8), (1, 4)))
    key_weight = noise(streams_of[3], (D, D), D ** -0.5, 0.21875, ((0, 8), (1, 4)))
    value_weight = noise(streams_of[4], (D, D), D ** -0.5, 0.21875, ((0, 8), (1, 4)))
    output_weight = noise(streams_of[5], (D, D), (D // 64) ** -0.5, 1.75, ((0, 4), (1, 8)))
    attn_gain = jnp.clip(1.0 + 0.1 * jax.random.normal(streams_of[6], (D,), jnp.float32), 0.5, 1.5).astype(jnp.bfloat16)
    attn_shift = noise(streams_of[7], (D,), 0.5, 3.0, ((0, 8),))
    inner_weight = noise(streams_of[8], (D, FF), D ** -0.5, 0.21875, ((0, 8), (1, 4)))
    outer_weight = noise(streams_of[9], (FF, D), (FF // 4) ** -0.5, 0.21875, ((0, 4), (1, 8)))
    ffn_gain = jnp.clip(1.0 + 0.1 * jax.random.normal(streams_of[10], (D,), jnp.float32), 0.5, 1.5).astype(jnp.bfloat16)
    ffn_shift = noise(streams_of[11], (D,), 0.5, 3.0, ((0, 8),))
    proj_weight = noise(streams_of[12], (D, P_SIZE), D ** -0.5, 0.21875, ((0, 8),))
    grad_embed = noise(streams_of[13], (MICRO, BATCH, SEQ, P_SIZE), 8.0, 48.0, ((1, 4), (2, 2)))
    return {"tokens": tokens, "segments": segments, "query_weight": query_weight, "key_weight": key_weight, "value_weight": value_weight, "output_weight": output_weight, "attn_gain": attn_gain, "attn_shift": attn_shift, "inner_weight": inner_weight, "outer_weight": outer_weight, "ffn_gain": ffn_gain, "ffn_shift": ffn_shift, "proj_weight": proj_weight, "grad_embed": grad_embed}


@jax.custom_vjp
def low(v):
    return lax.optimization_barrier(v.astype(jnp.bfloat16)).astype(jnp.float32)

@jax.custom_vjp
def low_back(v):
    return v

def low_keep(v):
    return (low(v), None)

def low_pass(kept, grad):
    return (grad,)

def back_keep(v):
    return (v, None)

def back_low(kept, grad):
    return (low(grad),)
low.defvjp(low_keep, low_pass)
low_back.defvjp(back_keep, back_low)
eps_norm = 1e-12
eps_unit = 1e-06
mask_fill = -1e+30

def precise(first_op, second_op):
    return jnp.dot(first_op, second_op, precision=lax.Precision.HIGHEST, preferred_element_type=jnp.float32)

def layer_norm(hidden, gain_vec, offset):
    row_mean = lax.optimization_barrier(jnp.mean(hidden, axis=-1, keepdims=True))
    centred = hidden - row_mean
    variance = lax.optimization_barrier(jnp.mean(centred * centred, axis=-1, keepdims=True))
    return centred * lax.rsqrt(variance + eps_norm) * gain_vec + offset

def forward(tok_seq, seg_seq, params):
    query_w, key_w, value_w, output_w, gain_one, shift_one, inner_w, outer_w, gain_two, shift_two, proj_w = params
    length = tok_seq.shape[0]
    queries = low(low_back(precise(tok_seq, query_w))).reshape(length, HEADS, DH)
    keys_all = low(low_back(precise(tok_seq, key_w))).reshape(length, HEADS, DH)
    values_all = low(low_back(precise(tok_seq, value_w))).reshape(length, HEADS, DH)
    scores = low_back(jnp.einsum('qhd,khd->hqk', queries, keys_all, precision=lax.Precision.HIGHEST) * DH ** (-0.5))
    same_doc = seg_seq[:, None] == seg_seq[None, :]
    scores = jnp.where(same_doc[None], scores, mask_fill)
    probs = low(jax.nn.softmax(scores, axis=-1))
    mixed = low(low_back(jnp.einsum('hqk,khd->qhd', probs, values_all, precision=lax.Precision.HIGHEST))).reshape(length, D)
    attn_out = low_back(precise(mixed, output_w))
    first = layer_norm(tok_seq + attn_out, gain_one, shift_one)
    pre_act = low_back(precise(low(first), inner_w))
    activated = low(jax.nn.gelu(pre_act, approximate=False))
    ffn_out = low_back(precise(activated, outer_w))
    second = layer_norm(first + ffn_out, gain_two, shift_two)
    projected = low_back(precise(low(second), proj_w))
    return projected * lax.rsqrt(lax.optimization_barrier(jnp.sum(projected * projected, axis=-1, keepdims=True)) + eps_unit)

def reference(tokens, segments, query_weight, key_weight, value_weight, output_weight, attn_gain, attn_shift, inner_weight, outer_weight, ffn_gain, ffn_shift, proj_weight, grad_embed):
    params = tuple((weight.astype(jnp.float32) for weight in (query_weight, key_weight, value_weight, output_weight, attn_gain, attn_shift, inner_weight, outer_weight, ffn_gain, ffn_shift, proj_weight)))
    tok_all = tokens.reshape(-1, SEQ, D).astype(jnp.float32)
    seg_all = segments.reshape(-1, SEQ)
    cot_all = grad_embed.reshape(-1, SEQ, P_SIZE).astype(jnp.float32)

    def one_sequence(totals, inputs):
        tok_seq, seg_seq, cot_seq = inputs
        embed_seq, pull = jax.vjp(lambda tok_in, param_in: forward(tok_in, seg_seq, param_in), tok_seq, params)
        grad_tok, grad_params = pull(cot_seq)
        totals = tuple((left_val + right_val for left_val, right_val in zip(totals, grad_params)))
        return (totals, (embed_seq, grad_tok))
    zeros = tuple((jnp.zeros(weight.shape, jnp.float32) for weight in params))
    totals, (embeds, grads) = lax.scan(one_sequence, zeros, (tok_all, seg_all, cot_all))
    return (embeds.reshape(MICRO, BATCH, SEQ, P_SIZE), grads.reshape(MICRO, BATCH, SEQ, D), totals[0], totals[1], totals[2], totals[3], totals[4], totals[5], totals[6], totals[7], totals[8], totals[9], totals[10])
```

```python
import functools

import jax
import jax.numpy as jnp
from jax import lax
from jax.experimental import pallas as pl
from jax.experimental.pallas import tpu as pltpu
from jax.sharding import PartitionSpec as P

DH = 64
SEG_COUNT = 6
SEG_MOST = 800
BQ = 256
BK = 256

eps_norm = 1e-12
eps_unit = 1e-06
mask_fill = -1e30

NN = (((1,), (0,)), ((), ()))
NT = (((1,), (1,)), ((), ()))
TN = (((0,), (0,)), ((), ()))


def dot(first_op, second_op, dims=NN):
    return lax.dot_general(first_op, second_op, dims, preferred_element_type=jnp.float32)


def norm_forward(hidden, gain_vec, offset):
    row_mean = jnp.mean(hidden, axis=-1, keepdims=True)
    centred = hidden - row_mean
    variance = jnp.mean(centred * centred, axis=-1, keepdims=True)
    inv_std = lax.rsqrt(variance + eps_norm)
    normed = centred * inv_std
    return (normed * gain_vec + offset, normed, inv_std)


def norm_backward(grad_out, normed, inv_std, gain_vec):
    scaled = grad_out * gain_vec
    grad_in = inv_std * (
        scaled
        - jnp.mean(scaled, axis=-1, keepdims=True)
        - normed * jnp.mean(scaled * normed, axis=-1, keepdims=True)
    )
    return (grad_in, jnp.sum(grad_out * normed, axis=0), jnp.sum(grad_out, axis=0))


def swap(v, axis, bit):
    count = lax.axis_size(axis)
    return lax.ppermute(v, axis, [(i, i ^ bit) for i in range(count)])


def route(v, target):
    shards, halves, groups = (lax.axis_size(a) for a in ("shard", "ctx", "tp"))

    def flat(s, c, t):
        return (s * halves + c) * groups + t

    pairs = []
    for s in range(shards):
        for c in range(halves):
            for t in range(groups):
                to = target(s, c, t)
                if to is not None:
                    pairs.append((flat(s, c, t), flat(*to)))
    return lax.ppermute(v, ("shard", "ctx", "tp"), pairs)


def row_steps(order):
    shard_bits = lax.axis_size("shard").bit_length() - 1
    named = {"x": [("ctx", 1, 1 + shard_bits)], "core": [("shard", 1, shard_bits)]}
    named["y"] = [("shard", 1 << i, shard_bits - i) for i in range(1, shard_bits)]
    return [step for name in order for step in named[name]]


def my_bit(axis, bit):
    return (lax.axis_index(axis) // bit) % 2


def gather_tree(own, order, with_tp=True):
    shard_bits = lax.axis_size("shard").bit_length() - 1
    cur = own.reshape((1,) * (shard_bits + 2) + own.shape)
    if with_tp:
        t = lax.axis_index("tp")
        parts = [cur] + [swap(cur, "tp", d) for d in range(1, lax.axis_size("tp"))]
        cur = jnp.concatenate([lax.select_n(t ^ j, *parts) for j in range(len(parts))], axis=0)
    for axis, bit, dim in row_steps(order):
        other = swap(cur, axis, bit)
        first = my_bit(axis, bit) == 0
        cur = jnp.concatenate(
            [jnp.where(first, cur, other), jnp.where(first, other, cur)], axis=dim
        )
    return cur.reshape(cur.shape[0], -1, cur.shape[-1])


def scatter_tree(full, order, with_tp=True):
    shard_bits = lax.axis_size("shard").bit_length() - 1
    rows = full.shape[1] // (lax.axis_size("shard") * lax.axis_size("ctx"))
    cur = full.reshape((full.shape[0],) + (2,) * (shard_bits + 1) + (rows, full.shape[-1]))
    steps = row_steps(order)
    for axis, bit, dim in steps:
        mine = my_bit(axis, bit)
        other = swap(lax.dynamic_slice_in_dim(cur, 1 - mine, 1, dim), axis, bit)
        kept = lax.dynamic_slice_in_dim(cur, mine, 1, dim)
        cur = kept.astype(jnp.float32) + other.astype(jnp.float32)
        if with_tp or (axis, bit, dim) != steps[-1]:
            cur = cur.astype(jnp.bfloat16)
    if with_tp:
        t = lax.axis_index("tp")
        parts = [
            swap(lax.dynamic_slice_in_dim(cur, t ^ d, 1, 0), "tp", d)
            for d in range(1, lax.axis_size("tp"))
        ]
        cur = lax.dynamic_slice_in_dim(cur, t, 1, 0).astype(jnp.float32)
        for part in parts:
            cur = cur + part.astype(jnp.float32)
    return cur.reshape(rows, -1)


def two_heads(pair):
    lane = lax.broadcasted_iota(jnp.int32, pair.shape, 1)
    zero = jnp.zeros_like(pair)
    return jnp.concatenate(
        [jnp.where(lane < DH, pair, zero), jnp.where(lane < DH, zero, pair)], axis=0
    )


def fold_heads(wide):
    rows = wide.shape[1] // 2
    both = jnp.concatenate([wide[:DH, :rows], wide[DH:, rows:]], axis=0)
    return both.T


def block_of(meta, i):
    qb = pl.program_id(0)
    here = meta[1, qb]
    is_here = i < here
    kb = jnp.where(is_here, meta[0, qb] + i, meta[2, qb] + (i - here))
    return kb, kb * BK + jnp.where(is_here, meta[4, 0], meta[4, 1])


def key_mask(bounds, base):
    key_pos = lax.broadcasted_iota(jnp.int32, (BK, BQ), 0) + base
    same = (key_pos >= bounds[0:1, :]) & (key_pos < bounds[1:2, :])
    return jnp.concatenate([same, same], axis=1)


def attn_fwd_kernel(meta, q_ref, bounds, k_ref, v_ref, o_ref, lse_ref, acc, top, den):
    qb = pl.program_id(0)
    pairs = q_ref.shape[1] // 128
    acc[...] = jnp.zeros_like(acc)
    top[...] = jnp.full_like(top, mask_fill)
    den[...] = jnp.zeros_like(den)
    queries = [two_heads(q_ref[:, 128 * p : 128 * p + 128]) for p in range(pairs)]

    @pl.loop(0, meta[1, qb] + meta[3, qb])
    def _(i):
        kb, base = block_of(meta, i)
        rows = pl.ds(pl.multiple_of(kb * BK, BK), BK)
        same = key_mask(bounds, base)
        for p in range(pairs):
            cols = slice(128 * p, 128 * p + 128)
            s = dot(k_ref[rows, cols], queries[p], NT)
            s = jnp.where(same, s, mask_fill)
            old = top[p]
            new = jnp.maximum(old, jnp.max(s, axis=0, keepdims=True))
            e = jnp.exp(s - new)
            shrink = jnp.exp(old - new)
            den[p] = den[p] * shrink + jnp.sum(e, axis=0, keepdims=True)
            top[p] = new
            acc[p] = acc[p] * shrink + dot(v_ref[rows, cols], e.astype(jnp.bfloat16), TN)

    for p in range(pairs):
        out = fold_heads(acc[p] / den[p])
        o_ref[:, 128 * p : 128 * p + 128] = out.astype(o_ref.dtype)
        lse_ref[p] = top[p] + jnp.log(den[p])


def attn_bwd_kernel(
    meta, q_ref, do_ref, bounds, lse_ref, delta_ref, k_ref, v_ref, dq_ref, dk_ref, dv_ref, dk_acc, dv_acc, dq_acc
):
    qb = pl.program_id(0)
    pairs = q_ref.shape[1] // 128

    @pl.when(qb == 0)
    def _():
        dk_acc[...] = jnp.zeros_like(dk_acc)
        dv_acc[...] = jnp.zeros_like(dv_acc)

    dq_acc[...] = jnp.zeros_like(dq_acc)
    queries = [two_heads(q_ref[:, 128 * p : 128 * p + 128]) for p in range(pairs)]
    grads = [two_heads(do_ref[:, 128 * p : 128 * p + 128]) for p in range(pairs)]

    @pl.loop(0, meta[1, qb] + meta[3, qb])
    def _(i):
        kb, base = block_of(meta, i)
        rows = pl.ds(pl.multiple_of(kb * BK, BK), BK)
        same = key_mask(bounds, base)
        for p in range(pairs):
            cols = slice(128 * p, 128 * p + 128)
            keys = k_ref[rows, cols]
            s = dot(keys, queries[p], NT)
            probs = jnp.exp(jnp.where(same, s, mask_fill) - lse_ref[p])
            dp = dot(v_ref[rows, cols], grads[p], NT)
            ds = (probs * (dp - delta_ref[p])).astype(jnp.bfloat16)
            dv_acc[rows, cols] += dot(probs.astype(jnp.bfloat16), grads[p])
            dk_acc[rows, cols] += dot(ds, queries[p])
            dq_acc[p] += dot(keys, ds, TN)

    for p in range(pairs):
        out = fold_heads(dq_acc[p]) * (DH**-0.5)
        dq_ref[:, 128 * p : 128 * p + 128] = out.astype(dq_ref.dtype)

    @pl.when(qb == pl.num_programs(0) - 1)
    def _():
        dk_ref[...] = dk_acc[...].astype(dk_ref.dtype)
        dv_ref[...] = dv_acc[...].astype(dv_ref.dtype)


def whole(shape):
    return pl.BlockSpec(shape, lambda i, m: (0,) * len(shape))


def attn_forward(meta, queries, bounds, keys, values):
    rows, width = queries.shape
    span = keys.shape[0]
    pairs = width // 128
    return pl.pallas_call(
        attn_fwd_kernel,
        grid_spec=pltpu.PrefetchScalarGridSpec(
            num_scalar_prefetch=1,
            grid=(rows // BQ,),
            in_specs=[
                pl.BlockSpec((BQ, width), lambda i, m: (i, 0)),
                pl.BlockSpec((2, BQ), lambda i, m: (0, i)),
                whole((span, width)),
                whole((span, width)),
            ],
            out_specs=[
                pl.BlockSpec((BQ, width), lambda i, m: (i, 0)),
                pl.BlockSpec((pairs, 1, 2 * BQ), lambda i, m: (0, 0, i)),
            ],
            scratch_shapes=[
                pltpu.VMEM((pairs, 128, 2 * BQ), jnp.float32),
                pltpu.VMEM((pairs, 1, 2 * BQ), jnp.float32),
                pltpu.VMEM((pairs, 1, 2 * BQ), jnp.float32),
            ],
        ),
        out_shape=[
            jax.ShapeDtypeStruct((rows, width), jnp.bfloat16),
            jax.ShapeDtypeStruct((pairs, 1, 2 * rows), jnp.float32),
        ],
        compiler_params=pltpu.CompilerParams(vmem_limit_bytes=40 * 2**20),
        cost_estimate=pl.CostEstimate(
            flops=8 * rows * span * width // 4, bytes_accessed=8 * 2**20, transcendentals=rows * span * pairs
        ),
        name="attn_fwd",
    )(meta, queries, bounds, keys, values)


def attn_backward(meta, queries, grads, bounds, lse, delta, keys, values):
    rows, width = queries.shape
    span = keys.shape[0]
    pairs = width // 128
    tile = pl.BlockSpec((BQ, width), lambda i, m: (i, 0))
    line = pl.BlockSpec((pairs, 1, 2 * BQ), lambda i, m: (0, 0, i))
    return pl.pallas_call(
        attn_bwd_kernel,
        grid_spec=pltpu.PrefetchScalarGridSpec(
            num_scalar_prefetch=1,
            grid=(rows // BQ,),
            in_specs=[
                tile,
                tile,
                pl.BlockSpec((2, BQ), lambda i, m: (0, i)),
                line,
                line,
                whole((span, width)),
                whole((span, width)),
            ],
            out_specs=[tile, whole((span, width)), whole((span, width))],
            scratch_shapes=[
                pltpu.VMEM((span, width), jnp.float32),
                pltpu.VMEM((span, width), jnp.float32),
                pltpu.VMEM((pairs, 128, 2 * BQ), jnp.float32),
            ],
        ),
        out_shape=[
            jax.ShapeDtypeStruct((rows, width), jnp.bfloat16),
            jax.ShapeDtypeStruct((span, width), jnp.bfloat16),
            jax.ShapeDtypeStruct((span, width), jnp.bfloat16),
        ],
        compiler_params=pltpu.CompilerParams(vmem_limit_bytes=48 * 2**20),
        cost_estimate=pl.CostEstimate(
            flops=20 * rows * span * width // 4, bytes_accessed=12 * 2**20, transcendentals=rows * span * pairs
        ),
        name="attn_bwd",
    )(meta, queries, grads, bounds, lse, delta, keys, values)


def pack_heads(parts):
    return jnp.concatenate([p[:, :128] for p in parts] + [p[:, 128:] for p in parts], axis=1)


def unpack_heads(packed):
    return [
        jnp.concatenate(
            [packed[:, 128 * i : 128 * i + 128], packed[:, 512 + DH * i : 512 + DH * i + DH]], axis=1
        )
        for i in range(4)
    ]


def head_columns(two, i):
    return jnp.concatenate(
        [
            two[0][:, 128 * i : 128 * i + 128],
            two[1][:, 128 * i : 128 * i + 128],
            two[0][:, 512 + DH * i : 512 + DH * i + DH],
            two[1][:, 512 + DH * i : 512 + DH * i + DH],
        ],
        axis=1,
    )


def to_slices(parts):
    first = [p[:, :128] for p in parts] + [p[:, 256 : 256 + DH] for p in parts]
    second = [p[:, 128:256] for p in parts] + [p[:, 256 + DH :] for p in parts]
    return jnp.stack([jnp.concatenate(first, axis=1), jnp.concatenate(second, axis=1)])


def per_device(
    tokens,
    segments,
    query_weight,
    key_weight,
    value_weight,
    output_weight,
    attn_gain,
    attn_shift,
    inner_weight,
    outer_weight,
    ffn_gain,
    ffn_shift,
    proj_weight,
    grad_embed,
):
    length, model_width = tokens.shape[2:]
    half = length // 2
    core = lax.axis_index("shard") % 2
    ctx = lax.axis_index("ctx")
    group = lax.axis_index("tp")
    micro, seat = group // 2, group % 2
    owner = core == seat
    edge = min(SEG_MOST, length)
    bf16, f32 = jnp.bfloat16, jnp.float32

    tok_m = lax.dynamic_index_in_dim(tokens, micro, 0, False)[0]
    seg_m = lax.dynamic_index_in_dim(segments, micro, 0, False)[0]
    cot_m = lax.dynamic_index_in_dim(grad_embed, micro, 0, False)[0]
    tok_here = jnp.where(owner, tok_m, swap(tok_m, "shard", 1))
    seg_here = jnp.where(owner, seg_m, swap(seg_m, "shard", 1))
    seg_far = swap(seg_here, "ctx", 1)
    sent = lax.dynamic_slice_in_dim(tok_m, (1 - ctx) * (length - edge), edge, 0)
    got = route(sent, lambda s, c, t: (s, 1 - c, t) if s % 2 == t % 2 else None)
    got = jnp.where(owner, got, swap(got, "shard", 1))
    tok_far = lax.dynamic_update_slice_in_dim(
        jnp.zeros_like(tok_here), got, ctx * (length - edge), 0
    )
    tok_all = jnp.concatenate([tok_here, tok_far], axis=0)
    cot_sent = swap(lax.dynamic_slice_in_dim(cot_m, (1 - core) * half, half, 0), "shard", 1)
    cot = jnp.where(owner, lax.dynamic_slice_in_dim(cot_m, core * half, half, 0), cot_sent)
    cot = cot.astype(f32)

    heads_own = pack_heads([query_weight, key_weight, value_weight, output_weight.T])
    heads_full = gather_tree(heads_own, ("y", "x", "core"))
    inner_full = gather_tree(inner_weight, ("x", "y", "core"))
    outer_full = gather_tree(outer_weight.T, ("y", "x", "core"))
    proj_full = gather_tree(proj_weight, ("x", "y", "core"), False)[0]
    norms_own = jnp.stack([attn_gain, attn_shift, ffn_gain, ffn_shift], axis=1)
    norms = gather_tree(norms_own, ("x", "y", "core"), False)[0].astype(f32)
    gain_one, shift_one, gain_two, shift_two = (norms[:, i][None, :] for i in range(4))
    two = lax.dynamic_slice_in_dim(heads_full, 2 * core, 2, 0)
    query_w, key_w, value_w, output_w = (head_columns(two, i) for i in range(4))
    output_all = jnp.concatenate([head_columns(heads_full[:2], 3), head_columns(heads_full[2:], 3)], axis=1)

    seg_all = jnp.where(
        ctx == 0, jnp.concatenate([seg_here, seg_far]), jnp.concatenate([seg_far, seg_here])
    )
    upto = [jnp.sum((seg_all <= d).astype(jnp.int32)) for d in range(SEG_COUNT)]
    first = jnp.zeros_like(seg_here)
    last = jnp.full_like(seg_here, upto[0])
    for d in range(1, SEG_COUNT):
        first = jnp.where(seg_here >= d, upto[d - 1], first)
        last = jnp.where(seg_here >= d, upto[d], last)
    bounds = jnp.stack([first, last])
    here, far = ctx * length, (1 - ctx) * length
    low, high = first[::BQ], last[BQ - 1 :: BQ]
    ks = jnp.clip(low - here, 0, length) // BK
    ke = (jnp.clip(high - here, 0, length) + BK - 1) // BK
    rs = jnp.clip(low - far, 0, length) // BK
    re = (jnp.clip(high - far, 0, length) + BK - 1) // BK
    offsets = jnp.zeros_like(ks).at[0].set(here).at[1].set(far - length)
    meta = jnp.stack([ks, ke - ks, rs + length // BK, jnp.maximum(re - rs, 0), offsets])

    queries = (dot(tok_here, query_w).astype(bf16).astype(f32) * DH**-0.5).astype(bf16)
    keys = dot(tok_all, key_w).astype(bf16)
    values = dot(tok_all, value_w).astype(bf16)
    mixed, lse = attn_forward(meta, queries, bounds, keys, values)
    mixed_got = swap(lax.dynamic_slice_in_dim(mixed, (1 - core) * half, half, 0), "shard", 1)
    mixed_kept = lax.dynamic_slice_in_dim(mixed, core * half, half, 0)
    mixed_own = jnp.concatenate(
        [jnp.where(core == 0, mixed_kept, mixed_got), jnp.where(core == 0, mixed_got, mixed_kept)],
        axis=1,
    )
    attn_out = dot(mixed_own, output_all, NT)

    tok_own = lax.dynamic_slice_in_dim(tok_here, core * half, half, 0).astype(f32)
    first_out, normed_one, inv_one = norm_forward(tok_own + attn_out, gain_one, shift_one)
    first_low = first_out.astype(bf16)
    pre_act = jnp.einsum("td,zdf->ztf", first_low, inner_full, preferred_element_type=f32)
    gelu_value, gelu_pull = jax.vjp(functools.partial(jax.nn.gelu, approximate=False), pre_act)
    activated = gelu_value.astype(bf16)
    ffn_out = jnp.einsum("ztf,zdf->td", activated, outer_full, preferred_element_type=f32)
    second, normed_two, inv_two = norm_forward(first_out + ffn_out, gain_two, shift_two)
    second_low = second.astype(bf16)
    projected = dot(second_low, proj_full)
    inv_norm = lax.rsqrt(jnp.sum(projected * projected, axis=-1, keepdims=True) + eps_unit)
    embedding = projected * inv_norm

    radial = jnp.sum(cot * embedding, axis=-1, keepdims=True)
    grad_projected = (inv_norm * (cot - embedding * radial)).astype(bf16)
    proj_part = dot(second_low, grad_projected, TN)
    grad_second = dot(grad_projected, proj_full, NT)
    grad_h2, gain_two_part, shift_two_part = norm_backward(
        grad_second, normed_two, inv_two, gain_two
    )
    grad_ffn = grad_h2.astype(bf16)
    outer_part = jnp.einsum("td,ztf->zdf", grad_ffn, activated, preferred_element_type=f32)
    grad_act = jnp.einsum("td,zdf->ztf", grad_ffn, outer_full, preferred_element_type=f32)
    (grad_pre,) = gelu_pull(grad_act)
    grad_pre = grad_pre.astype(bf16)
    inner_part = jnp.einsum("td,ztf->zdf", first_low, grad_pre, preferred_element_type=f32)
    hidden = jnp.einsum("ztf,zdf->td", grad_pre, inner_full, preferred_element_type=f32)
    grad_h1, gain_one_part, shift_one_part = norm_backward(
        grad_h2 + hidden, normed_one, inv_one, gain_one
    )
    grad_attn_own = grad_h1.astype(bf16)
    other = swap(grad_attn_own, "shard", 1)
    grad_attn = jnp.concatenate(
        [jnp.where(core == 0, grad_attn_own, other), jnp.where(core == 0, other, grad_attn_own)],
        axis=0,
    )
    output_part = dot(grad_attn, mixed, TN)
    grad_mixed = dot(grad_attn, output_w).astype(bf16)

    pairs = mixed.shape[1] // 128
    products = grad_mixed.astype(f32) * mixed.astype(f32)
    delta = jnp.sum(products.reshape(length // BQ, BQ, pairs, 2, DH), axis=-1)
    delta = delta.transpose(2, 0, 3, 1).reshape(pairs, 1, 2 * length)
    grad_q, grad_k, grad_v = attn_backward(
        meta, queries, grad_mixed, bounds, lse, delta, keys, values
    )
    query_part = dot(tok_here, grad_q, TN)
    key_part = dot(tok_all, grad_k, TN)
    value_part = dot(tok_all, grad_v, TN)
    input_all = dot(grad_k, key_w, NT) + dot(grad_v, value_w, NT)
    input_here = input_all[:length] + dot(grad_q, query_w, NT)
    input_far = input_all[length:]

    def halve(full):
        theirs = lax.dynamic_slice_in_dim(full, (1 - core) * half, half, 0).astype(bf16)
        return lax.dynamic_slice_in_dim(full, core * half, half, 0) + swap(
            theirs, "shard", 1
        ).astype(f32)

    from_far = swap(halve(input_far).astype(bf16), "ctx", 1).astype(f32)
    grad_tok = (halve(input_here) + from_far + grad_h1).astype(bf16)
    own_cols = model_width // lax.axis_size("tp")
    col_parts = [grad_tok[:, own_cols * j : own_cols * (j + 1)] for j in range(4)]
    place = 2 * micro + core
    arrived = [
        route(
            lax.select_n(place ^ d, *col_parts),
            lambda s, c, t, d=d: (s - s % 2 + t % 2, c, (2 * (t // 2) + s % 2) ^ d),
        )
        for d in range(4)
    ]
    grad_tokens = jnp.stack([lax.select_n(group ^ j, *arrived) for j in range(4)])
    grad_tokens = grad_tokens.reshape(2, 1, length, own_cols).astype(f32)

    quarter = half // 2
    emb_parts = [embedding[:quarter], embedding[quarter:]]
    emb_got = [
        route(
            lax.select_n(micro ^ d, *emb_parts),
            lambda s, c, t, d=d: (s - s % 2 + t % 2, c, 2 * (s % 2) + ((t // 2) ^ d)),
        )
        for d in range(2)
    ]
    embeddings = jnp.stack([lax.select_n((group % 2) ^ m, *emb_got) for m in range(2)])
    embeddings = embeddings.reshape(2, 1, quarter, -1)

    outer_grad = scatter_tree(outer_part.astype(bf16), ("core", "x", "y")).T
    inner_grad = scatter_tree(inner_part.astype(bf16), ("core", "y", "x"))
    slices = to_slices([query_part, key_part, value_part, output_part]).astype(bf16)
    zero = jnp.zeros_like(slices)
    slices = jnp.concatenate(
        [jnp.where(core == 0, slices, zero), jnp.where(core == 0, zero, slices)], axis=0
    )
    query_grad, key_grad, value_grad, output_grad = unpack_heads(
        scatter_tree(slices, ("core", "x", "y"))
    )
    small = jnp.concatenate(
        [proj_part]
        + [
            v[:, None]
            for v in (gain_one_part, shift_one_part, gain_two_part, shift_two_part)
        ],
        axis=1,
    ).astype(bf16)
    small = scatter_tree(small[None], ("core", "x", "y"), False).astype(bf16)
    parts = [swap(small, "tp", d) for d in range(1, 4)]
    small = small.astype(f32)
    for part in parts:
        small = small + part.astype(f32)
    p_width = proj_part.shape[1]
    return (
        embeddings,
        grad_tokens,
        query_grad,
        key_grad,
        value_grad,
        output_grad.T,
        small[:, p_width],
        small[:, p_width + 1],
        inner_grad,
        outer_grad,
        small[:, p_width + 2],
        small[:, p_width + 3],
        small[:, :p_width],
    )


def solution(mesh):
    rows = ("shard", "ctx")
    placed = (
        P(None, "shard", "ctx", None),
        P(None, "shard", "ctx"),
        P(rows, "tp"),
        P(rows, "tp"),
        P(rows, "tp"),
        P("tp", rows),
        P(rows),
        P(rows),
        P(rows, "tp"),
        P("tp", rows),
        P(rows),
        P(rows),
        P(rows, None),
        P(None, "shard", "ctx", None),
    )
    return jax.shard_map(
        per_device,
        mesh=mesh,
        in_specs=placed,
        out_specs=(
            P(None, "shard", ("ctx", "tp"), None),
            P(None, "shard", "ctx", "tp"),
            P(rows, "tp"),
            P(rows, "tp"),
            P(rows, "tp"),
            P("tp", rows),
            P(rows),
            P(rows),
            P(rows, "tp"),
            P("tp", rows),
            P(rows),
            P(rows),
            P(rows, None),
        ),
        check_vma=False,
    )
```

```python
import functools

import jax
import jax.numpy as jnp
from jax import lax
from jax.experimental import pallas as pl
from jax.experimental.pallas import tpu as pltpu
from jax.sharding import PartitionSpec as P

DH = 64
SEG_COUNT = 6
SEG_MOST = 800
BQ = 256
BK = 256
VMEM_MIB = 48

eps_norm = 1e-12
eps_unit = 1e-06
mask_fill = -1e30

NN = (((1,), (0,)), ((), ()))
NT = (((1,), (1,)), ((), ()))
TN = (((0,), (0,)), ((), ()))


def dot(first_op, second_op, dims=NN):
    return lax.dot_general(first_op, second_op, dims, preferred_element_type=jnp.float32)


def tie(*values):
    return lax.optimization_barrier(values)


def after(value, *others):
    return lax.optimization_barrier((value, *others))[0]


def after_all(done, *values):
    return lax.optimization_barrier((done, *values))[1:]


def swap(v, axis, bit):
    count = lax.axis_size(axis)
    return lax.ppermute(v, axis, [(i, i ^ bit) for i in range(count)])


def route(v, target):
    shards, halves, groups = (lax.axis_size(a) for a in ("shard", "ctx", "tp"))

    def flat(s, c, t):
        return (s * halves + c) * groups + t

    pairs = []
    for s in range(shards):
        for c in range(halves):
            for t in range(groups):
                to = target(s, c, t)
                if to is not None:
                    pairs.append((flat(s, c, t), flat(*to)))
    return lax.ppermute(v, ("shard", "ctx", "tp"), pairs)


def shard_bits():
    return lax.axis_size("shard").bit_length() - 1


def steps_of(name):
    bits = shard_bits()
    if name == "x":
        return [("ctx", 1, bits)]
    return [("shard", 1 << i, bits - 1 - i) for i in range(1, bits)]


def my_bit(axis, bit):
    return (lax.axis_index(axis) // bit) % 2


def gather_tp_start(own):
    return [
        route(
            own,
            lambda s, c, t, d=d: (s - s % 2 + t // 2, c, (2 * (s % 2) + t % 2) ^ d),
        )
        for d in range(4)
    ]


def gather_tp_finish(parts):
    t = lax.axis_index("tp")
    dim = shard_bits() - 1
    shape = (1,) * dim + (1, 1) + parts[0].shape
    return [
        jnp.concatenate(
            [lax.select_n(t ^ (2 * j + s), *parts).reshape(shape) for j in range(2)], axis=dim
        )
        for s in range(2)
    ]


def join(cur, other, axis, bit, dim):
    first = my_bit(axis, bit) == 0
    return jnp.concatenate([jnp.where(first, cur, other), jnp.where(first, other, cur)], axis=dim)


def gather_start(cur, name):
    axis, bit, _ = steps_of(name)[0]
    return swap(cur, axis, bit)


def gather_finish(cur, other, name):
    first, *rest = steps_of(name)
    cur = join(cur, other, *first)
    for axis, bit, dim in rest:
        cur = join(cur, swap(cur, axis, bit), axis, bit, dim)
    return cur


def flat_rows(cur):
    return cur.reshape(-1, cur.shape[-1])


def split_rows(full):
    rows = full.shape[-2] // (lax.axis_size("shard") * lax.axis_size("ctx"))
    return full.reshape(full.shape[:-2] + (2,) * (shard_bits() + 1) + (rows, full.shape[-1]))


def scatter_start(cur, name):
    axis, bit, dim = steps_of(name)[0]
    return swap(lax.dynamic_slice_in_dim(cur, 1 - my_bit(axis, bit), 1, dim), axis, bit)


def scatter_finish(cur, other, name):
    first, *rest = steps_of(name)
    kept = lax.dynamic_slice_in_dim(cur, my_bit(*first[:2]), 1, first[2])
    cur = (kept.astype(jnp.float32) + other.astype(jnp.float32)).astype(jnp.bfloat16)
    for axis, bit, dim in rest:
        mine = my_bit(axis, bit)
        other = swap(lax.dynamic_slice_in_dim(cur, 1 - mine, 1, dim), axis, bit)
        kept = lax.dynamic_slice_in_dim(cur, mine, 1, dim)
        cur = (kept.astype(jnp.float32) + other.astype(jnp.float32)).astype(jnp.bfloat16)
    return cur


def scatter_tp_start(first, second):
    z = lax.axis_index("tp")
    blocks = [lax.index_in_dim(s, j, s.ndim - 4, False) for j in range(2) for s in (first, second)]
    return [
        route(
            lax.select_n(z ^ d, *blocks),
            lambda s, c, t, d=d: (s - s % 2 + ((t ^ d) >> 1), c, 2 * (s % 2) + ((t ^ d) & 1)),
        )
        for d in range(4)
    ]


def sum_all(parts):
    total = parts[0].astype(jnp.float32)
    for part in parts[1:]:
        total = total + part.astype(jnp.float32)
    return total


def two_heads(pair):
    lane = lax.broadcasted_iota(jnp.int32, pair.shape, 1)
    zero = jnp.zeros_like(pair)
    return jnp.concatenate(
        [jnp.where(lane < DH, pair, zero), jnp.where(lane < DH, zero, pair)], axis=0
    )


def fold_heads(wide):
    rows = wide.shape[1] // 2
    both = jnp.concatenate([wide[:DH, :rows], wide[DH:, rows:]], axis=0)
    return both.T


def document(ends, start, stop, most):
    low, high = start * 0, start * 0 + most
    for d in range(SEG_COUNT):
        low = jnp.maximum(low, jnp.where(ends[d] <= start, ends[d], 0))
        high = jnp.minimum(high, jnp.where(ends[d] > stop, ends[d], most))
    return low, high


def key_blocks(ends, qb, span):
    length = span // 2
    here = ends[SEG_COUNT]
    far = length - here
    start = here + qb * BQ
    low, high = document(ends, start, start + BQ - 1, span)
    first = jnp.clip(low - here, 0, length) // BK
    count = (jnp.clip(high - here, 0, length) + (BK - 1)) // BK - first
    first_far = jnp.clip(low - far, 0, length) // BK
    count_far = (jnp.clip(high - far, 0, length) + (BK - 1)) // BK - first_far
    count_far = jnp.maximum(count_far, 0)

    def block(i):
        is_here = i < count
        kb = jnp.where(is_here, first + i, length // BK + first_far + (i - count))
        return kb, kb * BK + jnp.where(is_here, here, far - length)

    return count + count_far, block


def query_bounds(ends, qb, span):
    pos = ends[SEG_COUNT] + qb * BQ + lax.broadcasted_iota(jnp.int32, (1, BQ), 1)
    return document(ends, pos, pos, span)


def key_mask(bounds, base):
    key_pos = lax.broadcasted_iota(jnp.int32, (BK, BQ), 0) + base
    same = (key_pos >= bounds[0]) & (key_pos < bounds[1])
    return jnp.concatenate([same, same], axis=1)


def attn_fwd_kernel(first_block, ends, q_ref, k_ref, v_ref, o_ref, lse_ref, acc, top, den):
    span = k_ref.shape[0]
    qb = pl.program_id(0) + first_block
    pairs = q_ref.shape[1] // 128
    acc[...] = jnp.zeros_like(acc)
    top[...] = jnp.full_like(top, mask_fill)
    den[...] = jnp.zeros_like(den)
    queries = [two_heads(q_ref[:, 128 * p : 128 * p + 128]) for p in range(pairs)]
    bounds = query_bounds(ends, qb, span)
    count, block = key_blocks(ends, qb, span)

    @pl.loop(0, count)
    def _(i):
        kb, base = block(i)
        rows = pl.ds(pl.multiple_of(kb * BK, BK), BK)
        same = key_mask(bounds, base)
        for p in range(pairs):
            cols = slice(128 * p, 128 * p + 128)
            s = dot(k_ref[rows, cols], queries[p], NT)
            s = jnp.where(same, s, mask_fill)
            old = top[p]
            new = jnp.maximum(old, jnp.max(s, axis=0, keepdims=True))
            e = jnp.exp(s - new)
            shrink = jnp.exp(old - new)
            den[p] = den[p] * shrink + jnp.sum(e, axis=0, keepdims=True)
            top[p] = new
            acc[p] = acc[p] * shrink + dot(v_ref[rows, cols], e.astype(jnp.bfloat16), TN)

    for p in range(pairs):
        out = fold_heads(acc[p] / den[p])
        o_ref[:, 128 * p : 128 * p + 128] = out.astype(o_ref.dtype)
        lse_ref[p] = top[p] + jnp.log(den[p])


def row_sums(grads, outs):
    prod = (grads.astype(jnp.float32) * outs.astype(jnp.float32)).T
    return jnp.concatenate(
        [jnp.sum(prod[:DH], axis=0, keepdims=True), jnp.sum(prod[DH:], axis=0, keepdims=True)],
        axis=1,
    )


def attn_bwd_kernel(
    ends,
    q_ref,
    do_ref,
    o_low,
    o_high,
    lse_low,
    lse_high,
    k_ref,
    v_ref,
    dq_ref,
    dk_ref,
    dv_ref,
    dk_acc,
    dv_acc,
    dq_acc,
):
    span = k_ref.shape[0]
    qb = pl.program_id(0)
    is_low = qb < pl.num_programs(0) // 2
    pairs = q_ref.shape[1] // 128
    cols = [slice(128 * p, 128 * p + 128) for p in range(pairs)]

    @pl.when(qb == 0)
    def _():
        dk_acc[...] = jnp.zeros_like(dk_acc)
        dv_acc[...] = jnp.zeros_like(dv_acc)

    dq_acc[...] = jnp.zeros_like(dq_acc)
    outs = jnp.where(is_low, o_low[...], o_high[...])
    lses = jnp.where(is_low, lse_low[...], lse_high[...])
    queries = [two_heads(q_ref[:, c]) for c in cols]
    grads = [two_heads(do_ref[:, c]) for c in cols]
    deltas = [row_sums(do_ref[:, c], outs[:, c]) for c in cols]
    bounds = query_bounds(ends, qb, span)
    count, block = key_blocks(ends, qb, span)

    @pl.loop(0, count)
    def _(i):
        kb, base = block(i)
        rows = pl.ds(pl.multiple_of(kb * BK, BK), BK)
        same = key_mask(bounds, base)
        for p, c in enumerate(cols):
            keys = k_ref[rows, c]
            s = dot(keys, queries[p], NT)
            probs = jnp.exp(jnp.where(same, s, mask_fill) - lses[p])
            dp = dot(v_ref[rows, c], grads[p], NT)
            ds = (probs * (dp - deltas[p])).astype(jnp.bfloat16)
            dv_acc[rows, c] += dot(probs.astype(jnp.bfloat16), grads[p])
            dk_acc[rows, c] += dot(ds, queries[p])
            dq_acc[p] += dot(keys, ds, TN)

    for p, c in enumerate(cols):
        dq_ref[:, c] = (fold_heads(dq_acc[p]) * (DH**-0.5)).astype(dq_ref.dtype)

    @pl.when(qb == pl.num_programs(0) - 1)
    def _():
        dk_ref[...] = dk_acc[...].astype(dk_ref.dtype)
        dv_ref[...] = dv_acc[...].astype(dv_ref.dtype)


def params(mib):
    return pltpu.CompilerParams(vmem_limit_bytes=mib * 2**20)


def cost(seconds):
    return pl.CostEstimate(flops=int(seconds * 1.15e15), bytes_accessed=2**20, transcendentals=0)


def attn_forward(ends, first_block, queries, keys, values):
    rows, width = queries.shape
    span = keys.shape[0]
    pairs = width // 128
    every = pl.BlockSpec((span, width), lambda i, e: (0, 0))
    return pl.pallas_call(
        functools.partial(attn_fwd_kernel, first_block),
        grid_spec=pltpu.PrefetchScalarGridSpec(
            num_scalar_prefetch=1,
            grid=(rows // BQ // 2,),
            in_specs=[
                pl.BlockSpec((BQ, width), lambda i, e: (i + first_block, 0)),
                every,
                every,
            ],
            out_specs=[
                pl.BlockSpec((BQ, width), lambda i, e: (i, 0)),
                pl.BlockSpec((pairs, 1, 2 * BQ), lambda i, e: (0, 0, i)),
            ],
            scratch_shapes=[
                pltpu.VMEM((pairs, 128, 2 * BQ), jnp.float32),
                pltpu.VMEM((pairs, 1, 2 * BQ), jnp.float32),
                pltpu.VMEM((pairs, 1, 2 * BQ), jnp.float32),
            ],
        ),
        out_shape=[
            jax.ShapeDtypeStruct((rows // 2, width), jnp.bfloat16),
            jax.ShapeDtypeStruct((pairs, 1, rows), jnp.float32),
        ],
        compiler_params=params(VMEM_MIB),
        cost_estimate=cost(10e-6),
        name="attn_fwd",
    )(ends, queries, keys, values)


def attn_backward(ends, queries, grads, mixed, lse, keys, values):
    rows, width = queries.shape
    span = keys.shape[0]
    pairs = width // 128
    half = rows // BQ // 2
    tile = pl.BlockSpec((BQ, width), lambda i, e: (i, 0))
    low = pl.BlockSpec((BQ, width), lambda i, e: (jnp.minimum(i, half - 1), 0))
    high = pl.BlockSpec((BQ, width), lambda i, e: (jnp.maximum(i - half, 0), 0))
    low_line = pl.BlockSpec((pairs, 1, 2 * BQ), lambda i, e: (0, 0, jnp.minimum(i, half - 1)))
    high_line = pl.BlockSpec((pairs, 1, 2 * BQ), lambda i, e: (0, 0, jnp.maximum(i - half, 0)))
    every = pl.BlockSpec((span, width), lambda i, e: (0, 0))
    return pl.pallas_call(
        attn_bwd_kernel,
        grid_spec=pltpu.PrefetchScalarGridSpec(
            num_scalar_prefetch=1,
            grid=(rows // BQ,),
            in_specs=[tile, tile, low, high, low_line, high_line, every, every],
            out_specs=[tile, every, every],
            scratch_shapes=[
                pltpu.VMEM((span, width), jnp.float32),
                pltpu.VMEM((span, width), jnp.float32),
                pltpu.VMEM((pairs, 128, 2 * BQ), jnp.float32),
            ],
        ),
        out_shape=[
            jax.ShapeDtypeStruct((rows, width), jnp.bfloat16),
            jax.ShapeDtypeStruct((span, width), jnp.bfloat16),
            jax.ShapeDtypeStruct((span, width), jnp.bfloat16),
        ],
        compiler_params=params(VMEM_MIB),
        cost_estimate=cost(25e-6),
        name="attn_bwd",
    )(ends, queries, grads, *mixed, *lse, keys, values)


def full_spec(shape):
    return pl.BlockSpec(shape, lambda i: (0,) * len(shape))


def rows_spec(rows, cols):
    return pl.BlockSpec((rows, cols), lambda i: (i, 0))


def pack_kernel(q_ref, k_ref, v_ref, out_ref):
    parts = [q_ref[...], k_ref[...], v_ref[...]]
    for i, part in enumerate(parts):
        out_ref[:, 128 * i : 128 * i + 128] = part[:, :128]
    thirds = [p[:, 128:] for p in parts]
    thirds.append(jnp.zeros_like(thirds[0]))
    out_ref[:, 384:512] = jnp.concatenate(thirds[:2], axis=1)
    out_ref[:, 512:640] = jnp.concatenate(thirds[2:], axis=1)


def pack_heads(*parts):
    return pl.pallas_call(
        pack_kernel,
        out_shape=jax.ShapeDtypeStruct((parts[0].shape[0], 640), parts[0].dtype),
        compiler_params=params(8),
        cost_estimate=cost(1e-6),
        name="pack_heads",
    )(*parts)


def qkv_kernel(x_ref, a_ref, b_ref, q_ref, k_ref, v_ref, wq_ref, wk_ref, wv_ref):
    step = pl.program_id(0)

    @pl.when(step == 0)
    def _():
        for i, out in enumerate((wq_ref, wk_ref, wv_ref)):
            lo = 384 + DH * i
            out[:, :128] = a_ref[:, 128 * i : 128 * i + 128]
            out[:, 128:256] = b_ref[:, 128 * i : 128 * i + 128]
            out[:, 256:] = jnp.concatenate([a_ref[:, lo : lo + DH], b_ref[:, lo : lo + DH]], axis=1)

    x = x_ref[...]
    k_ref[...] = dot(x, wk_ref[...]).astype(k_ref.dtype)
    v_ref[...] = dot(x, wv_ref[...]).astype(v_ref.dtype)

    @pl.when(step < pl.num_programs(0) // 2)
    def _():
        q = dot(x, wq_ref[...]).astype(jnp.bfloat16).astype(jnp.float32)
        q_ref[...] = (q * DH**-0.5).astype(q_ref.dtype)


def project(tok_all, w_a, w_b):
    span, width = tok_all.shape
    block = 512
    steps = span // block
    cols = 384
    low = jnp.bfloat16
    return pl.pallas_call(
        qkv_kernel,
        grid=(steps,),
        in_specs=[rows_spec(block, width), full_spec(w_a.shape), full_spec(w_b.shape)],
        out_specs=[
            pl.BlockSpec((block, cols), lambda i: (jnp.minimum(i, steps // 2 - 1), 0)),
            rows_spec(block, cols),
            rows_spec(block, cols),
        ]
        + [full_spec((width, cols))] * 3,
        out_shape=[
            jax.ShapeDtypeStruct((span // 2, cols), low),
            jax.ShapeDtypeStruct((span, cols), low),
            jax.ShapeDtypeStruct((span, cols), low),
        ]
        + [jax.ShapeDtypeStruct((width, cols), low)] * 3,
        compiler_params=params(VMEM_MIB),
        cost_estimate=cost(6e-6),
        name="qkv",
    )(tok_all, w_a, w_b)


def attn_out_kernel(low_ref, high_ref, a_ref, b_ref, part_ref, ow_ref, proj_ref, norms_ref):
    step = pl.program_id(0)

    @pl.when(step == 0)
    def _():
        ow_ref[:, :128] = a_ref[:, :128]
        ow_ref[:, 128:256] = b_ref[:, :128]
        ow_ref[:, 256:] = jnp.concatenate([a_ref[:, 128:192], b_ref[:, 128:192]], axis=1)
        proj_ref[...] = a_ref[:, 192:320]
        turned = a_ref[:, 256:384].astype(jnp.float32).T
        norms_ref[...] = turned[64:72]

    mixed = jnp.where(step < pl.num_programs(0) // 2, low_ref[...], high_ref[...])
    part_ref[...] = dot(mixed, ow_ref[...], NT).astype(part_ref.dtype)


def attn_out(mixed, w_a, w_b):
    half, cols = mixed[0].shape
    width = w_a.shape[0]
    block = 256
    per = half // block
    low = jnp.bfloat16
    third = pl.BlockSpec((width, 384), lambda i: (0, 2))
    return pl.pallas_call(
        attn_out_kernel,
        grid=(2 * per,),
        in_specs=[
            pl.BlockSpec((block, cols), lambda i: (jnp.minimum(i, per - 1), 0)),
            pl.BlockSpec((block, cols), lambda i: (jnp.maximum(i - per, 0), 0)),
            third,
            third,
        ],
        out_specs=[
            rows_spec(block, width),
            full_spec((width, cols)),
            full_spec((width, 128)),
            full_spec((8, width)),
        ],
        out_shape=[
            jax.ShapeDtypeStruct((2 * half, width), low),
            jax.ShapeDtypeStruct((width, cols), low),
            jax.ShapeDtypeStruct((width, 128), low),
            jax.ShapeDtypeStruct((8, width), jnp.float32),
        ],
        compiler_params=params(VMEM_MIB),
        cost_estimate=cost(3e-6),
        name="attn_out",
    )(*mixed, w_a, w_b)


def normalize(hidden):
    row_mean = jnp.mean(hidden, axis=-1, keepdims=True)
    centred = hidden - row_mean
    variance = jnp.mean(centred * centred, axis=-1, keepdims=True)
    inv_std = lax.rsqrt(variance + eps_norm)
    return centred * inv_std, inv_std


def norm_backward(grad_out, normed, inv_std, gain):
    scaled = grad_out * gain
    return inv_std * (
        scaled
        - jnp.mean(scaled, axis=-1, keepdims=True)
        - normed * jnp.mean(scaled * normed, axis=-1, keepdims=True)
    )


def wide(ref):
    return ref[...].astype(jnp.float32)


def first_norm_kernel(x_ref, mine_ref, got_ref, norms, normed_ref, inv_ref, low_ref, turned_ref):
    normed, inv = normalize(wide(x_ref) + (wide(mine_ref) + wide(got_ref)))
    normed_ref[...] = normed
    inv_ref[...] = jnp.broadcast_to(inv, inv_ref.shape)
    low = (normed * norms[0:1, :] + norms[1:2, :]).astype(jnp.bfloat16)
    low_ref[...] = low
    turned_ref[...] = low.T


def first_norm(tok, mine, got, norms):
    rows, width = tok.shape
    block = 256
    tile = rows_spec(block, width)
    return pl.pallas_call(
        first_norm_kernel,
        grid=(rows // block,),
        in_specs=[tile, tile, tile, full_spec(norms.shape)],
        out_specs=[
            tile,
            rows_spec(block, 128),
            tile,
            pl.BlockSpec((width, block), lambda i: (0, i)),
        ],
        out_shape=[
            jax.ShapeDtypeStruct((rows, width), jnp.float32),
            jax.ShapeDtypeStruct((rows, 128), jnp.float32),
            jax.ShapeDtypeStruct((rows, width), jnp.bfloat16),
            jax.ShapeDtypeStruct((width, rows), jnp.bfloat16),
        ],
        compiler_params=params(VMEM_MIB),
        cost_estimate=cost(3e-6),
        name="first_norm",
    )(tok, mine, got, norms)


def gelu_parts(v):
    e = jnp.exp(v * v * -0.5)
    t = 1.0 / (1.0 + (0.3275911 * 0.5**0.5) * jnp.abs(v))
    poly = 0.5 * 1.061405429
    for c in (-1.453152027, 1.421413741, -0.284496736, 0.254829592):
        poly = poly * t + 0.5 * c
    upper = poly * t * e
    cdf = jnp.where(v >= 0, 1.0 - upper, upper)
    return v * cdf, cdf + v * e * 0.3989422804014327


def ffn_in_kernel(x_ref, a_ref, b_ref, act_ref, slope_ref):
    def work(w_ref):
        for r in range(0, x_ref.shape[0], 256):
            rows = slice(r, r + 256)
            act, slope = gelu_parts(dot(x_ref[rows, :], w_ref[...]))
            act_ref[rows, :] = act.astype(act_ref.dtype)
            slope_ref[rows, :] = slope.astype(slope_ref.dtype)

    first = pl.program_id(0) < pl.num_programs(0) // 2
    pl.when(first)(lambda: work(a_ref))
    pl.when(jnp.logical_not(first))(lambda: work(b_ref))


def ffn_in(x, w_a, w_b, hidden):
    rows, width = x.shape
    cols = 384
    per = hidden // cols
    out = pl.BlockSpec((rows, cols), lambda i: (0, i))
    shape = jax.ShapeDtypeStruct((rows, 2 * hidden), jnp.bfloat16)
    return pl.pallas_call(
        ffn_in_kernel,
        grid=(2 * per,),
        in_specs=[
            full_spec((rows, width)),
            pl.BlockSpec((width, cols), lambda i: (0, jnp.minimum(i, per - 1))),
            pl.BlockSpec((width, cols), lambda i: (0, jnp.maximum(i - per, 0))),
        ],
        out_specs=[out, out],
        out_shape=[shape, shape],
        compiler_params=params(VMEM_MIB),
        cost_estimate=cost(10e-6),
        name="ffn_in",
    )(x, w_a, w_b)


def ffn_out_kernel(act_ref, a_ref, b_ref, out_ref):
    hidden = a_ref.shape[1]
    part = dot(act_ref[:, :hidden], a_ref[...], NT) + dot(act_ref[:, hidden:], b_ref[...], NT)
    out_ref[...] = part.astype(out_ref.dtype)


def ffn_out(act, w_a, w_b):
    rows = act.shape[0]
    width = w_a.shape[0]
    block = 256
    return pl.pallas_call(
        ffn_out_kernel,
        grid=(rows // block,),
        in_specs=[rows_spec(block, act.shape[1]), full_spec(w_a.shape), full_spec(w_b.shape)],
        out_specs=rows_spec(block, width),
        out_shape=jax.ShapeDtypeStruct((rows, width), jnp.bfloat16),
        compiler_params=params(VMEM_MIB),
        cost_estimate=cost(3e-6),
        name="ffn_out",
    )(act, w_a, w_b)


def middle_kernel(
    normed_ref, mine_ref, got_ref, norms, proj_ref, cot_ref, emb_ref, gh2_ref, low_ref, turned_ref, pg_ref, vec_ref
):
    step = pl.program_id(0)
    first = normed_ref[...] * norms[0:1, :] + norms[1:2, :]
    normed, inv = normalize(first + (wide(mine_ref) + wide(got_ref)))
    second = (normed * norms[2:3, :] + norms[3:4, :]).astype(jnp.bfloat16)
    projected = dot(second, proj_ref[...])
    inv_norm = lax.rsqrt(jnp.sum(projected * projected, axis=-1, keepdims=True) + eps_unit)
    embedding = projected * inv_norm
    emb_ref[...] = embedding
    cot = wide(cot_ref)
    radial = jnp.sum(cot * embedding, axis=-1, keepdims=True)
    grad_projected = (inv_norm * (cot - embedding * radial)).astype(jnp.bfloat16)
    grad_second = dot(grad_projected, proj_ref[...], NT)
    grad = norm_backward(grad_second, normed, inv, norms[2:3, :])
    gh2_ref[...] = grad
    low = grad.astype(jnp.bfloat16)
    low_ref[...] = low
    turned_ref[...] = low.T

    @pl.when(step == 0)
    def _():
        pg_ref[...] = jnp.zeros_like(pg_ref)
        vec_ref[...] = jnp.zeros_like(vec_ref)

    pg_ref[...] += dot(second, grad_projected, TN)
    vec_ref[0:1, :] += jnp.sum(grad_second * normed, axis=0, keepdims=True)
    vec_ref[1:2, :] += jnp.sum(grad_second, axis=0, keepdims=True)


def middle(normed, mine, got, norms, proj, cot):
    rows, width = normed.shape
    p_width = proj.shape[1]
    block = 256
    tile = rows_spec(block, width)
    return pl.pallas_call(
        middle_kernel,
        grid=(rows // block,),
        in_specs=[
            tile,
            tile,
            tile,
            full_spec(norms.shape),
            full_spec(proj.shape),
            rows_spec(block, p_width),
        ],
        out_specs=[
            rows_spec(block, p_width),
            tile,
            tile,
            pl.BlockSpec((width, block), lambda i: (0, i)),
            full_spec((width, p_width)),
            full_spec((8, width)),
        ],
        out_shape=[
            jax.ShapeDtypeStruct((rows, p_width), jnp.float32),
            jax.ShapeDtypeStruct((rows, width), jnp.float32),
            jax.ShapeDtypeStruct((rows, width), jnp.bfloat16),
            jax.ShapeDtypeStruct((width, rows), jnp.bfloat16),
            jax.ShapeDtypeStruct((width, p_width), jnp.float32),
            jax.ShapeDtypeStruct((8, width), jnp.float32),
        ],
        compiler_params=params(VMEM_MIB),
        cost_estimate=cost(5e-6),
        name="middle",
    )(normed, mine, got, norms, proj, cot)


def back_outer_kernel(g_ref, gt_ref, act_ref, slope_ref, a_ref, b_ref, wga_ref, wgb_ref, gpre_ref):
    def work(w_ref, wg_ref):
        wg_ref[...] = dot(gt_ref[...], act_ref[...]).astype(wg_ref.dtype)
        for r in range(0, g_ref.shape[0], 256):
            rows = slice(r, r + 256)
            grad = dot(g_ref[rows, :], w_ref[...]) * slope_ref[rows, :].astype(jnp.float32)
            gpre_ref[rows, :] = grad.astype(gpre_ref.dtype)

    first = pl.program_id(0) < pl.num_programs(0) // 2
    pl.when(first)(lambda: work(a_ref, wga_ref))
    pl.when(jnp.logical_not(first))(lambda: work(b_ref, wgb_ref))


def back_outer(grad, grad_t, act, slope, w_a, w_b):
    rows, width = grad.shape
    hidden = w_a.shape[1]
    cols = 384
    per = hidden // cols
    tile = pl.BlockSpec((rows, cols), lambda i: (0, i))
    mat_a = pl.BlockSpec((width, cols), lambda i: (0, jnp.minimum(i, per - 1)))
    mat_b = pl.BlockSpec((width, cols), lambda i: (0, jnp.maximum(i - per, 0)))
    shape = jax.ShapeDtypeStruct((width, hidden), jnp.bfloat16)
    return pl.pallas_call(
        back_outer_kernel,
        grid=(2 * per,),
        in_specs=[full_spec((rows, width)), full_spec((width, rows)), tile, tile, mat_a, mat_b],
        out_specs=[mat_a, mat_b, tile],
        out_shape=[shape, shape, jax.ShapeDtypeStruct(act.shape, jnp.bfloat16)],
        compiler_params=params(VMEM_MIB),
        cost_estimate=cost(9e-6),
        name="back_outer",
    )(grad, grad_t, act, slope, w_a, w_b)


def back_inner_kernel(xt_ref, gpre_ref, a_ref, b_ref, wga_ref, wgb_ref, out_ref, acc):
    step = pl.program_id(0)

    @pl.when(step == 0)
    def _():
        acc[...] = jnp.zeros_like(acc)

    def work(w_ref, wg_ref):
        wg_ref[...] = dot(xt_ref[...], gpre_ref[...]).astype(wg_ref.dtype)
        acc[...] += dot(gpre_ref[...], w_ref[...], NT)

    first = step < pl.num_programs(0) // 2
    pl.when(first)(lambda: work(a_ref, wga_ref))
    pl.when(jnp.logical_not(first))(lambda: work(b_ref, wgb_ref))

    @pl.when(step == pl.num_programs(0) - 1)
    def _():
        out_ref[...] = acc[...].astype(out_ref.dtype)


def back_inner(x_t, grad_pre, w_a, w_b, hidden):
    width, rows = x_t.shape
    cols = 384
    per = hidden // cols
    mat_a = pl.BlockSpec((width, cols), lambda i: (0, jnp.minimum(i, per - 1)))
    mat_b = pl.BlockSpec((width, cols), lambda i: (0, jnp.maximum(i - per, 0)))
    shape = jax.ShapeDtypeStruct((width, hidden), jnp.bfloat16)
    return pl.pallas_call(
        back_inner_kernel,
        grid=(2 * per,),
        in_specs=[
            full_spec((width, rows)),
            pl.BlockSpec((rows, cols), lambda i: (0, i)),
            mat_a,
            mat_b,
        ],
        out_specs=[mat_a, mat_b, full_spec((rows, width))],
        out_shape=[shape, shape, jax.ShapeDtypeStruct((rows, width), jnp.bfloat16)],
        scratch_shapes=[pltpu.VMEM((rows, width), jnp.float32)],
        compiler_params=params(VMEM_MIB),
        cost_estimate=cost(9e-6),
        name="back_inner",
    )(x_t, grad_pre, w_a, w_b)


def first_back_kernel(
    mine_ref,
    got_ref,
    gh2_ref,
    normed_ref,
    inv_ref,
    norms,
    ow_ref,
    low_ref,
    high_ref,
    pg_ref,
    vec2_ref,
    gh1_ref,
    gmix_ref,
    og_ref,
    small_ref,
    og_acc,
    vec,
):
    step = pl.program_id(0)
    steps = pl.num_programs(0)

    @pl.when(step == 0)
    def _():
        og_acc[...] = jnp.zeros_like(og_acc)
        vec[...] = jnp.zeros_like(vec)
        vec[2:4, :] = vec2_ref[0:2, :]

    grad = gh2_ref[...] + (wide(mine_ref) + wide(got_ref))
    normed = normed_ref[...]
    vec[0:1, :] += jnp.sum(grad * normed, axis=0, keepdims=True)
    vec[1:2, :] += jnp.sum(grad, axis=0, keepdims=True)
    grad_h1 = norm_backward(grad, normed, inv_ref[:, 0:1], norms[0:1, :])
    gh1_ref[...] = grad_h1
    low = grad_h1.astype(jnp.bfloat16)
    gmix_ref[...] = dot(low, ow_ref[...]).astype(gmix_ref.dtype)
    mixed = jnp.where(step < steps // 2, low_ref[...], high_ref[...])
    og_acc[...] += dot(low, mixed, TN)

    @pl.when(step == steps - 1)
    def _():
        og_ref[...] = og_acc[...].astype(og_ref.dtype)
        p_width = pg_ref.shape[1]
        small_ref[:, :p_width] = pg_ref[...].astype(small_ref.dtype)
        small_ref[:, p_width:] = vec[...].T.astype(small_ref.dtype)


def first_back(mine, got, grad_h2, normed, inv, norms, output_w, mixed, proj_part, vec2):
    rows, width = grad_h2.shape
    cols = output_w.shape[1]
    block = 256
    per = rows // block // 2
    tile = rows_spec(block, width)
    low = jnp.bfloat16
    p_width = proj_part.shape[1]
    return pl.pallas_call(
        first_back_kernel,
        grid=(2 * per,),
        in_specs=[
            tile,
            tile,
            tile,
            tile,
            rows_spec(block, 128),
            full_spec(norms.shape),
            full_spec(output_w.shape),
            pl.BlockSpec((block, cols), lambda i: (jnp.minimum(i, per - 1), 0)),
            pl.BlockSpec((block, cols), lambda i: (jnp.maximum(i - per, 0), 0)),
            full_spec(proj_part.shape),
            full_spec(vec2.shape),
        ],
        out_specs=[
            tile,
            rows_spec(block, cols),
            full_spec((width, cols)),
            full_spec((width, p_width + 128)),
        ],
        out_shape=[
            jax.ShapeDtypeStruct((rows, width), jnp.float32),
            jax.ShapeDtypeStruct((rows, cols), low),
            jax.ShapeDtypeStruct((width, cols), low),
            jax.ShapeDtypeStruct((width, p_width + 128), low),
        ],
        scratch_shapes=[pltpu.VMEM((width, cols), jnp.float32), pltpu.VMEM((128, width), jnp.float32)],
        compiler_params=params(VMEM_MIB),
        cost_estimate=cost(6e-6),
        name="first_back",
    )(mine, got, grad_h2, normed, inv, norms, output_w, *mixed, proj_part, vec2)


def far_kernel(dk, dv, wk, wv, gx_ref):
    gx_ref[...] = (dot(dk[...], wk[...], NT) + dot(dv[...], wv[...], NT)).astype(gx_ref.dtype)


def far_grads(dk, dv, key_w, value_w):
    rows = dk.shape[0] // 2
    width, cols = key_w.shape
    block = 512
    tile = pl.BlockSpec((block, cols), lambda i: (i + rows // block, 0))
    return pl.pallas_call(
        far_kernel,
        grid=(rows // block,),
        in_specs=[tile] * 2 + [full_spec((width, cols))] * 2,
        out_specs=rows_spec(block, width),
        out_shape=jax.ShapeDtypeStruct((rows, width), jnp.bfloat16),
        compiler_params=params(VMEM_MIB),
        cost_estimate=cost(3e-6),
        name="far_grads",
    )(dk, dv, key_w, value_w)


def head_grads_kernel(x_ref, dq, dk, dv, wq, wk, wv, og_ref, gx_ref, a_ref, b_ref, acc):
    step = pl.program_id(0)
    steps = pl.num_programs(0)

    @pl.when(step == 0)
    def _():
        acc[...] = jnp.zeros_like(acc)

    x_t = x_ref[...].T
    acc[1] += dot(x_t, dk[...])
    acc[2] += dot(x_t, dv[...])

    @pl.when(step < steps // 2)
    def _():
        acc[0] += dot(x_t, dq[...])
        gx = dot(dk[...], wk[...], NT) + dot(dv[...], wv[...], NT) + dot(dq[...], wq[...], NT)
        gx_ref[...] = gx.astype(gx_ref.dtype)

    @pl.when(step == steps - 1)
    def _():
        for s, out in enumerate((a_ref, b_ref)):
            for i in range(4):
                part = og_ref if i == 3 else acc.at[i]
                lo = 128 * s
                out[:, 128 * i : 128 * i + 128] = part[:, lo : lo + 128].astype(out.dtype)
            for i in (0, 2):
                lo = 256 + DH * s
                both = [
                    (og_ref if j == 3 else acc.at[j])[:, lo : lo + DH].astype(out.dtype)
                    for j in (i, i + 1)
                ]
                out[:, 512 + DH * i : 512 + DH * i + 128] = jnp.concatenate(both, axis=1)


def head_grads(tok_all, dq, dk, dv, weights, output_part):
    span, width = tok_all.shape
    block = 512
    steps = span // block
    cols = dq.shape[1]
    low = jnp.bfloat16
    near = lambda i: (jnp.minimum(i, steps // 2 - 1), 0)
    packed = full_spec((width, 768))
    return pl.pallas_call(
        head_grads_kernel,
        grid=(steps,),
        in_specs=[
            rows_spec(block, width),
            pl.BlockSpec((block, cols), near),
            rows_spec(block, cols),
            rows_spec(block, cols),
        ]
        + [full_spec((width, cols))] * 4,
        out_specs=[pl.BlockSpec((block, width), near), packed, packed],
        out_shape=[
            jax.ShapeDtypeStruct((span // 2, width), low),
            jax.ShapeDtypeStruct((width, 768), low),
            jax.ShapeDtypeStruct((width, 768), low),
        ],
        scratch_shapes=[pltpu.VMEM((3, width, cols), jnp.float32)],
        compiler_params=params(VMEM_MIB),
        cost_estimate=cost(9e-6),
        name="head_grads",
    )(tok_all, dq, dk, dv, *weights, output_part)


def unpack_heads(packed):
    return [
        jnp.concatenate(
            [packed[:, 128 * i : 128 * i + 128], packed[:, 512 + DH * i : 512 + DH * i + DH]], axis=1
        )
        for i in range(4)
    ]


def per_device(
    tokens,
    segments,
    query_weight,
    key_weight,
    value_weight,
    output_weight,
    attn_gain,
    attn_shift,
    inner_weight,
    outer_weight,
    ffn_gain,
    ffn_shift,
    proj_weight,
    grad_embed,
):
    length, model_width = tokens.shape[2:]
    half = length // 2
    core = lax.axis_index("shard") % 2
    ctx = lax.axis_index("ctx")
    group = lax.axis_index("tp")
    micro, seat = group // 2, group % 2
    owner = core == seat
    edge = min(SEG_MOST, length)
    bf16, f32 = jnp.bfloat16, jnp.float32

    tok_m = lax.dynamic_index_in_dim(tokens, micro, 0, False)[0]
    sent = lax.dynamic_slice_in_dim(tok_m, (1 - ctx) * (length - edge), edge, 0)
    got = route(sent, lambda s, c, t: (s, 1 - c, t) if s % 2 == t % 2 else None)
    heads_own = pack_heads(query_weight, key_weight, value_weight)
    heads_parts = gather_tp_start(heads_own)
    tokens_in, segments_in, outer_in, output_in, cot_in = after_all(
        heads_own, tokens, segments, outer_weight, output_weight, grad_embed
    )
    vectors = jnp.stack([attn_gain, attn_shift, ffn_gain, ffn_shift])
    vectors = dot(vectors, jnp.eye(4, 64, dtype=bf16), TN).astype(bf16)
    ffn_own = jnp.concatenate([inner_weight, output_in.T, proj_weight, vectors, outer_in.T], axis=1)
    ffn_all = lax.all_gather(ffn_own, "tp", axis=0)
    tok_m = lax.dynamic_index_in_dim(tokens_in, micro, 0, False)[0]
    tok_got = swap(tok_m, "shard", 1)
    seg_m = lax.dynamic_index_in_dim(segments_in, micro, 0, False)
    seg_m = seg_m.reshape(1, -1, 128)
    upto = jnp.arange(8, dtype=jnp.int32).reshape(8, 1, 1)
    counts_own = jnp.sum((seg_m <= upto).astype(jnp.int32), axis=(1, 2))
    counts_got = swap(counts_own, "shard", 1)

    heads_a, heads_b = gather_tp_finish(tie(*heads_parts, ffn_own, counts_own)[:4])
    other_a, other_b = gather_start(heads_a, "y"), gather_start(heads_b, "x")
    cot_m = lax.dynamic_index_in_dim(after(cot_in, heads_a), micro, 0, False)[0]
    cot_got = swap(cot_m, "shard", 1)
    other_a, other_b, got, tok_got, counts_got = tie(other_a, other_b, got, tok_got, counts_got)
    heads_a, heads_b = gather_finish(heads_a, other_a, "y"), gather_finish(heads_b, other_b, "x")
    other_a, other_b = gather_start(heads_a, "x"), gather_start(heads_b, "y")
    got_core = swap(got, "shard", 1)
    counts = jnp.where(owner, counts_own, counts_got)
    counts = counts + swap(counts, "ctx", 1)
    place_of = jnp.arange(8)
    ends = jnp.where(place_of == SEG_COUNT, ctx * length, counts).astype(jnp.int32)
    tok_here = jnp.where(owner, tok_m, tok_got)
    tok_far = lax.dynamic_update_slice_in_dim(
        jnp.zeros_like(tok_here), jnp.where(owner, got, got_core), ctx * (length - edge), 0
    )
    tok_all = jnp.concatenate([tok_here, tok_far], axis=0)
    cot = jnp.where(owner, cot_m, cot_got)
    other_a, other_b, tok_all, cot, ends = tie(other_a, other_b, tok_all, cot, ends)
    heads_a, heads_b = gather_finish(heads_a, other_a, "x"), gather_finish(heads_b, other_b, "y")

    queries, keys, values, *head_w = project(tok_all, flat_rows(heads_a), flat_rows(heads_b))
    ffn_all = after(ffn_all, heads_a, heads_b)
    kept = lax.dynamic_slice_in_dim(ffn_all, 2 * core, 2, 0)
    other = swap(lax.dynamic_slice_in_dim(ffn_all, 2 - 2 * core, 2, 0), "shard", 1)
    other, queries, keys, values = tie(other, queries, keys, values)
    core_dim = shard_bits() - 1
    shape = (1,) * core_dim + (1, 1) + ffn_own.shape
    split = 1152
    inner, outer = [], []
    for s in range(2):
        both = join(kept[s].reshape(shape), other[s].reshape(shape), "shard", 1, core_dim)
        inner.append(both[..., :split])
        outer.append(both[..., split:])
    inner_got = [gather_start(inner[0], "x"), gather_start(inner[1], "y")]
    outer_got = [gather_start(outer[0], "x"), gather_start(outer[1], "y")]
    mixed_low, lse_low = attn_forward(after(ends, *inner, *outer), 0, queries, keys, values)
    inner_got = after_all(mixed_low, *inner_got)
    inner = [gather_finish(inner[0], inner_got[0], "x"), gather_finish(inner[1], inner_got[1], "y")]
    inner_got = [gather_start(inner[0], "y"), gather_start(inner[1], "x")]
    mixed_high, lse_high = attn_forward(
        after(ends, mixed_low, *inner), half // BQ, queries, keys, values
    )
    outer_got = after_all(mixed_high, *outer_got)
    outer = [gather_finish(outer[0], outer_got[0], "x"), gather_finish(outer[1], outer_got[1], "y")]
    outer_got = [gather_start(outer[0], "y"), gather_start(outer[1], "x")]
    inner_got = after_all(mixed_high, *inner_got)
    inner_got = after_all(outer[0], *inner_got)
    inner_a = flat_rows(gather_finish(inner[0], inner_got[0], "y"))
    inner_b = flat_rows(gather_finish(inner[1], inner_got[1], "x"))
    mixed = (mixed_low, mixed_high)
    part, output_w, proj, norms = attn_out(mixed, inner_a, inner_b)

    hidden_cols = outer_weight.shape[0]
    normed, inv, first_low, first_t = first_norm(tok_here, part, swap(part, "shard", 1), norms)
    act, slope = ffn_in(first_low, inner_a, inner_b, hidden_cols)
    outer_got = after_all(act, *outer_got)
    outer_a = flat_rows(gather_finish(outer[0], outer_got[0], "y"))
    outer_b = flat_rows(gather_finish(outer[1], outer_got[1], "x"))
    part = ffn_out(act, outer_a, outer_b)
    embedding, grad_h2, grad_ffn, grad_ffn_t, proj_part, vec2 = middle(
        normed, part, swap(part, "shard", 1), norms, proj, cot
    )

    outer_a, outer_b, grad_pre = back_outer(grad_ffn, grad_ffn_t, act, slope, outer_a, outer_b)
    outer = [split_rows(outer_a), split_rows(outer_b)]
    outer_got = [scatter_start(outer[0], "x"), scatter_start(outer[1], "y")]
    inner_a, inner_b, part = back_inner(
        first_t, after(grad_pre, *outer), inner_a, inner_b, hidden_cols
    )
    part_got = swap(part, "shard", 1)
    inner = [split_rows(inner_a), split_rows(inner_b)]
    inner_got = [scatter_start(inner[0], "x"), scatter_start(inner[1], "y")]
    outer_got = after_all(part, *outer_got)
    outer = [
        scatter_finish(outer[0], outer_got[0], "x"),
        scatter_finish(outer[1], outer_got[1], "y"),
    ]
    outer_got = [scatter_start(outer[0], "y"), scatter_start(outer[1], "x")]
    grad_h1, grad_mixed, output_part, small = first_back(
        part,
        after(part_got, *outer, *inner),
        grad_h2,
        normed,
        inv,
        norms,
        output_w,
        mixed,
        proj_part,
        vec2,
    )
    inner_got = after_all(grad_mixed, *inner_got)
    inner = [
        scatter_finish(inner[0], inner_got[0], "x"),
        scatter_finish(inner[1], inner_got[1], "y"),
    ]
    inner_got = [scatter_start(inner[0], "y"), scatter_start(inner[1], "x")]
    outer_got = after_all(grad_mixed, *outer_got)
    outer = [
        scatter_finish(outer[0], outer_got[0], "y"),
        scatter_finish(outer[1], outer_got[1], "x"),
    ]
    outer_parts = scatter_tp_start(*outer)

    small = lax.dynamic_slice_in_dim(split_rows(small), core, 1, core_dim)
    small_got = scatter_start(small, "y")
    quarter = half // 2
    emb_half = lax.dynamic_slice_in_dim(after(embedding, grad_mixed), core * half, half, 0)
    emb_got = [
        route(
            lax.select_n(micro ^ d, emb_half[:quarter], emb_half[quarter:]),
            lambda s, c, t, d=d: (s - s % 2 + t % 2, c, 2 * (s % 2) + ((t // 2) ^ d)),
        )
        for d in range(2)
    ]
    dq, dk, dv = attn_backward(
        after(ends, *inner, *outer, small, emb_half),
        queries,
        grad_mixed,
        mixed,
        (lse_low, lse_high),
        keys,
        values,
    )

    def start_half(full):
        return swap(lax.dynamic_slice_in_dim(full, (1 - core) * half, half, 0), "shard", 1)

    def sum_half(full, got_half):
        kept_half = lax.dynamic_slice_in_dim(full, core * half, half, 0)
        return kept_half.astype(f32) + got_half.astype(f32)

    gx_far = far_grads(dk, dv, *head_w[1:])
    far_got = start_half(gx_far)
    *inner_got, small_got = after_all(gx_far, *inner_got, small_got)
    inner = [
        scatter_finish(inner[0], inner_got[0], "y"),
        scatter_finish(inner[1], inner_got[1], "x"),
    ]
    small = scatter_finish(small, small_got, "y")
    small_got = scatter_start(small, "x")
    far_sum = sum_half(gx_far, after(far_got, *inner, small)).astype(bf16)
    from_far = swap(far_sum, "ctx", 1)
    inner_parts = scatter_tp_start(*inner)
    gx, grad_a, grad_b = head_grads(
        after(tok_all, far_sum, *inner), dq, dk, dv, head_w, output_part
    )
    gx_got = start_half(gx)
    grad_a, grad_b = split_rows(grad_a), split_rows(grad_b)
    got_a, got_b = scatter_start(grad_a, "y"), scatter_start(grad_b, "x")
    outer_parts = after_all(gx, *outer_parts)
    outer_grad = sum_all(outer_parts).reshape(-1, hidden_cols).T
    small = scatter_finish(small, after(small_got, gx), "x").reshape(-1, small.shape[-1])
    small_parts = [small] + [swap(small, "tp", d) for d in range(1, 4)]
    mine = lax.dynamic_slice_in_dim(grad_h1, core * half, half, 0)
    gx_sum = sum_half(gx, gx_got)
    grad_tok = (gx_sum + after(from_far, gx_got).astype(f32) + mine).astype(bf16)
    own_cols = model_width // lax.axis_size("tp")
    col_parts = [grad_tok[:, own_cols * j : own_cols * (j + 1)] for j in range(4)]
    place = 2 * micro + core
    arrived = [
        route(
            lax.select_n(place ^ d, *col_parts),
            lambda s, c, t, d=d: (s - s % 2 + t % 2, c, (2 * (t // 2) + s % 2) ^ d),
        )
        for d in range(4)
    ]
    got_a, got_b, *inner_parts = after_all(grad_tok, got_a, got_b, *inner_parts)
    grad_a, grad_b = scatter_finish(grad_a, got_a, "y"), scatter_finish(grad_b, got_b, "x")
    got_a, got_b = scatter_start(grad_a, "x"), scatter_start(grad_b, "y")
    *inner_parts, small_last = after_all((grad_a, grad_b), *inner_parts, small_parts[-1])
    inner_grad = sum_all(inner_parts).reshape(-1, hidden_cols)
    small = sum_all(small_parts[:3] + [small_last])
    emb_got = after_all(grad_tok, *emb_got)
    embeddings = jnp.stack([lax.select_n((group % 2) ^ m, *emb_got) for m in range(2)])
    embeddings = embeddings.reshape(2, 1, quarter, -1)
    got_a, got_b = after_all(inner_grad, got_a, got_b)
    grad_a, grad_b = scatter_finish(grad_a, got_a, "x"), scatter_finish(grad_b, got_b, "y")
    heads_grad = sum_all(scatter_tp_start(grad_a, grad_b))
    heads_grad = heads_grad.reshape(-1, heads_grad.shape[-1])
    arrived = after_all((grad_a, grad_b), *arrived)
    grad_tokens = jnp.stack([lax.select_n(group ^ j, *arrived) for j in range(4)])
    grad_tokens = grad_tokens.reshape(2, 1, length, own_cols).astype(f32)
    query_grad, key_grad, value_grad, output_grad = unpack_heads(heads_grad)
    p_width = proj_part.shape[1]
    return (
        embeddings,
        grad_tokens,
        query_grad,
        key_grad,
        value_grad,
        output_grad.T,
        small[:, p_width],
        small[:, p_width + 1],
        inner_grad,
        outer_grad,
        small[:, p_width + 2],
        small[:, p_width + 3],
        small[:, :p_width],
    )


def solution(mesh):
    rows = ("shard", "ctx")
    placed = (
        P(None, "shard", "ctx", None),
        P(None, "shard", "ctx"),
        P(rows, "tp"),
        P(rows, "tp"),
        P(rows, "tp"),
        P("tp", rows),
        P(rows),
        P(rows),
        P(rows, "tp"),
        P("tp", rows),
        P(rows),
        P(rows),
        P(rows, None),
        P(None, "shard", "ctx", None),
    )
    return jax.shard_map(
        per_device,
        mesh=mesh,
        in_specs=placed,
        out_specs=(
            P(None, "shard", ("ctx", "tp"), None),
            P(None, "shard", "ctx", "tp"),
            P(rows, "tp"),
            P(rows, "tp"),
            P(rows, "tp"),
            P("tp", rows),
            P(rows),
            P(rows),
            P(rows, "tp"),
            P("tp", rows),
            P(rows),
            P(rows),
            P(rows, None),
        ),
        check_vma=False,
    )
```

```python
import functools

import jax
import jax.numpy as jnp
from jax import lax
from jax.experimental import pallas as pl
from jax.experimental.pallas import tpu as pltpu
from jax.sharding import PartitionSpec as P

DH = 64
SEG_COUNT = 6
SEG_MOST = 800
BQ = 256
BK = 256
VMEM_MIB = 34

eps_norm = 1e-12
eps_unit = 1e-06
mask_fill = -1e30

NN = (((1,), (0,)), ((), ()))
NT = (((1,), (1,)), ((), ()))
TN = (((0,), (0,)), ((), ()))


def dot(first_op, second_op, dims=NN):
    return lax.dot_general(first_op, second_op, dims, preferred_element_type=jnp.float32)


def tie(*values):
    return lax.optimization_barrier(values)


def after(value, *others):
    return lax.optimization_barrier((value, *others))[0]


def after_all(done, *values):
    return lax.optimization_barrier((done, *values))[1:]


def swap(v, axis, bit):
    count = lax.axis_size(axis)
    return lax.ppermute(v, axis, [(i, i ^ bit) for i in range(count)])


def route(v, target):
    shards, halves, groups = (lax.axis_size(a) for a in ("shard", "ctx", "tp"))

    def flat(s, c, t):
        return (s * halves + c) * groups + t

    pairs = []
    for s in range(shards):
        for c in range(halves):
            for t in range(groups):
                to = target(s, c, t)
                if to is not None:
                    pairs.append((flat(s, c, t), flat(*to)))
    return lax.ppermute(v, ("shard", "ctx", "tp"), pairs)


def shard_bits():
    return lax.axis_size("shard").bit_length() - 1


def steps_of(name):
    bits = shard_bits()
    if name == "x":
        return [("ctx", 1, bits)]
    return [("shard", 1 << i, bits - 1 - i) for i in range(bits - 1, 0, -1)]


def my_bit(axis, bit):
    return (lax.axis_index(axis) // bit) % 2


def gather_tp_start(own):
    return [
        route(
            own,
            lambda s, c, t, d=d: (s - s % 2 + t // 2, c, (2 * (s % 2) + t % 2) ^ d),
        )
        for d in range(4)
    ]


def gather_tp_finish(parts):
    t = lax.axis_index("tp")
    dim = shard_bits() - 1
    shape = (1,) * dim + (1, 1) + parts[0].shape
    return [
        jnp.concatenate(
            [lax.select_n(t ^ (2 * j + s), *parts).reshape(shape) for j in range(2)], axis=dim
        )
        for s in range(2)
    ]


def join(cur, other, axis, bit, dim):
    first = my_bit(axis, bit) == 0
    return jnp.concatenate([jnp.where(first, cur, other), jnp.where(first, other, cur)], axis=dim)


def gather_start(cur, name):
    axis, bit, _ = steps_of(name)[0]
    return swap(cur, axis, bit)


def gather_finish(cur, other, name):
    first, *rest = steps_of(name)
    cur = join(cur, other, *first)
    for axis, bit, dim in rest:
        cur = join(cur, swap(cur, axis, bit), axis, bit, dim)
    return cur


def flat_rows(cur):
    return cur.reshape(-1, cur.shape[-1])


def split_rows(full):
    rows = full.shape[-2] // (lax.axis_size("shard") * lax.axis_size("ctx"))
    return full.reshape(full.shape[:-2] + (2,) * (shard_bits() + 1) + (rows, full.shape[-1]))


def scatter_start(cur, name, lead=0):
    axis, bit, dim = steps_of(name)[0]
    return swap(lax.dynamic_slice_in_dim(cur, 1 - my_bit(axis, bit), 1, dim + lead), axis, bit)


def scatter_finish(cur, other, name, lead=0):
    first, *rest = steps_of(name)
    kept = lax.dynamic_slice_in_dim(cur, my_bit(*first[:2]), 1, first[2] + lead)
    cur = (kept.astype(jnp.float32) + other.astype(jnp.float32)).astype(jnp.bfloat16)
    for axis, bit, dim in rest:
        mine = my_bit(axis, bit)
        other = swap(lax.dynamic_slice_in_dim(cur, 1 - mine, 1, dim + lead), axis, bit)
        kept = lax.dynamic_slice_in_dim(cur, mine, 1, dim + lead)
        cur = (kept.astype(jnp.float32) + other.astype(jnp.float32)).astype(jnp.bfloat16)
    return cur


def scatter_rest(cur, name, lead=0):
    for axis, bit, dim in steps_of(name)[1:]:
        mine = my_bit(axis, bit)
        other = swap(lax.dynamic_slice_in_dim(cur, 1 - mine, 1, dim + lead), axis, bit)
        kept = lax.dynamic_slice_in_dim(cur, mine, 1, dim + lead)
        cur = (kept.astype(jnp.float32) + other.astype(jnp.float32)).astype(jnp.bfloat16)
    return cur


def scatter_tp_start(first, second):
    z = lax.axis_index("tp")
    blocks = [lax.index_in_dim(s, j, s.ndim - 4, False) for j in range(2) for s in (first, second)]
    return [
        route(
            lax.select_n(z ^ d, *blocks),
            lambda s, c, t, d=d: (s - s % 2 + ((t ^ d) >> 1), c, 2 * (s % 2) + ((t ^ d) & 1)),
        )
        for d in range(4)
    ]


def sum_all(parts):
    total = parts[0].astype(jnp.float32)
    for part in parts[1:]:
        total = total + part.astype(jnp.float32)
    return total


def two_heads(pair):
    lane = lax.broadcasted_iota(jnp.int32, pair.shape, 1)
    zero = jnp.zeros_like(pair)
    return jnp.concatenate(
        [jnp.where(lane < DH, pair, zero), jnp.where(lane < DH, zero, pair)], axis=0
    )


def fold_heads(wide):
    rows = wide.shape[1] // 2
    both = jnp.concatenate([wide[:DH, :rows], wide[DH:, rows:]], axis=0)
    return both.T


def document(ends, start, stop, most):
    low, high = start * 0, start * 0 + most
    for d in range(SEG_COUNT):
        low = jnp.maximum(low, jnp.where(ends[d] <= start, ends[d], 0))
        high = jnp.minimum(high, jnp.where(ends[d] > stop, ends[d], most))
    return low, high


def key_blocks(ends, qb, span):
    length = span // 2
    here = ends[SEG_COUNT]
    far = length - here
    start = here + qb * BQ
    low, high = document(ends, start, start + BQ - 1, span)
    first = jnp.clip(low - here, 0, length) // BK
    count = (jnp.clip(high - here, 0, length) + (BK - 1)) // BK - first
    first_far = jnp.clip(low - far, 0, length) // BK
    count_far = (jnp.clip(high - far, 0, length) + (BK - 1)) // BK - first_far
    count_far = jnp.maximum(count_far, 0)

    def block(i):
        is_here = i < count
        kb = jnp.where(is_here, first + i, length // BK + first_far + (i - count))
        return kb, kb * BK + jnp.where(is_here, here, far - length)

    return count + count_far, block


def query_bounds(ends, qb, span):
    pos = ends[SEG_COUNT] + qb * BQ + lax.broadcasted_iota(jnp.int32, (1, BQ), 1)
    return document(ends, pos, pos, span)


def key_mask(bounds, base):
    key_pos = lax.broadcasted_iota(jnp.int32, (BK, BQ), 0) + base
    same = (key_pos >= bounds[0]) & (key_pos < bounds[1])
    return jnp.concatenate([same, same], axis=1)


def attn_fwd_kernel(first_block, ends, q_ref, k_ref, v_ref, o_ref, lse_ref, acc, top, den):
    span = k_ref.shape[0]
    qb = pl.program_id(0) + first_block
    pairs = q_ref.shape[1] // 128
    acc[...] = jnp.zeros_like(acc)
    top[...] = jnp.full_like(top, mask_fill)
    den[...] = jnp.zeros_like(den)
    queries = [two_heads(q_ref[:, 128 * p : 128 * p + 128]) for p in range(pairs)]
    bounds = query_bounds(ends, qb, span)
    count, block = key_blocks(ends, qb, span)

    @pl.loop(0, count)
    def _(i):
        kb, base = block(i)
        rows = pl.ds(pl.multiple_of(kb * BK, BK), BK)
        same = key_mask(bounds, base)
        for p in range(pairs):
            cols = slice(128 * p, 128 * p + 128)
            s = dot(k_ref[rows, cols], queries[p], NT)
            s = jnp.where(same, s, mask_fill)
            old = top[p]
            new = jnp.maximum(old, jnp.max(s, axis=0, keepdims=True))
            e = jnp.exp(s - new)
            shrink = jnp.exp(old - new)
            den[p] = den[p] * shrink + jnp.sum(e, axis=0, keepdims=True)
            top[p] = new
            acc[p] = acc[p] * shrink + dot(v_ref[rows, cols], e.astype(jnp.bfloat16), TN)

    for p in range(pairs):
        out = fold_heads(acc[p] / den[p])
        o_ref[:, 128 * p : 128 * p + 128] = out.astype(o_ref.dtype)
        lse_ref[p] = top[p] + jnp.log(den[p])


def row_sums(grads, outs):
    prod = (grads.astype(jnp.float32) * outs.astype(jnp.float32)).T
    return jnp.concatenate(
        [jnp.sum(prod[:DH], axis=0, keepdims=True), jnp.sum(prod[DH:], axis=0, keepdims=True)],
        axis=1,
    )


def attn_bwd_kernel(
    ends,
    q_ref,
    do_ref,
    o_low,
    o_high,
    lse_low,
    lse_high,
    k_ref,
    v_ref,
    dq_ref,
    dk_ref,
    dv_ref,
    dk_acc,
    dv_acc,
    dq_acc,
):
    span = k_ref.shape[0]
    qb = pl.program_id(0)
    is_low = qb < pl.num_programs(0) // 2
    pairs = q_ref.shape[1] // 128
    cols = [slice(128 * p, 128 * p + 128) for p in range(pairs)]

    @pl.when(qb == 0)
    def _():
        dk_acc[...] = jnp.zeros_like(dk_acc)
        dv_acc[...] = jnp.zeros_like(dv_acc)

    dq_acc[...] = jnp.zeros_like(dq_acc)
    outs = jnp.where(is_low, o_low[...], o_high[...])
    lses = jnp.where(is_low, lse_low[...], lse_high[...])
    queries = [two_heads(q_ref[:, c]) for c in cols]
    grads = [two_heads(do_ref[:, c]) for c in cols]
    deltas = [row_sums(do_ref[:, c], outs[:, c]) for c in cols]
    bounds = query_bounds(ends, qb, span)
    count, block = key_blocks(ends, qb, span)

    @pl.loop(0, count)
    def _(i):
        kb, base = block(i)
        rows = pl.ds(pl.multiple_of(kb * BK, BK), BK)
        same = key_mask(bounds, base)
        for p, c in enumerate(cols):
            keys = k_ref[rows, c]
            s = dot(keys, queries[p], NT)
            probs = jnp.exp(jnp.where(same, s, mask_fill) - lses[p])
            dp = dot(v_ref[rows, c], grads[p], NT)
            ds = (probs * (dp - deltas[p])).astype(jnp.bfloat16)
            dv_acc[rows, c] += dot(probs.astype(jnp.bfloat16), grads[p])
            dk_acc[rows, c] += dot(ds, queries[p])
            dq_acc[p] += dot(keys, ds, TN)

    for p, c in enumerate(cols):
        dq_ref[:, c] = (fold_heads(dq_acc[p]) * (DH**-0.5)).astype(dq_ref.dtype)

    @pl.when(qb == pl.num_programs(0) - 1)
    def _():
        dk_ref[...] = dk_acc[...].astype(dk_ref.dtype)
        dv_ref[...] = dv_acc[...].astype(dv_ref.dtype)


def params(mib):
    return pltpu.CompilerParams(vmem_limit_bytes=mib * 2**20)


def cost(seconds):
    return pl.CostEstimate(flops=int(seconds * 1.15e15), bytes_accessed=2**20, transcendentals=0)


def attn_forward(ends, first_block, queries, keys, values):
    rows, width = queries.shape
    span = keys.shape[0]
    pairs = width // 128
    every = pl.BlockSpec((span, width), lambda i, e: (0, 0))
    return pl.pallas_call(
        functools.partial(attn_fwd_kernel, first_block),
        grid_spec=pltpu.PrefetchScalarGridSpec(
            num_scalar_prefetch=1,
            grid=(rows // BQ // 2,),
            in_specs=[
                pl.BlockSpec((BQ, width), lambda i, e: (i + first_block, 0)),
                every,
                every,
            ],
            out_specs=[
                pl.BlockSpec((BQ, width), lambda i, e: (i, 0)),
                pl.BlockSpec((pairs, 1, 2 * BQ), lambda i, e: (0, 0, i)),
            ],
            scratch_shapes=[
                pltpu.VMEM((pairs, 128, 2 * BQ), jnp.float32),
                pltpu.VMEM((pairs, 1, 2 * BQ), jnp.float32),
                pltpu.VMEM((pairs, 1, 2 * BQ), jnp.float32),
            ],
        ),
        out_shape=[
            jax.ShapeDtypeStruct((rows // 2, width), jnp.bfloat16),
            jax.ShapeDtypeStruct((pairs, 1, rows), jnp.float32),
        ],
        compiler_params=params(VMEM_MIB),
        cost_estimate=cost(10e-6),
        name="attn_fwd",
    )(ends, queries, keys, values)


def attn_backward(ends, start, pairs, queries, grads, mixed, lse, keys, values):
    rows = queries.shape[0]
    span = keys.shape[0]
    half = rows // BQ // 2
    width = 128 * pairs
    col = start // pairs
    tile = pl.BlockSpec((BQ, width), lambda i, e: (i, col))
    low = pl.BlockSpec((BQ, width), lambda i, e: (jnp.minimum(i, half - 1), col))
    high = pl.BlockSpec((BQ, width), lambda i, e: (jnp.maximum(i - half, 0), col))
    low_line = pl.BlockSpec((pairs, 1, 2 * BQ), lambda i, e: (col, 0, jnp.minimum(i, half - 1)))
    high_line = pl.BlockSpec((pairs, 1, 2 * BQ), lambda i, e: (col, 0, jnp.maximum(i - half, 0)))
    every = pl.BlockSpec((span, width), lambda i, e: (0, col))
    out = pl.BlockSpec((span, width), lambda i, e: (0, 0))
    shape = jax.ShapeDtypeStruct((span, width), jnp.bfloat16)
    return pl.pallas_call(
        attn_bwd_kernel,
        grid_spec=pltpu.PrefetchScalarGridSpec(
            num_scalar_prefetch=1,
            grid=(rows // BQ,),
            in_specs=[tile, tile, low, high, low_line, high_line, every, every],
            out_specs=[pl.BlockSpec((BQ, width), lambda i, e: (i, 0)), out, out],
            scratch_shapes=[
                pltpu.VMEM((span, width), jnp.float32),
                pltpu.VMEM((span, width), jnp.float32),
                pltpu.VMEM((pairs, 128, 2 * BQ), jnp.float32),
            ],
        ),
        out_shape=[jax.ShapeDtypeStruct((rows, width), jnp.bfloat16), shape, shape],
        compiler_params=params(VMEM_MIB),
        cost_estimate=cost(1e-6 * pairs),
        name="attn_bwd",
    )(ends, queries, grads, *mixed, *lse, keys, values)


def full_spec(shape):
    return pl.BlockSpec(shape, lambda i: (0,) * len(shape))


def rows_spec(rows, cols):
    return pl.BlockSpec((rows, cols), lambda i: (i, 0))


def pack_kernel(q_ref, k_ref, v_ref, out_ref):
    parts = [q_ref[...], k_ref[...], v_ref[...]]
    for i, part in enumerate(parts):
        out_ref[:, 128 * i : 128 * i + 128] = part[:, :128]
    thirds = [p[:, 128:] for p in parts]
    thirds.append(jnp.zeros_like(thirds[0]))
    out_ref[:, 384:512] = jnp.concatenate(thirds[:2], axis=1)
    out_ref[:, 512:640] = jnp.concatenate(thirds[2:], axis=1)


def pack_heads(*parts):
    return pl.pallas_call(
        pack_kernel,
        out_shape=jax.ShapeDtypeStruct((parts[0].shape[0], 640), parts[0].dtype),
        compiler_params=params(8),
        cost_estimate=cost(1e-6),
        name="pack_heads",
    )(*parts)


def build_heads(outs, a_ref, b_ref):
    for i, out in enumerate(outs):
        lo = 384 + DH * i
        out[:, :128] = a_ref[:, 128 * i : 128 * i + 128]
        out[:, 128:256] = b_ref[:, 128 * i : 128 * i + 128]
        out[:, 256:] = jnp.concatenate([a_ref[:, lo : lo + DH], b_ref[:, lo : lo + DH]], axis=1)


def qkv_kernel(x_ref, a_ref, b_ref, q_ref, k_ref, v_ref, wq, wk, wv):
    step = pl.program_id(0)

    @pl.when(step == 0)
    def _():
        build_heads((wq, wk, wv), a_ref, b_ref)

    x = x_ref[...]
    k_ref[...] = dot(x, wk[...]).astype(k_ref.dtype)
    v_ref[...] = dot(x, wv[...]).astype(v_ref.dtype)

    @pl.when(step < pl.num_programs(0) // 2)
    def _():
        q = dot(x, wq[...]).astype(jnp.bfloat16).astype(jnp.float32)
        q_ref[...] = (q * DH**-0.5).astype(q_ref.dtype)


def project(tok_all, w_a, w_b):
    span, width = tok_all.shape
    block = 512
    steps = span // block
    cols = 384
    low = jnp.bfloat16
    return pl.pallas_call(
        qkv_kernel,
        grid=(steps,),
        in_specs=[rows_spec(block, width), full_spec(w_a.shape), full_spec(w_b.shape)],
        out_specs=[
            pl.BlockSpec((block, cols), lambda i: (jnp.minimum(i, steps // 2 - 1), 0)),
            rows_spec(block, cols),
            rows_spec(block, cols),
        ],
        out_shape=[
            jax.ShapeDtypeStruct((span // 2, cols), low),
            jax.ShapeDtypeStruct((span, cols), low),
            jax.ShapeDtypeStruct((span, cols), low),
        ],
        scratch_shapes=[pltpu.VMEM((width, cols), low)] * 3,
        compiler_params=params(VMEM_MIB),
        cost_estimate=cost(6e-6),
        name="qkv",
    )(tok_all, w_a, w_b)


def attn_out_kernel(low_ref, high_ref, a_ref, b_ref, part_ref, ow_ref, proj_ref, norms_ref):
    step = pl.program_id(0)

    @pl.when(step == 0)
    def _():
        ow_ref[:, :128] = a_ref[:, :128]
        ow_ref[:, 128:256] = b_ref[:, :128]
        ow_ref[:, 256:] = jnp.concatenate([a_ref[:, 128:192], b_ref[:, 128:192]], axis=1)
        proj_ref[...] = a_ref[:, 192:320]
        turned = a_ref[:, 256:384].astype(jnp.float32).T
        norms_ref[...] = turned[64:72]

    mixed = jnp.where(step < pl.num_programs(0) // 2, low_ref[...], high_ref[...])
    part_ref[...] = dot(mixed, ow_ref[...], NT).astype(part_ref.dtype)


def attn_out(mixed, w_a, w_b):
    half, cols = mixed[0].shape
    width = w_a.shape[0]
    block = 256
    per = half // block
    low = jnp.bfloat16
    third = pl.BlockSpec((width, 384), lambda i: (0, w_a.shape[1] // 384 - 1))
    return pl.pallas_call(
        attn_out_kernel,
        grid=(2 * per,),
        in_specs=[
            pl.BlockSpec((block, cols), lambda i: (jnp.minimum(i, per - 1), 0)),
            pl.BlockSpec((block, cols), lambda i: (jnp.maximum(i - per, 0), 0)),
            third,
            third,
        ],
        out_specs=[
            rows_spec(block, width),
            full_spec((width, cols)),
            full_spec((width, 128)),
            full_spec((8, width)),
        ],
        out_shape=[
            jax.ShapeDtypeStruct((2 * half, width), low),
            jax.ShapeDtypeStruct((width, cols), low),
            jax.ShapeDtypeStruct((width, 128), low),
            jax.ShapeDtypeStruct((8, width), jnp.float32),
        ],
        compiler_params=params(VMEM_MIB),
        cost_estimate=cost(3e-6),
        name="attn_out",
    )(*mixed, w_a, w_b)


def normalize(hidden):
    row_mean = jnp.mean(hidden, axis=-1, keepdims=True)
    centred = hidden - row_mean
    variance = jnp.mean(centred * centred, axis=-1, keepdims=True)
    inv_std = lax.rsqrt(variance + eps_norm)
    return centred * inv_std, inv_std


def norm_backward(grad_out, normed, inv_std, gain):
    scaled = grad_out * gain
    return inv_std * (
        scaled
        - jnp.mean(scaled, axis=-1, keepdims=True)
        - normed * jnp.mean(scaled * normed, axis=-1, keepdims=True)
    )


def wide(ref):
    return ref[...].astype(jnp.float32)


def gelu_parts(v):
    e = jnp.exp(v * v * -0.5)
    t = 1.0 / (1.0 + (0.3275911 * 0.5**0.5) * jnp.abs(v))
    poly = 0.5 * 1.061405429
    for c in (-1.453152027, 1.421413741, -0.284496736, 0.254829592):
        poly = poly * t + 0.5 * c
    upper = poly * t * e
    cdf = jnp.where(v >= 0, 1.0 - upper, upper)
    return v * cdf, cdf + v * e * 0.3989422804014327


def ffn_kernel(
    x_ref, mine_ref, got_ref, norms, ia, ib, normed_ref, inv_ref, low_ref, act_ref, slope_ref
):
    step = pl.program_id(0)
    steps = pl.num_programs(0)
    parts = [slice(r, r + 256) for r in range(0, x_ref.shape[0], 256)]

    @pl.when(step == 0)
    def _():
        for rows in parts:
            hidden = x_ref[rows, :].astype(jnp.float32) + (
                mine_ref[rows, :].astype(jnp.float32) + got_ref[rows, :].astype(jnp.float32)
            )
            normed, inv = normalize(hidden)
            normed_ref[rows, :] = normed.astype(normed_ref.dtype)
            inv_ref[rows, :] = jnp.broadcast_to(inv, (256, 128))
            low_ref[rows, :] = (normed * norms[0:1, :] + norms[1:2, :]).astype(low_ref.dtype)

    def work(i_ref):
        for rows in parts:
            act, slope = gelu_parts(dot(low_ref[rows, :], i_ref[...]))
            act_ref[rows, :] = act.astype(act_ref.dtype)
            slope_ref[rows, :] = slope.astype(slope_ref.dtype)

    first = step < steps // 2
    pl.when(first)(lambda: work(ia))
    pl.when(jnp.logical_not(first))(lambda: work(ib))


def slice_specs(width, cols, per):
    return [
        pl.BlockSpec((width, cols), lambda i: (0, jnp.minimum(i, per - 1))),
        pl.BlockSpec((width, cols), lambda i: (0, jnp.maximum(i - per, 0))),
    ]


FFN_COLS = 256
GROUPS = 1


def feed_forward(tok, mine, got, norms, inner, hidden):
    rows, width = tok.shape
    cols = FFN_COLS
    per = hidden // cols
    tile = full_spec((rows, width))
    chunk = pl.BlockSpec((rows, cols), lambda i: (0, i))
    low = jax.ShapeDtypeStruct((rows, width), jnp.bfloat16)
    units = jax.ShapeDtypeStruct((rows, 2 * hidden), jnp.bfloat16)
    return pl.pallas_call(
        ffn_kernel,
        grid=(2 * per,),
        in_specs=[tile, tile, tile, full_spec(norms.shape)]
        + slice_specs(width, cols, per),
        out_specs=[tile, full_spec((rows, 128)), tile, chunk, chunk],
        out_shape=[low, jax.ShapeDtypeStruct((rows, 128), jnp.float32), low, units, units],
        compiler_params=params(VMEM_MIB),
        cost_estimate=cost(14e-6),
        name="feed_forward",
    )(tok, mine, got, norms, *inner)


def ffn_out_kernel(act_ref, a_ref, b_ref, out_ref):
    hidden = a_ref.shape[1]
    part = dot(act_ref[:, :hidden], a_ref[...], NT) + dot(act_ref[:, hidden:], b_ref[...], NT)
    out_ref[...] = part.astype(out_ref.dtype)


def ffn_out(act, w_a, w_b):
    rows = act.shape[0]
    width = w_a.shape[0]
    block = 256
    return pl.pallas_call(
        ffn_out_kernel,
        grid=(rows // block,),
        in_specs=[rows_spec(block, act.shape[1]), full_spec(w_a.shape), full_spec(w_b.shape)],
        out_specs=rows_spec(block, width),
        out_shape=jax.ShapeDtypeStruct((rows, width), jnp.bfloat16),
        compiler_params=params(VMEM_MIB),
        cost_estimate=cost(3e-6),
        name="ffn_out",
    )(act, w_a, w_b)


def middle_kernel(
    normed_ref, mine_ref, got_ref, norms, proj_ref, cot_ref, emb_ref, gh2_ref, low_ref, pg_ref, vec_ref
):
    step = pl.program_id(0)
    first = wide(normed_ref) * norms[0:1, :] + norms[1:2, :]
    normed, inv = normalize(first + (wide(mine_ref) + wide(got_ref)))
    second = (normed * norms[2:3, :] + norms[3:4, :]).astype(jnp.bfloat16)
    projected = dot(second, proj_ref[...])
    inv_norm = lax.rsqrt(jnp.sum(projected * projected, axis=-1, keepdims=True) + eps_unit)
    embedding = projected * inv_norm
    emb_ref[...] = embedding
    cot = wide(cot_ref)
    radial = jnp.sum(cot * embedding, axis=-1, keepdims=True)
    grad_projected = (inv_norm * (cot - embedding * radial)).astype(jnp.bfloat16)
    grad_second = dot(grad_projected, proj_ref[...], NT)
    grad = norm_backward(grad_second, normed, inv, norms[2:3, :])
    gh2_ref[...] = grad
    low_ref[...] = grad.astype(low_ref.dtype)

    @pl.when(step == 0)
    def _():
        pg_ref[...] = jnp.zeros_like(pg_ref)
        vec_ref[...] = jnp.zeros_like(vec_ref)

    pg_ref[...] += dot(second, grad_projected, TN)
    vec_ref[0:1, :] += jnp.sum(grad_second * normed, axis=0, keepdims=True)
    vec_ref[1:2, :] += jnp.sum(grad_second, axis=0, keepdims=True)


def middle(normed, mine, got, norms, proj, cot):
    rows, width = normed.shape
    p_width = proj.shape[1]
    block = 256
    tile = rows_spec(block, width)
    return pl.pallas_call(
        middle_kernel,
        grid=(rows // block,),
        in_specs=[
            tile,
            tile,
            tile,
            full_spec(norms.shape),
            full_spec(proj.shape),
            rows_spec(block, p_width),
        ],
        out_specs=[
            rows_spec(block, p_width),
            tile,
            tile,
            full_spec((width, p_width)),
            full_spec((8, width)),
        ],
        out_shape=[
            jax.ShapeDtypeStruct((rows, p_width), jnp.float32),
            jax.ShapeDtypeStruct((rows, width), jnp.float32),
            jax.ShapeDtypeStruct((rows, width), jnp.bfloat16),
            jax.ShapeDtypeStruct((width, p_width), jnp.float32),
            jax.ShapeDtypeStruct((8, width), jnp.float32),
        ],
        compiler_params=params(VMEM_MIB),
        cost_estimate=cost(5e-6),
        name="middle",
    )(normed, mine, got, norms, proj, cot)


def ffn_back_kernel(
    turns, bits, g_ref, x_ref, act_ref, slope_ref, ia, ib, oa, ob, keep_a, send_a, keep_b, send_b, out_ref, acc, g_t, x_t, wgrad
):
    step = pl.program_id(0)
    steps = pl.num_programs(0)

    @pl.when(step == 0)
    def _():
        g_t[...] = g_ref[...].T
        x_t[...] = x_ref[...].T
        acc[...] = jnp.zeros_like(acc)

    def put(which, run, keep, send, bit):
        for j in range(keep.shape[1] // run):
            for out, side in ((keep, bit), (send, 1 - bit)):
                rows = pl.ds(pl.multiple_of((2 * j + side) * run, run), run)
                out[which, j * run : (j + 1) * run, :] = wgrad[rows, :].astype(out.dtype)

    def work(i_ref, o_ref, run, keep, send, bit):
        wgrad[...] = dot(g_t[...], act_ref[...])
        put(0, run, keep, send, bit)
        grad = dot(g_ref[...], o_ref[...]) * slope_ref[...].astype(jnp.float32)
        grad = grad.astype(jnp.bfloat16)
        wgrad[...] = dot(x_t[...], grad)
        put(1, run, keep, send, bit)
        acc[...] += dot(grad, i_ref[...], NT)

    first = step < steps // 2
    pl.when(first)(lambda: work(ia, oa, turns[0], keep_a, send_a, bits[0]))
    pl.when(jnp.logical_not(first))(lambda: work(ib, ob, turns[1], keep_b, send_b, bits[1]))

    @pl.when(step == steps - 1)
    def _():
        out_ref[...] = acc[...].astype(out_ref.dtype)


def ffn_back(bits, turns, grad, x, act, slope, inner, outer, hidden):
    rows, width = grad.shape
    cols = FFN_COLS
    per = hidden // cols

    def left(i):
        return jnp.minimum(i, per - 1)

    def right(i):
        return jnp.maximum(i - per, 0)

    tile = pl.BlockSpec((rows, width), lambda i, e: (0, 0))
    chunk = pl.BlockSpec((rows, cols), lambda i, e: (0, i))
    mats = [
        pl.BlockSpec((width, cols), lambda i, e: (0, left(i))),
        pl.BlockSpec((width, cols), lambda i, e: (0, right(i))),
    ]
    outs = [
        pl.BlockSpec((2, width // 2, cols), lambda i, e: (0, 0, left(i))),
        pl.BlockSpec((2, width // 2, cols), lambda i, e: (0, 0, right(i))),
    ]
    low = jnp.bfloat16
    shape = jax.ShapeDtypeStruct((2, width // 2, hidden), low)
    return pl.pallas_call(
        functools.partial(ffn_back_kernel, turns),
        grid_spec=pltpu.PrefetchScalarGridSpec(
            num_scalar_prefetch=1,
            grid=(2 * per,),
            in_specs=[tile, tile, chunk, chunk] + mats * 2,
            out_specs=[outs[0], outs[0], outs[1], outs[1], tile],
            scratch_shapes=[
                pltpu.VMEM((rows, width), jnp.float32),
                pltpu.VMEM((width, rows), low),
                pltpu.VMEM((width, rows), low),
                pltpu.VMEM((width, cols), jnp.float32),
            ],
        ),
        out_shape=[shape] * 4 + [jax.ShapeDtypeStruct((rows, width), low)],
        compiler_params=params(VMEM_MIB),
        cost_estimate=cost(17e-6),
        name="ffn_back",
    )(bits, grad, x, act, slope, *inner, *outer)


def first_back_kernel(
    mine_ref,
    got_ref,
    gh2_ref,
    normed_ref,
    inv_ref,
    norms,
    ow_ref,
    low_ref,
    high_ref,
    pg_ref,
    vec2_ref,
    gh1_ref,
    gmix_ref,
    og_ref,
    small_ref,
    og_acc,
    vec,
):
    step = pl.program_id(0)
    steps = pl.num_programs(0)

    @pl.when(step == 0)
    def _():
        og_acc[...] = jnp.zeros_like(og_acc)
        vec[...] = jnp.zeros_like(vec)
        vec[2:4, :] = vec2_ref[0:2, :]

    grad = gh2_ref[...] + (wide(mine_ref) + wide(got_ref))
    normed = wide(normed_ref)
    vec[0:1, :] += jnp.sum(grad * normed, axis=0, keepdims=True)
    vec[1:2, :] += jnp.sum(grad, axis=0, keepdims=True)
    grad_h1 = norm_backward(grad, normed, inv_ref[:, 0:1], norms[0:1, :])
    gh1_ref[...] = grad_h1
    low = grad_h1.astype(jnp.bfloat16)
    gmix_ref[...] = dot(low, ow_ref[...]).astype(gmix_ref.dtype)
    mixed = jnp.where(step < steps // 2, low_ref[...], high_ref[...])
    og_acc[...] += dot(low, mixed, TN)

    @pl.when(step == steps - 1)
    def _():
        og_ref[...] = og_acc[...].astype(og_ref.dtype)
        p_width = pg_ref.shape[1]
        small_ref[:, :p_width] = pg_ref[...].astype(small_ref.dtype)
        small_ref[:, p_width:] = vec[...].T.astype(small_ref.dtype)


def first_back(mine, got, grad_h2, normed, inv, norms, output_w, mixed, proj_part, vec2):
    rows, width = grad_h2.shape
    cols = output_w.shape[1]
    block = 256
    per = rows // block // 2
    tile = rows_spec(block, width)
    low = jnp.bfloat16
    p_width = proj_part.shape[1]
    return pl.pallas_call(
        first_back_kernel,
        grid=(2 * per,),
        in_specs=[
            tile,
            tile,
            tile,
            tile,
            rows_spec(block, 128),
            full_spec(norms.shape),
            full_spec(output_w.shape),
            pl.BlockSpec((block, cols), lambda i: (jnp.minimum(i, per - 1), 0)),
            pl.BlockSpec((block, cols), lambda i: (jnp.maximum(i - per, 0), 0)),
            full_spec(proj_part.shape),
            full_spec(vec2.shape),
        ],
        out_specs=[
            tile,
            rows_spec(block, cols),
            full_spec((width, cols)),
            full_spec((width, p_width + 128)),
        ],
        out_shape=[
            jax.ShapeDtypeStruct((rows, width), jnp.float32),
            jax.ShapeDtypeStruct((rows, cols), low),
            jax.ShapeDtypeStruct((width, cols), low),
            jax.ShapeDtypeStruct((width, p_width + 128), low),
        ],
        scratch_shapes=[pltpu.VMEM((width, cols), jnp.float32), pltpu.VMEM((128, width), jnp.float32)],
        compiler_params=params(VMEM_MIB),
        cost_estimate=cost(1e-6),
        name="first_back",
    )(mine, got, grad_h2, normed, inv, norms, output_w, *mixed, proj_part, vec2)


def token_grads_kernel(core, *refs):
    *parts, a_ref, b_ref, theirs, mine, wq, wk, wv = refs
    step = pl.program_id(0)
    weights = (wq, wk, wv)[-(len(parts) // GROUPS) :]

    @pl.when(step == 0)
    def _():
        build_heads((wq, wk, wv), a_ref, b_ref)

    total = 0.0
    for i, w in enumerate(weights):
        grads = [parts[p * len(weights) + i][...] for p in range(GROUPS)]
        total = total + dot(jnp.concatenate(grads, axis=1), w[...], NT)

    @pl.when(step == 0)
    def _():
        theirs[...] = total.astype(theirs.dtype)

    @pl.when(step == 1)
    def _():
        mine[...] = total.astype(mine.dtype)


def token_grads(core, far, grads, w_a, w_b):
    half = grads[0][0].shape[0] // 2
    width = w_a.shape[0]
    skip = 2 if far else 0
    used = [arrays[1:] if far else arrays for arrays in grads]
    rows = lambda i, core: (skip + jnp.where(i < 1, 1 - core[0], core[0]), 0)
    specs = [pl.BlockSpec((half, x.shape[1]), rows) for arrays in used for x in arrays]
    mat = pl.BlockSpec(w_a.shape, lambda i, core: (0, 0))
    shape = jax.ShapeDtypeStruct((half, width), jnp.bfloat16)
    whole = pl.BlockSpec((half, width), lambda i, core: (0, 0))
    return pl.pallas_call(
        token_grads_kernel,
        grid_spec=pltpu.PrefetchScalarGridSpec(
            num_scalar_prefetch=1,
            grid=(2,),
            in_specs=specs + [mat, mat],
            out_specs=[whole, whole],
            scratch_shapes=[pltpu.VMEM((width, 384), jnp.bfloat16)] * 3,
        ),
        out_shape=[shape, shape],
        compiler_params=params(VMEM_MIB),
        cost_estimate=cost(0.5e-6),
        name="token_grads",
    )(core.reshape(1), *[x for arrays in used for x in arrays], w_a, w_b)


def head_grads_kernel(x_ref, *refs):
    *parts, og_ref, a_ref, b_ref, acc = refs
    step = pl.program_id(0)
    steps = pl.num_programs(0)

    @pl.when(step == 0)
    def _():
        acc[...] = jnp.zeros_like(acc)

    x_t = x_ref[...].T

    def add(i):
        grads = [parts[3 * p + i][...] for p in range(GROUPS)]
        acc[i] += dot(x_t, jnp.concatenate(grads, axis=1))

    add(1)
    add(2)
    pl.when(step < steps // 2)(lambda: add(0))

    @pl.when(step == steps - 1)
    def _():
        for s, out in enumerate((a_ref, b_ref)):
            for i in range(4):
                part = og_ref if i == 3 else acc.at[i]
                lo = 128 * s
                out[:, 128 * i : 128 * i + 128] = part[:, lo : lo + 128].astype(out.dtype)
            for i in (0, 2):
                lo = 256 + DH * s
                both = [
                    (og_ref if j == 3 else acc.at[j])[:, lo : lo + DH].astype(out.dtype)
                    for j in (i, i + 1)
                ]
                out[:, 512 + DH * i : 512 + DH * i + 128] = jnp.concatenate(both, axis=1)


def head_grads(tok_all, grads, output_part):
    span, width = tok_all.shape
    block = 512
    steps = span // block
    near = lambda i: (jnp.minimum(i, steps // 2 - 1), 0)
    specs = []
    for dq, _, _ in grads:
        cols = dq.shape[1]
        specs += [pl.BlockSpec((block, cols), near), rows_spec(block, cols), rows_spec(block, cols)]
    packed = full_spec((width, 768))
    shape = jax.ShapeDtypeStruct((width, 768), jnp.bfloat16)
    return pl.pallas_call(
        head_grads_kernel,
        grid=(steps,),
        in_specs=[rows_spec(block, width)] + specs + [full_spec(output_part.shape)],
        out_specs=[packed, packed],
        out_shape=[shape, shape],
        scratch_shapes=[pltpu.VMEM((3, width, 384), jnp.float32)],
        compiler_params=params(VMEM_MIB),
        cost_estimate=cost(0.5e-6),
        name="head_grads",
    )(tok_all, *[x for arrays in grads for x in arrays], output_part)


def unpack_heads(packed):
    return [
        jnp.concatenate(
            [packed[:, 128 * i : 128 * i + 128], packed[:, 512 + DH * i : 512 + DH * i + DH]], axis=1
        )
        for i in range(4)
    ]


def per_device(
    tokens,
    segments,
    query_weight,
    key_weight,
    value_weight,
    output_weight,
    attn_gain,
    attn_shift,
    inner_weight,
    outer_weight,
    ffn_gain,
    ffn_shift,
    proj_weight,
    grad_embed,
):
    length, model_width = tokens.shape[2:]
    half = length // 2
    core = lax.axis_index("shard") % 2
    ctx = lax.axis_index("ctx")
    group = lax.axis_index("tp")
    micro, seat = group // 2, group % 2
    owner = core == seat
    edge = min(SEG_MOST, length)
    bf16, f32 = jnp.bfloat16, jnp.float32

    def by_core(mine, theirs, axis):
        return jnp.concatenate(
            [jnp.where(core == 0, mine, theirs), jnp.where(core == 0, theirs, mine)], axis=axis
        )

    tok_m = lax.dynamic_index_in_dim(tokens, micro, 0, False)[0]
    sent = lax.dynamic_slice_in_dim(tok_m, (1 - ctx) * (length - edge), edge, 0)
    got = route(sent, lambda s, c, t: (s, 1 - c, t) if s % 2 == t % 2 else None)
    heads_own = pack_heads(query_weight, key_weight, value_weight)
    heads_parts = gather_tp_start(heads_own)
    tokens_in, segments_in, outer_in, output_in, cot_in = after_all(
        heads_own, tokens, segments, outer_weight, output_weight, grad_embed
    )
    vectors = jnp.stack([attn_gain, attn_shift, ffn_gain, ffn_shift])
    vectors = dot(vectors, jnp.eye(4, 64, dtype=bf16), TN).astype(bf16)
    ffn_own = jnp.concatenate([inner_weight, output_in.T, proj_weight, vectors, outer_in.T], axis=1)
    ffn_all = lax.all_gather(ffn_own, "tp", axis=0)
    tok_m = lax.dynamic_index_in_dim(tokens_in, micro, 0, False)[0]

    *heads_parts, got, ffn_own, tok_m, segments_in, cot_in = tie(
        *heads_parts, got, ffn_own, tok_m, segments_in, cot_in
    )
    heads_a, heads_b = gather_tp_finish(heads_parts)
    other_a, other_b = gather_start(heads_a, "y"), gather_start(heads_b, "x")
    tok_got = swap(tok_m, "shard", 1)
    seg_m = lax.dynamic_index_in_dim(segments_in, micro, 0, False)
    seg_m = seg_m.reshape(1, -1, 128)
    upto = jnp.arange(8, dtype=jnp.int32).reshape(8, 1, 1)
    counts_own = jnp.sum((seg_m <= upto).astype(jnp.int32), axis=(1, 2))
    counts_got = swap(counts_own, "shard", 1)
    cot_m = lax.dynamic_index_in_dim(cot_in, micro, 0, False)[0]
    other_a, other_b, tok_got, counts_got, cot_m = tie(other_a, other_b, tok_got, counts_got, cot_m)
    heads_a, heads_b = gather_finish(heads_a, other_a, "y"), gather_finish(heads_b, other_b, "x")
    other_a, other_b = gather_start(heads_a, "x"), gather_start(heads_b, "y")
    got_core = swap(got, "shard", 1)
    cot_got = swap(cot_m, "shard", 1)
    counts = jnp.where(owner, counts_own, counts_got)
    counts = counts + swap(counts, "ctx", 1)
    place_of = jnp.arange(8)
    ends = jnp.where(place_of == SEG_COUNT, ctx * length, counts).astype(jnp.int32)
    tok_here = jnp.where(owner, tok_m, tok_got)
    tok_far = lax.dynamic_update_slice_in_dim(
        jnp.zeros_like(tok_here), jnp.where(owner, got, got_core), ctx * (length - edge), 0
    )
    tok_all = jnp.concatenate([tok_here, tok_far], axis=0)
    cot = jnp.where(owner, cot_m, cot_got)
    other_a, other_b, tok_all, cot, ends = tie(other_a, other_b, tok_all, cot, ends)
    heads_a, heads_b = gather_finish(heads_a, other_a, "x"), gather_finish(heads_b, other_b, "y")
    heads_a, heads_b = flat_rows(heads_a), flat_rows(heads_b)

    core_dim = shard_bits() - 1
    queries, keys, values = project(tok_all, heads_a, heads_b)
    ffn_all = after(ffn_all, keys)
    kept = lax.dynamic_slice_in_dim(ffn_all, 2 * core, 2, 0)
    other = swap(lax.dynamic_slice_in_dim(ffn_all, 2 - 2 * core, 2, 0), "shard", 1)
    shape = (1,) * core_dim + (1, 1) + ffn_own.shape
    split = inner_weight.shape[1] + 384
    inner, outer = [], []
    for s in range(2):
        both = join(kept[s].reshape(shape), other[s].reshape(shape), "shard", 1, core_dim)
        inner.append(both[..., :split])
        outer.append(both[..., split:])
    inner_got = [gather_start(inner[0], "x"), gather_start(inner[1], "y")]
    outer_got = [gather_start(outer[0], "x"), gather_start(outer[1], "y")]
    mixed_low, lse_low = attn_forward(after(ends, *inner, *outer), 0, queries, keys, values)
    mixed_low, *inner_got = tie(mixed_low, *inner_got)
    inner = [gather_finish(inner[0], inner_got[0], "x"), gather_finish(inner[1], inner_got[1], "y")]
    inner_got = [gather_start(inner[0], "y"), gather_start(inner[1], "x")]
    mixed_high, lse_high = attn_forward(
        after(ends, mixed_low, *inner), half // BQ, queries, keys, values
    )
    mixed_high, *got_all = tie(mixed_high, *inner_got, *outer_got)
    outer = [gather_finish(outer[0], got_all[2], "x"), gather_finish(outer[1], got_all[3], "y")]
    outer_got = [gather_start(outer[0], "y"), gather_start(outer[1], "x")]
    inner = [
        flat_rows(gather_finish(inner[0], got_all[0], "y")),
        flat_rows(gather_finish(inner[1], got_all[1], "x")),
    ]
    mixed = (mixed_low, mixed_high)
    part, output_w, proj, norms = attn_out(mixed, *inner)

    hidden_cols = outer_weight.shape[0]
    normed, inv, first_low, act, slope = feed_forward(
        tok_here, part, swap(part, "shard", 1), norms, inner, hidden_cols
    )
    act, *outer_got = tie(act, *outer_got)
    outer = [
        flat_rows(gather_finish(outer[0], outer_got[0], "y")),
        flat_rows(gather_finish(outer[1], outer_got[1], "x")),
    ]
    part = ffn_out(act, *outer)
    embedding, grad_h2, grad_ffn, proj_part, vec2 = middle(
        normed, part, swap(part, "shard", 1), norms, proj, cot
    )

    rows = model_width // (lax.axis_size("shard") * lax.axis_size("ctx"))
    y_axis, y_bit, _ = steps_of("y")[0]
    y_mine = my_bit(y_axis, y_bit)
    x_first = rows % 16 == 0
    bits = jnp.stack([ctx if x_first else y_mine, y_mine]).astype(jnp.int32)
    turns = (rows if x_first else model_width // 2, model_width // 2)
    keep_a, send_a, keep_b, send_b, part = ffn_back(
        bits, turns, grad_ffn, first_low, act, slope, inner, outer, hidden_cols
    )
    wgrad_got = [
        swap(send_a, "ctx", 1) if x_first else swap(send_a, y_axis, y_bit),
        swap(send_b, y_axis, y_bit),
    ]
    part_got = swap(part, "shard", 1)
    grad_h1, grad_mixed, output_part, small = first_back(
        part, part_got, grad_h2, normed, inv, norms, output_w, mixed, proj_part, vec2
    )

    small = lax.dynamic_slice_in_dim(split_rows(small), core, 1, core_dim)
    small_got = scatter_start(small, "y")
    quarter = half // 2
    emb_half = lax.dynamic_slice_in_dim(after(embedding, grad_mixed), core * half, half, 0)
    emb_got = [
        route(
            lax.select_n(micro ^ d, emb_half[:quarter], emb_half[quarter:]),
            lambda s, c, t, d=d: (s - s % 2 + t % 2, c, 2 * (s % 2) + ((t // 2) ^ d)),
        )
        for d in range(2)
    ]
    flow = (queries, grad_mixed, mixed, (lse_low, lse_high), keys, values)
    grads = attn_backward(after(ends, small, emb_half), 0, 3, *flow)
    *grads, wgrad_got[0], wgrad_got[1], small_got, emb_got[0], emb_got[1] = tie(
        *grads, *wgrad_got, small_got, *emb_got
    )
    grads = [grads]

    def added(kept, got):
        return (kept.astype(f32) + got.astype(f32)).astype(bf16)

    theirs, far_mine = token_grads(core, True, grads, heads_a, heads_b)
    far_got = swap(theirs, "shard", 1)
    wgrad_got = after_all(theirs, *wgrad_got)
    lead = (2,) * (shard_bits() - 1)
    last = (rows, hidden_cols)
    shapes = [(2, *lead, 2, 1, *last), (2, 1, *lead[1:], 2, 2, *last)]
    second_steps = ("y" if x_first else "x", "x")
    wgrad = [
        added(keep_a, wgrad_got[0]).reshape(shapes[0 if x_first else 1]),
        added(keep_b, wgrad_got[1]).reshape(shapes[1]),
    ]
    wgrad = [scatter_rest(w, "y", 1) if n == "x" else w for w, n in zip(wgrad, second_steps)]
    far_got, *wgrad = tie(far_got, *wgrad)
    far_sum = added(far_mine, far_got)
    from_far = swap(far_sum, "ctx", 1)
    wgrad_got = [scatter_start(w, n, 1) for w, n in zip(after_all(far_sum, *wgrad), second_steps)]
    small = scatter_finish(small, after(small_got, far_sum), "y")
    small_got = scatter_start(small, "x")
    theirs, near_mine = token_grads(core, False, grads, after(heads_a, far_sum, *wgrad), heads_b)
    near_got = swap(theirs, "shard", 1)
    grad_a, grad_b = head_grads(after(tok_all, theirs), grads, output_part)
    grad_a, grad_b, near_got, *wgrad_got = tie(grad_a, grad_b, near_got, *wgrad_got)
    grad_a, grad_b = split_rows(grad_a), split_rows(grad_b)
    got_a, got_b = scatter_start(grad_a, "y"), scatter_start(grad_b, "x")
    wgrad = [scatter_finish(w, g, n, 1) for w, g, n in zip(wgrad, wgrad_got, second_steps)]
    mine = lax.dynamic_slice_in_dim(grad_h1, core * half, half, 0)
    near_sum = near_mine.astype(f32) + near_got.astype(f32) + mine
    small = scatter_finish(small, after(small_got, near_sum), "x").reshape(-1, small.shape[-1])
    near_sum, from_far, small, *wgrad = tie(near_sum, from_far, small, *wgrad)
    grad_tok = (near_sum + from_far.astype(f32)).astype(bf16)
    wgrad_parts = scatter_tp_start(*wgrad)
    own_cols = model_width // lax.axis_size("tp")
    col_parts = [grad_tok[:, own_cols * j : own_cols * (j + 1)] for j in range(4)]
    place = 2 * micro + core
    arrived = [
        route(
            lax.select_n(place ^ d, *col_parts),
            lambda s, c, t, d=d: (s - s % 2 + t % 2, c, (2 * (t // 2) + s % 2) ^ d),
        )
        for d in range(4)
    ]
    small_parts = [small] + [swap(small, "tp", d) for d in range(1, 4)]
    got_a, got_b = after_all(grad_tok, got_a, got_b)
    grad_a, grad_b = scatter_finish(grad_a, got_a, "y"), scatter_finish(grad_b, got_b, "x")
    got_a, got_b = scatter_start(grad_a, "x"), scatter_start(grad_b, "y")
    wgrad_parts = after_all((grad_a, grad_b), *wgrad_parts)
    wgrad_sum = sum_all(wgrad_parts).reshape(2, -1, hidden_cols)
    outer_grad, inner_grad = wgrad_sum[0].T, wgrad_sum[1]
    small = sum_all(small_parts)
    embeddings = jnp.stack([lax.select_n((group % 2) ^ m, *emb_got) for m in range(2)])
    embeddings = embeddings.reshape(2, 1, quarter, -1)
    got_a, got_b = after_all(inner_grad, got_a, got_b)
    grad_a, grad_b = scatter_finish(grad_a, got_a, "x"), scatter_finish(grad_b, got_b, "y")
    arrived = after_all((grad_a, grad_b), *arrived)
    heads_grad = sum_all(scatter_tp_start(grad_a, grad_b))
    heads_grad = heads_grad.reshape(-1, heads_grad.shape[-1])
    grad_tokens = jnp.stack([lax.select_n(group ^ j, *arrived) for j in range(4)])
    grad_tokens = grad_tokens.reshape(2, 1, length, own_cols).astype(f32)
    query_grad, key_grad, value_grad, output_grad = unpack_heads(heads_grad)
    p_width = proj_part.shape[1]
    return (
        embeddings,
        grad_tokens,
        query_grad,
        key_grad,
        value_grad,
        output_grad.T,
        small[:, p_width],
        small[:, p_width + 1],
        inner_grad,
        outer_grad,
        small[:, p_width + 2],
        small[:, p_width + 3],
        small[:, :p_width],
    )


def solution(mesh):
    rows = ("shard", "ctx")
    placed = (
        P(None, "shard", "ctx", None),
        P(None, "shard", "ctx"),
        P(rows, "tp"),
        P(rows, "tp"),
        P(rows, "tp"),
        P("tp", rows),
        P(rows),
        P(rows),
        P(rows, "tp"),
        P("tp", rows),
        P(rows),
        P(rows),
        P(rows, None),
        P(None, "shard", "ctx", None),
    )
    return jax.shard_map(
        per_device,
        mesh=mesh,
        in_specs=placed,
        out_specs=(
            P(None, "shard", ("ctx", "tp"), None),
            P(None, "shard", "ctx", "tp"),
            P(rows, "tp"),
            P(rows, "tp"),
            P(rows, "tp"),
            P("tp", rows),
            P(rows),
            P(rows),
            P(rows, "tp"),
            P("tp", rows),
            P(rows),
            P(rows),
            P(rows, None),
        ),
        check_vma=False,
    )
```

```python
import functools

import jax
import jax.numpy as jnp
from jax import lax
from jax.experimental import pallas as pl
from jax.experimental.pallas import tpu as pltpu
from jax.sharding import PartitionSpec as P

DH = 64
SEG_COUNT = 6
SEG_MOST = 800
BQ = 256
BK = 256
VMEM_MIB = 34

eps_norm = 1e-12
eps_unit = 1e-06
mask_fill = -1e30

NN = (((1,), (0,)), ((), ()))
NT = (((1,), (1,)), ((), ()))
TN = (((0,), (0,)), ((), ()))


def dot(first_op, second_op, dims=NN):
    return lax.dot_general(first_op, second_op, dims, preferred_element_type=jnp.float32)


def tie(*values):
    return lax.optimization_barrier(values)


def after(value, *others):
    return lax.optimization_barrier((value, *others))[0]


def after_all(done, *values):
    return lax.optimization_barrier((done, *values))[1:]


def swap(v, axis, bit):
    count = lax.axis_size(axis)
    return lax.ppermute(v, axis, [(i, i ^ bit) for i in range(count)])


def route(v, target):
    shards, halves, groups = (lax.axis_size(a) for a in ("shard", "ctx", "tp"))

    def flat(s, c, t):
        return (s * halves + c) * groups + t

    pairs = []
    for s in range(shards):
        for c in range(halves):
            for t in range(groups):
                to = target(s, c, t)
                if to is not None:
                    pairs.append((flat(s, c, t), flat(*to)))
    return lax.ppermute(v, ("shard", "ctx", "tp"), pairs)


def shard_bits():
    return lax.axis_size("shard").bit_length() - 1


def steps_of(name):
    bits = shard_bits()
    if name == "x":
        return [("ctx", 1, bits)]
    return [("shard", 1 << i, bits - 1 - i) for i in range(bits - 1, 0, -1)]


def my_bit(axis, bit):
    return (lax.axis_index(axis) // bit) % 2


def gather_tp_start(own):
    return [
        route(
            own,
            lambda s, c, t, d=d: (s - s % 2 + t // 2, c, (2 * (s % 2) + t % 2) ^ d),
        )
        for d in range(4)
    ]


def gather_tp_finish(parts):
    t = lax.axis_index("tp")
    dim = shard_bits() - 1
    shape = (1,) * dim + (1, 1) + parts[0].shape
    return [
        jnp.concatenate(
            [lax.select_n(t ^ (2 * j + s), *parts).reshape(shape) for j in range(2)], axis=dim
        )
        for s in range(2)
    ]


def join(cur, other, axis, bit, dim):
    first = my_bit(axis, bit) == 0
    return jnp.concatenate([jnp.where(first, cur, other), jnp.where(first, other, cur)], axis=dim)


def gather_start(cur, name):
    axis, bit, _ = steps_of(name)[0]
    return swap(cur, axis, bit)


def gather_finish(cur, other, name):
    first, *rest = steps_of(name)
    cur = join(cur, other, *first)
    for axis, bit, dim in rest:
        cur = join(cur, swap(cur, axis, bit), axis, bit, dim)
    return cur


def flat_rows(cur):
    return cur.reshape(-1, cur.shape[-1])


def split_rows(full):
    rows = full.shape[-2] // (lax.axis_size("shard") * lax.axis_size("ctx"))
    return full.reshape(full.shape[:-2] + (2,) * (shard_bits() + 1) + (rows, full.shape[-1]))


def scatter_start(cur, name, lead=0):
    axis, bit, dim = steps_of(name)[0]
    return swap(lax.dynamic_slice_in_dim(cur, 1 - my_bit(axis, bit), 1, dim + lead), axis, bit)


def scatter_finish(cur, other, name, lead=0):
    first, *rest = steps_of(name)
    kept = lax.dynamic_slice_in_dim(cur, my_bit(*first[:2]), 1, first[2] + lead)
    cur = (kept.astype(jnp.float32) + other.astype(jnp.float32)).astype(jnp.bfloat16)
    for axis, bit, dim in rest:
        mine = my_bit(axis, bit)
        other = swap(lax.dynamic_slice_in_dim(cur, 1 - mine, 1, dim + lead), axis, bit)
        kept = lax.dynamic_slice_in_dim(cur, mine, 1, dim + lead)
        cur = (kept.astype(jnp.float32) + other.astype(jnp.float32)).astype(jnp.bfloat16)
    return cur


def scatter_rest(cur, name, lead=0):
    for axis, bit, dim in steps_of(name)[1:]:
        mine = my_bit(axis, bit)
        other = swap(lax.dynamic_slice_in_dim(cur, 1 - mine, 1, dim + lead), axis, bit)
        kept = lax.dynamic_slice_in_dim(cur, mine, 1, dim + lead)
        cur = (kept.astype(jnp.float32) + other.astype(jnp.float32)).astype(jnp.bfloat16)
    return cur


def scatter_tp_start(first, second):
    z = lax.axis_index("tp")
    blocks = [lax.index_in_dim(s, j, s.ndim - 4, False) for j in range(2) for s in (first, second)]
    return [
        route(
            lax.select_n(z ^ d, *blocks),
            lambda s, c, t, d=d: (s - s % 2 + ((t ^ d) >> 1), c, 2 * (s % 2) + ((t ^ d) & 1)),
        )
        for d in range(4)
    ]


def sum_all(parts):
    total = parts[0].astype(jnp.float32)
    for part in parts[1:]:
        total = total + part.astype(jnp.float32)
    return total


def two_heads(pair):
    lane = lax.broadcasted_iota(jnp.int32, pair.shape, 1)
    zero = jnp.zeros_like(pair)
    return jnp.concatenate(
        [jnp.where(lane < DH, pair, zero), jnp.where(lane < DH, zero, pair)], axis=0
    )


def fold_heads(wide):
    rows = wide.shape[1] // 2
    both = jnp.concatenate([wide[:DH, :rows], wide[DH:, rows:]], axis=0)
    return both.T


def document(ends, start, stop, most):
    low, high = start * 0, start * 0 + most
    for d in range(SEG_COUNT):
        low = jnp.maximum(low, jnp.where(ends[d] <= start, ends[d], 0))
        high = jnp.minimum(high, jnp.where(ends[d] > stop, ends[d], most))
    return low, high


def key_blocks(ends, qb, span):
    length = span // 2
    here = ends[SEG_COUNT]
    far = length - here
    start = here + qb * BQ
    low, high = document(ends, start, start + BQ - 1, span)
    first = jnp.clip(low - here, 0, length) // BK
    count = (jnp.clip(high - here, 0, length) + (BK - 1)) // BK - first
    first_far = jnp.clip(low - far, 0, length) // BK
    count_far = (jnp.clip(high - far, 0, length) + (BK - 1)) // BK - first_far
    count_far = jnp.maximum(count_far, 0)

    def block(i):
        is_here = i < count
        kb = jnp.where(is_here, first + i, length // BK + first_far + (i - count))
        return kb, kb * BK + jnp.where(is_here, here, far - length)

    return count + count_far, block


def query_bounds(ends, qb, span):
    pos = ends[SEG_COUNT] + qb * BQ + lax.broadcasted_iota(jnp.int32, (1, BQ), 1)
    return document(ends, pos, pos, span)


def key_mask(bounds, base):
    key_pos = lax.broadcasted_iota(jnp.int32, (BK, BQ), 0) + base
    same = (key_pos >= bounds[0]) & (key_pos < bounds[1])
    return jnp.concatenate([same, same], axis=1)


def attn_fwd_kernel(first_block, ends, q_ref, k_ref, v_ref, o_ref, lse_ref, acc, top, den):
    span = k_ref.shape[0]
    qb = pl.program_id(0) + first_block
    pairs = q_ref.shape[1] // 128
    acc[...] = jnp.zeros_like(acc)
    top[...] = jnp.full_like(top, mask_fill)
    den[...] = jnp.zeros_like(den)
    queries = [two_heads(q_ref[:, 128 * p : 128 * p + 128]) for p in range(pairs)]
    bounds = query_bounds(ends, qb, span)
    count, block = key_blocks(ends, qb, span)

    @pl.loop(0, count)
    def _(i):
        kb, base = block(i)
        rows = pl.ds(pl.multiple_of(kb * BK, BK), BK)
        same = key_mask(bounds, base)
        for p in range(pairs):
            cols = slice(128 * p, 128 * p + 128)
            s = dot(k_ref[rows, cols], queries[p], NT)
            s = jnp.where(same, s, mask_fill)
            old = top[p]
            new = jnp.maximum(old, jnp.max(s, axis=0, keepdims=True))
            e = jnp.exp(s - new)
            shrink = jnp.exp(old - new)
            den[p] = den[p] * shrink + jnp.sum(e, axis=0, keepdims=True)
            top[p] = new
            acc[p] = acc[p] * shrink + dot(v_ref[rows, cols], e.astype(jnp.bfloat16), TN)

    for p in range(pairs):
        out = fold_heads(acc[p] / den[p])
        o_ref[:, 128 * p : 128 * p + 128] = out.astype(o_ref.dtype)
        lse_ref[p] = top[p] + jnp.log(den[p])


def row_sums(grads, outs):
    prod = (grads.astype(jnp.float32) * outs.astype(jnp.float32)).T
    return jnp.concatenate(
        [jnp.sum(prod[:DH], axis=0, keepdims=True), jnp.sum(prod[DH:], axis=0, keepdims=True)],
        axis=1,
    )


def attn_bwd_kernel(
    ends,
    q_ref,
    do_ref,
    o_low,
    o_high,
    lse_low,
    lse_high,
    k_ref,
    v_ref,
    dq_ref,
    dk_ref,
    dv_ref,
    dk_acc,
    dv_acc,
    dq_acc,
):
    span = k_ref.shape[0]
    qb = pl.program_id(0)
    is_low = qb < pl.num_programs(0) // 2
    pairs = q_ref.shape[1] // 128
    cols = [slice(128 * p, 128 * p + 128) for p in range(pairs)]

    @pl.when(qb == 0)
    def _():
        dk_acc[...] = jnp.zeros_like(dk_acc)
        dv_acc[...] = jnp.zeros_like(dv_acc)

    dq_acc[...] = jnp.zeros_like(dq_acc)
    outs = jnp.where(is_low, o_low[...], o_high[...])
    lses = jnp.where(is_low, lse_low[...], lse_high[...])
    queries = [two_heads(q_ref[:, c]) for c in cols]
    grads = [two_heads(do_ref[:, c]) for c in cols]
    deltas = [row_sums(do_ref[:, c], outs[:, c]) for c in cols]
    bounds = query_bounds(ends, qb, span)
    count, block = key_blocks(ends, qb, span)

    @pl.loop(0, count)
    def _(i):
        kb, base = block(i)
        rows = pl.ds(pl.multiple_of(kb * BK, BK), BK)
        same = key_mask(bounds, base)
        for p, c in enumerate(cols):
            keys = k_ref[rows, c]
            s = dot(keys, queries[p], NT)
            probs = jnp.exp(jnp.where(same, s, mask_fill) - lses[p])
            dp = dot(v_ref[rows, c], grads[p], NT)
            ds = (probs * (dp - deltas[p])).astype(jnp.bfloat16)
            dv_acc[rows, c] += dot(probs.astype(jnp.bfloat16), grads[p])
            dk_acc[rows, c] += dot(ds, queries[p])
            dq_acc[p] += dot(keys, ds, TN)

    for p, c in enumerate(cols):
        dq_ref[:, c] = (fold_heads(dq_acc[p]) * (DH**-0.5)).astype(dq_ref.dtype)

    @pl.when(qb == pl.num_programs(0) - 1)
    def _():
        dk_ref[...] = dk_acc[...].astype(dk_ref.dtype)
        dv_ref[...] = dv_acc[...].astype(dv_ref.dtype)


def in_hbm(*arrays):
    return [pltpu.with_memory_space_constraint(a, pltpu.HBM) for a in arrays]


def params(mib):
    return pltpu.CompilerParams(vmem_limit_bytes=mib * 2**20)


def cost(seconds):
    return pl.CostEstimate(flops=int(seconds * 1.15e15), bytes_accessed=2**20, transcendentals=0)


def attn_forward(ends, first_block, queries, keys, values):
    rows, width = queries.shape
    span = keys.shape[0]
    pairs = width // 128
    every = pl.BlockSpec((span, width), lambda i, e: (0, 0))
    return pl.pallas_call(
        functools.partial(attn_fwd_kernel, first_block),
        grid_spec=pltpu.PrefetchScalarGridSpec(
            num_scalar_prefetch=1,
            grid=(rows // BQ // 2,),
            in_specs=[
                pl.BlockSpec((BQ, width), lambda i, e: (i + first_block, 0)),
                every,
                every,
            ],
            out_specs=[
                pl.BlockSpec((BQ, width), lambda i, e: (i, 0)),
                pl.BlockSpec((pairs, 1, 2 * BQ), lambda i, e: (0, 0, i)),
            ],
            scratch_shapes=[
                pltpu.VMEM((pairs, 128, 2 * BQ), jnp.float32),
                pltpu.VMEM((pairs, 1, 2 * BQ), jnp.float32),
                pltpu.VMEM((pairs, 1, 2 * BQ), jnp.float32),
            ],
        ),
        out_shape=[
            jax.ShapeDtypeStruct((rows // 2, width), jnp.bfloat16),
            jax.ShapeDtypeStruct((pairs, 1, rows), jnp.float32),
        ],
        compiler_params=params(VMEM_MIB),
        cost_estimate=cost(10e-6),
        name="attn_fwd",
    )(ends, queries, keys, values)


def attn_backward(ends, start, pairs, queries, grads, mixed, lse, keys, values):
    rows = queries.shape[0]
    span = keys.shape[0]
    half = rows // BQ // 2
    width = 128 * pairs
    col = start // pairs
    tile = pl.BlockSpec((BQ, width), lambda i, e: (i, col))
    low = pl.BlockSpec((BQ, width), lambda i, e: (jnp.minimum(i, half - 1), col))
    high = pl.BlockSpec((BQ, width), lambda i, e: (jnp.maximum(i - half, 0), col))
    low_line = pl.BlockSpec((pairs, 1, 2 * BQ), lambda i, e: (col, 0, jnp.minimum(i, half - 1)))
    high_line = pl.BlockSpec((pairs, 1, 2 * BQ), lambda i, e: (col, 0, jnp.maximum(i - half, 0)))
    every = pl.BlockSpec((span, width), lambda i, e: (0, col))
    out = pl.BlockSpec((span, width), lambda i, e: (0, 0))
    shape = jax.ShapeDtypeStruct((span, width), jnp.bfloat16)
    return pl.pallas_call(
        attn_bwd_kernel,
        grid_spec=pltpu.PrefetchScalarGridSpec(
            num_scalar_prefetch=1,
            grid=(rows // BQ,),
            in_specs=[tile, tile, low, high, low_line, high_line, every, every],
            out_specs=[pl.BlockSpec((BQ, width), lambda i, e: (i, 0)), out, out],
            scratch_shapes=[
                pltpu.VMEM((span, width), jnp.float32),
                pltpu.VMEM((span, width), jnp.float32),
                pltpu.VMEM((pairs, 128, 2 * BQ), jnp.float32),
            ],
        ),
        out_shape=[jax.ShapeDtypeStruct((rows, width), jnp.bfloat16), shape, shape],
        compiler_params=params(VMEM_MIB),
        cost_estimate=cost(1e-6 * pairs),
        name="attn_bwd",
    )(ends, queries, grads, *mixed, *lse, keys, values)


def full_spec(shape):
    return pl.BlockSpec(shape, lambda i: (0,) * len(shape))


def rows_spec(rows, cols):
    return pl.BlockSpec((rows, cols), lambda i: (i, 0))


def pack_kernel(q_ref, k_ref, v_ref, out_ref):
    parts = [q_ref[...], k_ref[...], v_ref[...]]
    for i, part in enumerate(parts):
        out_ref[:, 128 * i : 128 * i + 128] = part[:, :128]
    thirds = [p[:, 128:] for p in parts]
    thirds.append(jnp.zeros_like(thirds[0]))
    out_ref[:, 384:512] = jnp.concatenate(thirds[:2], axis=1)
    out_ref[:, 512:640] = jnp.concatenate(thirds[2:], axis=1)


def pack_heads(*parts):
    return pl.pallas_call(
        pack_kernel,
        out_shape=jax.ShapeDtypeStruct((parts[0].shape[0], 640), parts[0].dtype),
        compiler_params=params(8),
        cost_estimate=cost(1e-6),
        name="pack_heads",
    )(*parts)


def build_heads(outs, a_ref, b_ref):
    for i, out in enumerate(outs):
        lo = 384 + DH * i
        out[:, :128] = a_ref[:, 128 * i : 128 * i + 128]
        out[:, 128:256] = b_ref[:, 128 * i : 128 * i + 128]
        out[:, 256:] = jnp.concatenate([a_ref[:, lo : lo + DH], b_ref[:, lo : lo + DH]], axis=1)


def qkv_kernel(x_ref, a_ref, b_ref, q_ref, k_ref, v_ref, wq, wk, wv):
    step = pl.program_id(0)

    @pl.when(step == 0)
    def _():
        build_heads((wq, wk, wv), a_ref, b_ref)

    x = x_ref[...]
    k_ref[...] = dot(x, wk[...]).astype(k_ref.dtype)
    v_ref[...] = dot(x, wv[...]).astype(v_ref.dtype)

    @pl.when(step < pl.num_programs(0) // 2)
    def _():
        q = dot(x, wq[...]).astype(jnp.bfloat16).astype(jnp.float32)
        q_ref[...] = (q * DH**-0.5).astype(q_ref.dtype)


def project(tok_all, w_a, w_b):
    span, width = tok_all.shape
    block = 512
    steps = span // block
    cols = 384
    low = jnp.bfloat16
    return pl.pallas_call(
        qkv_kernel,
        grid=(steps,),
        in_specs=[rows_spec(block, width), full_spec(w_a.shape), full_spec(w_b.shape)],
        out_specs=[
            pl.BlockSpec((block, cols), lambda i: (jnp.minimum(i, steps // 2 - 1), 0)),
            rows_spec(block, cols),
            rows_spec(block, cols),
        ],
        out_shape=[
            jax.ShapeDtypeStruct((span // 2, cols), low),
            jax.ShapeDtypeStruct((span, cols), low),
            jax.ShapeDtypeStruct((span, cols), low),
        ],
        scratch_shapes=[pltpu.VMEM((width, cols), low)] * 3,
        compiler_params=params(VMEM_MIB),
        cost_estimate=cost(6e-6),
        name="qkv",
    )(tok_all, w_a, w_b)


def attn_out_kernel(low_ref, high_ref, a_ref, b_ref, part_ref, ow_ref, proj_ref, norms_ref):
    step = pl.program_id(0)

    @pl.when(step == 0)
    def _():
        ow_ref[:, :128] = a_ref[:, :128]
        ow_ref[:, 128:256] = b_ref[:, :128]
        ow_ref[:, 256:] = jnp.concatenate([a_ref[:, 128:192], b_ref[:, 128:192]], axis=1)
        proj_ref[...] = a_ref[:, 192:320]
        turned = a_ref[:, 256:384].astype(jnp.float32).T
        norms_ref[...] = turned[64:72]

    mixed = jnp.where(step < pl.num_programs(0) // 2, low_ref[...], high_ref[...])
    part_ref[...] = dot(mixed, ow_ref[...], NT).astype(part_ref.dtype)


def attn_out(mixed, w_a, w_b):
    half, cols = mixed[0].shape
    width = w_a.shape[0]
    block = 256
    per = half // block
    low = jnp.bfloat16
    third = pl.BlockSpec((width, 384), lambda i: (0, w_a.shape[1] // 384 - 1))
    return pl.pallas_call(
        attn_out_kernel,
        grid=(2 * per,),
        in_specs=[
            pl.BlockSpec((block, cols), lambda i: (jnp.minimum(i, per - 1), 0)),
            pl.BlockSpec((block, cols), lambda i: (jnp.maximum(i - per, 0), 0)),
            third,
            third,
        ],
        out_specs=[
            rows_spec(block, width),
            full_spec((width, cols)),
            full_spec((width, 128)),
            full_spec((8, width)),
        ],
        out_shape=[
            jax.ShapeDtypeStruct((2 * half, width), low),
            jax.ShapeDtypeStruct((width, cols), low),
            jax.ShapeDtypeStruct((width, 128), low),
            jax.ShapeDtypeStruct((8, width), jnp.float32),
        ],
        compiler_params=params(VMEM_MIB),
        cost_estimate=cost(3e-6),
        name="attn_out",
    )(*mixed, w_a, w_b)


def normalize(hidden):
    row_mean = jnp.mean(hidden, axis=-1, keepdims=True)
    centred = hidden - row_mean
    variance = jnp.mean(centred * centred, axis=-1, keepdims=True)
    inv_std = lax.rsqrt(variance + eps_norm)
    return centred * inv_std, inv_std


def norm_backward(grad_out, normed, inv_std, gain):
    scaled = grad_out * gain
    return inv_std * (
        scaled
        - jnp.mean(scaled, axis=-1, keepdims=True)
        - normed * jnp.mean(scaled * normed, axis=-1, keepdims=True)
    )


def wide(ref):
    return ref[...].astype(jnp.float32)


def gelu_parts(v):
    e = jnp.exp(v * v * -0.5)
    t = 1.0 / (1.0 + (0.3275911 * 0.5**0.5) * jnp.abs(v))
    poly = 0.5 * 1.061405429
    for c in (-1.453152027, 1.421413741, -0.284496736, 0.254829592):
        poly = poly * t + 0.5 * c
    upper = poly * t * e
    cdf = jnp.where(v >= 0, 1.0 - upper, upper)
    return v * cdf, cdf + v * e * 0.3989422804014327


def ffn_kernel(
    x_ref, mine_ref, got_ref, norms, ia, ib, normed_ref, inv_ref, low_ref, act_ref, slope_ref
):
    step = pl.program_id(0)
    steps = pl.num_programs(0)
    parts = [slice(r, r + 256) for r in range(0, x_ref.shape[0], 256)]

    @pl.when(step == 0)
    def _():
        for rows in parts:
            hidden = x_ref[rows, :].astype(jnp.float32) + (
                mine_ref[rows, :].astype(jnp.float32) + got_ref[rows, :].astype(jnp.float32)
            )
            normed, inv = normalize(hidden)
            normed_ref[rows, :] = normed.astype(normed_ref.dtype)
            inv_ref[rows, :] = jnp.broadcast_to(inv, (256, 128))
            low_ref[rows, :] = (normed * norms[0:1, :] + norms[1:2, :]).astype(low_ref.dtype)

    def work(i_ref):
        for rows in parts:
            act, slope = gelu_parts(dot(low_ref[rows, :], i_ref[...]))
            act_ref[rows, :] = act.astype(act_ref.dtype)
            slope_ref[rows, :] = slope.astype(slope_ref.dtype)

    first = step < steps // 2
    pl.when(first)(lambda: work(ia))
    pl.when(jnp.logical_not(first))(lambda: work(ib))


def slice_specs(width, cols, per):
    return [
        pl.BlockSpec((width, cols), lambda i: (0, jnp.minimum(i, per - 1))),
        pl.BlockSpec((width, cols), lambda i: (0, jnp.maximum(i - per, 0))),
    ]


FFN_COLS = 256
GROUPS = 1


def feed_forward(tok, mine, got, norms, inner, hidden):
    rows, width = tok.shape
    cols = FFN_COLS
    per = hidden // cols
    tile = full_spec((rows, width))
    chunk = pl.BlockSpec((rows, cols), lambda i: (0, i))
    low = jax.ShapeDtypeStruct((rows, width), jnp.bfloat16)
    units = jax.ShapeDtypeStruct((rows, 2 * hidden), jnp.bfloat16)
    return pl.pallas_call(
        ffn_kernel,
        grid=(2 * per,),
        in_specs=[tile, tile, tile, full_spec(norms.shape)]
        + slice_specs(width, cols, per),
        out_specs=[tile, full_spec((rows, 128)), tile, chunk, chunk],
        out_shape=[low, jax.ShapeDtypeStruct((rows, 128), jnp.float32), low, units, units],
        compiler_params=params(VMEM_MIB),
        cost_estimate=cost(14e-6),
        name="feed_forward",
    )(tok, mine, got, norms, *inner)


def ffn_out_kernel(act_ref, a_ref, b_ref, out_ref):
    hidden = a_ref.shape[1]
    part = dot(act_ref[:, :hidden], a_ref[...], NT) + dot(act_ref[:, hidden:], b_ref[...], NT)
    out_ref[...] = part.astype(out_ref.dtype)


def ffn_out(act, w_a, w_b):
    rows = act.shape[0]
    width = w_a.shape[0]
    block = 256
    return pl.pallas_call(
        ffn_out_kernel,
        grid=(rows // block,),
        in_specs=[rows_spec(block, act.shape[1]), full_spec(w_a.shape), full_spec(w_b.shape)],
        out_specs=rows_spec(block, width),
        out_shape=jax.ShapeDtypeStruct((rows, width), jnp.bfloat16),
        compiler_params=params(VMEM_MIB),
        cost_estimate=cost(3e-6),
        name="ffn_out",
    )(act, w_a, w_b)


def middle_kernel(
    normed_ref, mine_ref, got_ref, norms, proj_ref, cot_ref, emb_ref, gh2_ref, low_ref, pg_ref, vec_ref
):
    step = pl.program_id(0)
    first = wide(normed_ref) * norms[0:1, :] + norms[1:2, :]
    normed, inv = normalize(first + (wide(mine_ref) + wide(got_ref)))
    second = (normed * norms[2:3, :] + norms[3:4, :]).astype(jnp.bfloat16)
    projected = dot(second, proj_ref[...])
    inv_norm = lax.rsqrt(jnp.sum(projected * projected, axis=-1, keepdims=True) + eps_unit)
    embedding = projected * inv_norm
    emb_ref[...] = embedding
    cot = wide(cot_ref)
    radial = jnp.sum(cot * embedding, axis=-1, keepdims=True)
    grad_projected = (inv_norm * (cot - embedding * radial)).astype(jnp.bfloat16)
    grad_second = dot(grad_projected, proj_ref[...], NT)
    grad = norm_backward(grad_second, normed, inv, norms[2:3, :])
    gh2_ref[...] = grad
    low_ref[...] = grad.astype(low_ref.dtype)

    @pl.when(step == 0)
    def _():
        pg_ref[...] = jnp.zeros_like(pg_ref)
        vec_ref[...] = jnp.zeros_like(vec_ref)

    pg_ref[...] += dot(second, grad_projected, TN)
    vec_ref[0:1, :] += jnp.sum(grad_second * normed, axis=0, keepdims=True)
    vec_ref[1:2, :] += jnp.sum(grad_second, axis=0, keepdims=True)


def middle(normed, mine, got, norms, proj, cot):
    rows, width = normed.shape
    p_width = proj.shape[1]
    block = 256
    tile = rows_spec(block, width)
    return pl.pallas_call(
        middle_kernel,
        grid=(rows // block,),
        in_specs=[
            tile,
            tile,
            tile,
            full_spec(norms.shape),
            full_spec(proj.shape),
            rows_spec(block, p_width),
        ],
        out_specs=[
            rows_spec(block, p_width),
            tile,
            tile,
            full_spec((width, p_width)),
            full_spec((8, width)),
        ],
        out_shape=[
            jax.ShapeDtypeStruct((rows, p_width), jnp.float32),
            jax.ShapeDtypeStruct((rows, width), jnp.float32),
            jax.ShapeDtypeStruct((rows, width), jnp.bfloat16),
            jax.ShapeDtypeStruct((width, p_width), jnp.float32),
            jax.ShapeDtypeStruct((8, width), jnp.float32),
        ],
        compiler_params=params(VMEM_MIB),
        cost_estimate=cost(5e-6),
        name="middle",
    )(normed, mine, got, norms, proj, cot)


def ffn_back_kernel(
    turns, bits, g_ref, x_ref, act_ref, slope_ref, ia, ib, oa, ob, keep_a, send_a, keep_b, send_b, out_ref, acc, g_t, x_t, wgrad
):
    step = pl.program_id(0)
    steps = pl.num_programs(0)

    @pl.when(step == 0)
    def _():
        g_t[...] = g_ref[...].T
        x_t[...] = x_ref[...].T
        acc[...] = jnp.zeros_like(acc)

    def put(which, run, keep, send, bit):
        for j in range(keep.shape[1] // run):
            for out, side in ((keep, bit), (send, 1 - bit)):
                rows = pl.ds(pl.multiple_of((2 * j + side) * run, run), run)
                out[which, j * run : (j + 1) * run, :] = wgrad[rows, :].astype(out.dtype)

    def work(i_ref, o_ref, run, keep, send, bit):
        wgrad[...] = dot(g_t[...], act_ref[...])
        put(0, run, keep, send, bit)
        grad = dot(g_ref[...], o_ref[...]) * slope_ref[...].astype(jnp.float32)
        grad = grad.astype(jnp.bfloat16)
        wgrad[...] = dot(x_t[...], grad)
        put(1, run, keep, send, bit)
        acc[...] += dot(grad, i_ref[...], NT)

    first = step < steps // 2
    pl.when(first)(lambda: work(ia, oa, turns[0], keep_a, send_a, bits[0]))
    pl.when(jnp.logical_not(first))(lambda: work(ib, ob, turns[1], keep_b, send_b, bits[1]))

    @pl.when(step == steps - 1)
    def _():
        out_ref[...] = acc[...].astype(out_ref.dtype)


def ffn_back(bits, turns, grad, x, act, slope, inner, outer, hidden):
    rows, width = grad.shape
    cols = FFN_COLS
    per = hidden // cols

    def left(i):
        return jnp.minimum(i, per - 1)

    def right(i):
        return jnp.maximum(i - per, 0)

    tile = pl.BlockSpec((rows, width), lambda i, e: (0, 0))
    chunk = pl.BlockSpec((rows, cols), lambda i, e: (0, i))
    mats = [
        pl.BlockSpec((width, cols), lambda i, e: (0, left(i))),
        pl.BlockSpec((width, cols), lambda i, e: (0, right(i))),
    ]
    outs = [
        pl.BlockSpec((2, width // 2, cols), lambda i, e: (0, 0, left(i))),
        pl.BlockSpec((2, width // 2, cols), lambda i, e: (0, 0, right(i))),
    ]
    low = jnp.bfloat16
    shape = jax.ShapeDtypeStruct((2, width // 2, hidden), low)
    return pl.pallas_call(
        functools.partial(ffn_back_kernel, turns),
        grid_spec=pltpu.PrefetchScalarGridSpec(
            num_scalar_prefetch=1,
            grid=(2 * per,),
            in_specs=[tile, tile, chunk, chunk] + mats * 2,
            out_specs=[outs[0], outs[0], outs[1], outs[1], tile],
            scratch_shapes=[
                pltpu.VMEM((rows, width), jnp.float32),
                pltpu.VMEM((width, rows), low),
                pltpu.VMEM((width, rows), low),
                pltpu.VMEM((width, cols), jnp.float32),
            ],
        ),
        out_shape=[pltpu.HBM(shape.shape, low)] * 4 + [jax.ShapeDtypeStruct((rows, width), low)],
        compiler_params=params(VMEM_MIB),
        cost_estimate=cost(17e-6),
        name="ffn_back",
    )(bits, grad, *in_hbm(x, act, slope, *inner, *outer))


def first_back_kernel(
    mine_ref,
    got_ref,
    gh2_ref,
    normed_ref,
    inv_ref,
    norms,
    ow_ref,
    low_ref,
    high_ref,
    pg_ref,
    vec2_ref,
    gh1_ref,
    gmix_ref,
    og_ref,
    small_ref,
    og_acc,
    vec,
):
    step = pl.program_id(0)
    steps = pl.num_programs(0)

    @pl.when(step == 0)
    def _():
        og_acc[...] = jnp.zeros_like(og_acc)
        vec[...] = jnp.zeros_like(vec)
        vec[2:4, :] = vec2_ref[0:2, :]

    grad = gh2_ref[...] + (wide(mine_ref) + wide(got_ref))
    normed = wide(normed_ref)
    vec[0:1, :] += jnp.sum(grad * normed, axis=0, keepdims=True)
    vec[1:2, :] += jnp.sum(grad, axis=0, keepdims=True)
    grad_h1 = norm_backward(grad, normed, inv_ref[:, 0:1], norms[0:1, :])
    gh1_ref[...] = grad_h1
    low = grad_h1.astype(jnp.bfloat16)
    gmix_ref[...] = dot(low, ow_ref[...]).astype(gmix_ref.dtype)
    mixed = jnp.where(step < steps // 2, low_ref[...], high_ref[...])
    og_acc[...] += dot(low, mixed, TN)

    @pl.when(step == steps - 1)
    def _():
        og_ref[...] = og_acc[...].astype(og_ref.dtype)
        p_width = pg_ref.shape[1]
        small_ref[:, :p_width] = pg_ref[...].astype(small_ref.dtype)
        small_ref[:, p_width:] = vec[...].T.astype(small_ref.dtype)


def first_back(mine, got, grad_h2, normed, inv, norms, output_w, mixed, proj_part, vec2):
    rows, width = grad_h2.shape
    cols = output_w.shape[1]
    block = 256
    per = rows // block // 2
    tile = rows_spec(block, width)
    low = jnp.bfloat16
    p_width = proj_part.shape[1]
    return pl.pallas_call(
        first_back_kernel,
        grid=(2 * per,),
        in_specs=[
            tile,
            tile,
            tile,
            tile,
            rows_spec(block, 128),
            full_spec(norms.shape),
            full_spec(output_w.shape),
            pl.BlockSpec((block, cols), lambda i: (jnp.minimum(i, per - 1), 0)),
            pl.BlockSpec((block, cols), lambda i: (jnp.maximum(i - per, 0), 0)),
            full_spec(proj_part.shape),
            full_spec(vec2.shape),
        ],
        out_specs=[
            tile,
            rows_spec(block, cols),
            full_spec((width, cols)),
            full_spec((width, p_width + 128)),
        ],
        out_shape=[
            pltpu.HBM((rows, width), jnp.float32),
            jax.ShapeDtypeStruct((rows, cols), low),
            jax.ShapeDtypeStruct((width, cols), low),
            jax.ShapeDtypeStruct((width, p_width + 128), low),
        ],
        scratch_shapes=[pltpu.VMEM((width, cols), jnp.float32), pltpu.VMEM((128, width), jnp.float32)],
        compiler_params=params(VMEM_MIB),
        cost_estimate=cost(1e-6),
        name="first_back",
    )(mine, got, *in_hbm(grad_h2, normed, inv), norms, *in_hbm(output_w, *mixed, proj_part), vec2)


def token_grads_kernel(core, *refs):
    *parts, a_ref, b_ref, theirs, mine, wq, wk, wv = refs
    step = pl.program_id(0)
    weights = (wq, wk, wv)[-(len(parts) // GROUPS) :]

    @pl.when(step == 0)
    def _():
        build_heads((wq, wk, wv), a_ref, b_ref)

    total = 0.0
    for i, w in enumerate(weights):
        grads = [parts[p * len(weights) + i][...] for p in range(GROUPS)]
        total = total + dot(jnp.concatenate(grads, axis=1), w[...], NT)

    @pl.when(step == 0)
    def _():
        theirs[...] = total.astype(theirs.dtype)

    @pl.when(step == 1)
    def _():
        mine[...] = total.astype(mine.dtype)


def token_grads(core, far, grads, w_a, w_b):
    half = grads[0][0].shape[0] // 2
    width = w_a.shape[0]
    skip = 2 if far else 0
    used = [arrays[1:] if far else arrays for arrays in grads]
    rows = lambda i, core: (skip + jnp.where(i < 1, 1 - core[0], core[0]), 0)
    specs = [pl.BlockSpec((half, x.shape[1]), rows) for arrays in used for x in arrays]
    mat = pl.BlockSpec(w_a.shape, lambda i, core: (0, 0))
    shape = jax.ShapeDtypeStruct((half, width), jnp.bfloat16)
    whole = pl.BlockSpec((half, width), lambda i, core: (0, 0))
    return pl.pallas_call(
        token_grads_kernel,
        grid_spec=pltpu.PrefetchScalarGridSpec(
            num_scalar_prefetch=1,
            grid=(2,),
            in_specs=specs + [mat, mat],
            out_specs=[whole, whole],
            scratch_shapes=[pltpu.VMEM((width, 384), jnp.bfloat16)] * 3,
        ),
        out_shape=[shape, shape],
        compiler_params=params(VMEM_MIB),
        cost_estimate=cost(0.5e-6),
        name="token_grads",
    )(core.reshape(1), *[x for arrays in used for x in arrays], w_a, w_b)


def head_grads_kernel(x_ref, *refs):
    *parts, og_ref, twos, thirds, acc = refs
    step = pl.program_id(0)
    steps = pl.num_programs(0)

    @pl.when(step == 0)
    def _():
        acc[...] = jnp.zeros_like(acc)

    x_t = x_ref[...].T

    def add(i):
        grads = [parts[3 * p + i][...] for p in range(GROUPS)]
        acc[i] += dot(x_t, jnp.concatenate(grads, axis=1))

    add(1)
    add(2)
    pl.when(step < steps // 2)(lambda: add(0))

    @pl.when(step == steps - 1)
    def _():
        for s in range(2):
            for i in range(4):
                part = og_ref if i == 3 else acc.at[i]
                lo = 128 * s
                twos[s, :, 128 * i : 128 * i + 128] = part[:, lo : lo + 128].astype(twos.dtype)
            for i in (0, 2):
                lo = 256 + DH * s
                both = [
                    (og_ref if j == 3 else acc.at[j])[:, lo : lo + DH].astype(thirds.dtype)
                    for j in (i, i + 1)
                ]
                thirds[s, :, DH * i : DH * i + 128] = jnp.concatenate(both, axis=1)


def head_grads(tok_all, grads, output_part):
    span, width = tok_all.shape
    block = 512
    steps = span // block
    near = lambda i: (jnp.minimum(i, steps // 2 - 1), 0)
    specs = []
    for dq, _, _ in grads:
        cols = dq.shape[1]
        specs += [pl.BlockSpec((block, cols), near), rows_spec(block, cols), rows_spec(block, cols)]
    return pl.pallas_call(
        head_grads_kernel,
        grid=(steps,),
        in_specs=[rows_spec(block, width)] + specs + [full_spec(output_part.shape)],
        out_specs=[full_spec((2, width, 512)), full_spec((2, width, 256))],
        out_shape=[
            jax.ShapeDtypeStruct((2, width, 512), jnp.bfloat16),
            jax.ShapeDtypeStruct((2, width, 256), jnp.bfloat16),
        ],
        scratch_shapes=[pltpu.VMEM((3, width, 384), jnp.float32)],
        compiler_params=params(VMEM_MIB),
        cost_estimate=cost(0.5e-6),
        name="head_grads",
    )(*in_hbm(tok_all), *[x for arrays in grads for x in arrays], output_part)


def finish_kernel(p0, p1, p2, p3, small, q_ref, k_ref, v_ref, o_ref, proj_ref, vec_ref):
    total = (wide(p0) + wide(p1)) + (wide(p2) + wide(p3))
    rows = total.shape[0]

    def part(i):
        third = total[:, 512 + DH * i : 512 + DH * i + DH]
        return jnp.concatenate([total[:, 128 * i : 128 * i + 128], third], axis=1)

    def turned(block):
        pad = jnp.zeros((128 - rows, block.shape[1]), block.dtype)
        return jnp.concatenate([block, pad], axis=0).T[:, :rows]

    for i, out in enumerate((q_ref, k_ref, v_ref)):
        out[...] = part(i)
    o_ref[:128, :] = turned(total[:, 384:512])
    o_ref[128:, :] = turned(total[:, 640:768])[DH:, :]
    sums = wide(small)
    proj_ref[...] = sums[:, :128]
    vec_ref[...] = turned(sums[:, 128:])[:8, :]


def finish(parts, small):
    rows = parts[0].shape[0]
    shapes = [(rows, 192)] * 3 + [(192, rows), (rows, 128), (8, rows)]
    return pl.pallas_call(
        finish_kernel,
        out_shape=[jax.ShapeDtypeStruct(s, jnp.float32) for s in shapes],
        compiler_params=params(16),
        cost_estimate=cost(2e-6),
        name="finish",
    )(*parts, small)


def per_device(
    tokens,
    segments,
    query_weight,
    key_weight,
    value_weight,
    output_weight,
    attn_gain,
    attn_shift,
    inner_weight,
    outer_weight,
    ffn_gain,
    ffn_shift,
    proj_weight,
    grad_embed,
):
    length, model_width = tokens.shape[2:]
    half = length // 2
    core = lax.axis_index("shard") % 2
    ctx = lax.axis_index("ctx")
    group = lax.axis_index("tp")
    micro, seat = group // 2, group % 2
    owner = core == seat
    edge = min(SEG_MOST, length)
    bf16, f32 = jnp.bfloat16, jnp.float32

    def by_core(mine, theirs, axis):
        return jnp.concatenate(
            [jnp.where(core == 0, mine, theirs), jnp.where(core == 0, theirs, mine)], axis=axis
        )

    tok_m = lax.dynamic_index_in_dim(tokens, micro, 0, False)[0]
    sent = lax.dynamic_slice_in_dim(tok_m, (1 - ctx) * (length - edge), edge, 0)
    got = route(sent, lambda s, c, t: (s, 1 - c, t) if s % 2 == t % 2 else None)
    heads_own = pack_heads(query_weight, key_weight, value_weight)
    heads_parts = gather_tp_start(heads_own)
    tokens_in, segments_in, outer_in, output_in, cot_in = after_all(
        heads_own, tokens, segments, outer_weight, output_weight, grad_embed
    )
    vectors = jnp.stack([attn_gain, attn_shift, ffn_gain, ffn_shift])
    vectors = dot(vectors, jnp.eye(4, 64, dtype=bf16), TN).astype(bf16)
    ffn_own = jnp.concatenate([inner_weight, output_in.T, proj_weight, vectors, outer_in.T], axis=1)
    ffn_all = lax.all_gather(ffn_own, "tp", axis=0)
    tok_m = lax.dynamic_index_in_dim(tokens_in, micro, 0, False)[0]

    *heads_parts, got, ffn_own, tok_m, segments_in, cot_in = tie(
        *heads_parts, got, ffn_own, tok_m, segments_in, cot_in
    )
    heads_a, heads_b = gather_tp_finish(heads_parts)
    other_a, other_b = gather_start(heads_a, "y"), gather_start(heads_b, "x")
    tok_got = swap(tok_m, "shard", 1)
    seg_m = lax.dynamic_index_in_dim(segments_in, micro, 0, False)
    seg_m = seg_m.reshape(1, -1, 128)
    upto = jnp.arange(8, dtype=jnp.int32).reshape(8, 1, 1)
    counts_own = jnp.sum((seg_m <= upto).astype(jnp.int32), axis=(1, 2))
    counts_got = swap(counts_own, "shard", 1)
    cot_m = lax.dynamic_index_in_dim(cot_in, micro, 0, False)[0]
    other_a, other_b, tok_got, counts_got, cot_m = tie(other_a, other_b, tok_got, counts_got, cot_m)
    heads_a, heads_b = gather_finish(heads_a, other_a, "y"), gather_finish(heads_b, other_b, "x")
    other_a, other_b = gather_start(heads_a, "x"), gather_start(heads_b, "y")
    got_core = swap(got, "shard", 1)
    cot_got = swap(cot_m, "shard", 1)
    counts = jnp.where(owner, counts_own, counts_got)
    counts = counts + swap(counts, "ctx", 1)
    place_of = jnp.arange(8)
    ends = jnp.where(place_of == SEG_COUNT, ctx * length, counts).astype(jnp.int32)
    tok_here = jnp.where(owner, tok_m, tok_got)
    tok_far = lax.dynamic_update_slice_in_dim(
        jnp.zeros_like(tok_here), jnp.where(owner, got, got_core), ctx * (length - edge), 0
    )
    tok_all = jnp.concatenate([tok_here, tok_far], axis=0)
    cot = jnp.where(owner, cot_m, cot_got)
    other_a, other_b, tok_all, cot, ends = tie(other_a, other_b, tok_all, cot, ends)
    heads_a, heads_b = gather_finish(heads_a, other_a, "x"), gather_finish(heads_b, other_b, "y")
    heads_a, heads_b = flat_rows(heads_a), flat_rows(heads_b)

    core_dim = shard_bits() - 1
    queries, keys, values = project(tok_all, heads_a, heads_b)
    ffn_all = after(ffn_all, keys)
    kept = lax.dynamic_slice_in_dim(ffn_all, 2 * core, 2, 0)
    other = swap(lax.dynamic_slice_in_dim(ffn_all, 2 - 2 * core, 2, 0), "shard", 1)
    shape = (1,) * core_dim + (1, 1) + ffn_own.shape
    split = inner_weight.shape[1] + 384
    inner, outer = [], []
    for s in range(2):
        both = join(kept[s].reshape(shape), other[s].reshape(shape), "shard", 1, core_dim)
        inner.append(both[..., :split])
        outer.append(both[..., split:])
    inner_got = [gather_start(inner[0], "x"), gather_start(inner[1], "y")]
    outer_got = [gather_start(outer[0], "x"), gather_start(outer[1], "y")]
    mixed_low, lse_low = attn_forward(after(ends, *inner, *outer), 0, queries, keys, values)
    mixed_low, *inner_got = tie(mixed_low, *inner_got)
    inner = [gather_finish(inner[0], inner_got[0], "x"), gather_finish(inner[1], inner_got[1], "y")]
    inner_got = [gather_start(inner[0], "y"), gather_start(inner[1], "x")]
    mixed_high, lse_high = attn_forward(
        after(ends, mixed_low, *inner), half // BQ, queries, keys, values
    )
    mixed_high, *got_all = tie(mixed_high, *inner_got, *outer_got)
    outer = [gather_finish(outer[0], got_all[2], "x"), gather_finish(outer[1], got_all[3], "y")]
    outer_got = [gather_start(outer[0], "y"), gather_start(outer[1], "x")]
    inner = [
        flat_rows(gather_finish(inner[0], got_all[0], "y")),
        flat_rows(gather_finish(inner[1], got_all[1], "x")),
    ]
    mixed = (mixed_low, mixed_high)
    part, output_w, proj, norms = attn_out(mixed, *inner)

    hidden_cols = outer_weight.shape[0]
    normed, inv, first_low, act, slope = feed_forward(
        tok_here, part, swap(part, "shard", 1), norms, inner, hidden_cols
    )
    act, *outer_got = tie(act, *outer_got)
    outer = [
        flat_rows(gather_finish(outer[0], outer_got[0], "y")),
        flat_rows(gather_finish(outer[1], outer_got[1], "x")),
    ]
    part = ffn_out(act, *outer)
    embedding, grad_h2, grad_ffn, proj_part, vec2 = middle(
        normed, part, swap(part, "shard", 1), norms, proj, cot
    )

    rows = model_width // (lax.axis_size("shard") * lax.axis_size("ctx"))
    y_axis, y_bit, _ = steps_of("y")[0]
    y_mine = my_bit(y_axis, y_bit)
    x_first = rows % 16 == 0
    bits = jnp.stack([ctx if x_first else y_mine, y_mine]).astype(jnp.int32)
    turns = (rows if x_first else model_width // 2, model_width // 2)
    keep_a, send_a, keep_b, send_b, part = ffn_back(
        bits, turns, grad_ffn, first_low, act, slope, inner, outer, hidden_cols
    )
    wgrad_got = [
        swap(send_a, "ctx", 1) if x_first else swap(send_a, y_axis, y_bit),
        swap(send_b, y_axis, y_bit),
    ]
    part_got = swap(part, "shard", 1)
    grad_h1, grad_mixed, output_part, small = first_back(
        part, part_got, grad_h2, normed, inv, norms, output_w, mixed, proj_part, vec2
    )

    small = split_rows(small)
    small_got = scatter_start(small, "y")
    quarter = half // 2
    emb_half = lax.dynamic_slice_in_dim(after(embedding, grad_mixed), core * half, half, 0)
    emb_got = [
        route(
            lax.select_n(micro ^ d, emb_half[:quarter], emb_half[quarter:]),
            lambda s, c, t, d=d: (s - s % 2 + t % 2, c, 2 * (s % 2) + ((t // 2) ^ d)),
        )
        for d in range(2)
    ]
    flow = (queries, grad_mixed, mixed, (lse_low, lse_high), keys, values)
    grads = attn_backward(after(ends, small, emb_half), 0, 3, *flow)
    *grads, wgrad_got[0], wgrad_got[1], small_got, emb_got[0], emb_got[1] = tie(
        *grads, *wgrad_got, small_got, *emb_got
    )
    grads = [grads]

    def added(kept, got):
        return (kept.astype(f32) + got.astype(f32)).astype(bf16)

    lead = (2,) * (shard_bits() - 1)
    last = (rows, hidden_cols)
    shapes = [(2, *lead, 2, 1, *last), (2, 1, *lead[1:], 2, 2, *last)]
    second_steps = ("y" if x_first else "x", "x")
    wgrad = [
        added(keep_a, wgrad_got[0]).reshape(shapes[0 if x_first else 1]),
        added(keep_b, wgrad_got[1]).reshape(shapes[1]),
    ]
    wgrad = [scatter_rest(w, "y", 1) if n == "x" else w for w, n in zip(wgrad, second_steps)]
    small = scatter_finish(small, small_got, "y")
    *wgrad, small, dq, dk, dv = tie(*wgrad, small, *grads[0])
    grads = [[dq, dk, dv]]
    wgrad_got = [scatter_start(w, n, 1) for w, n in zip(wgrad, second_steps)]
    small_got = scatter_start(small, "x")

    far_theirs, far_mine = token_grads(core, True, grads, heads_a, heads_b)
    near_theirs, near_mine = token_grads(core, False, grads, heads_a, heads_b)
    far_theirs, near_theirs, tok_in = tie(far_theirs, near_theirs, tok_all)
    far_got = swap(far_theirs, "shard", 1)
    near_got = swap(near_theirs, "shard", 1)
    twos, thirds = head_grads(tok_in, grads, output_part)
    twos, thirds, far_got, near_got, small_got, *wgrad_got = tie(
        twos, thirds, far_got, near_got, small_got, *wgrad_got
    )
    far_sum = added(far_mine, far_got)
    from_far = swap(far_sum, "ctx", 1)
    wgrad = [scatter_finish(w, g, n, 1) for w, g, n in zip(wgrad, wgrad_got, second_steps)]
    blocks = jnp.stack([w.reshape(2, 2, rows, hidden_cols) for w in wgrad], axis=0)
    wgrad_theirs = swap(lax.dynamic_index_in_dim(blocks, 1 - core, 2, False), "shard", 1)
    twos, thirds = split_rows(twos), split_rows(thirds)
    twos_got, thirds_got = scatter_start(twos, "y", 1), scatter_start(thirds, "x", 1)
    mine = lax.dynamic_slice_in_dim(grad_h1, core * half, half, 0)
    near_sum = near_mine.astype(f32) + near_got.astype(f32) + mine
    small = scatter_finish(small, small_got, "x")
    near_sum, wgrad_theirs, small = tie(near_sum, wgrad_theirs, small)
    ours = lax.dynamic_index_in_dim(blocks, core, 2, False)
    blocks = by_core(ours, wgrad_theirs, 0).reshape(4, 2 * rows, hidden_cols)
    small = lax.dynamic_index_in_dim(small.reshape(2, rows, -1), core, 0, False)
    extra = small.reshape(1, -1, hidden_cols)
    blocks = jnp.concatenate([blocks, jnp.concatenate([extra] * 4, axis=0)], axis=1)
    wgrad_sum = lax.psum_scatter(blocks, "tp", scatter_dimension=0)
    near_sum, from_far, twos_got, thirds_got = tie(near_sum, from_far, twos_got, thirds_got)
    grad_tok = (near_sum + from_far.astype(f32)).astype(bf16)

    own_cols = model_width // lax.axis_size("tp")
    cols = [grad_tok[:, own_cols * j : own_cols * (j + 1)] for j in range(4)]
    even, odd = jnp.stack(cols[0::2]), jnp.stack(cols[1::2])
    kept = jnp.where(core == 0, even, odd)
    other = swap(jnp.where(core == 0, odd, even), "shard", 1)
    twos = scatter_finish(twos, twos_got, "y", 1)
    thirds = scatter_finish(thirds, thirds_got, "x", 1)
    twos_got, thirds_got = scatter_start(twos, "x", 1), scatter_start(thirds, "y", 1)
    both = [jnp.where(core == 0, kept, other), jnp.where(core == 0, other, kept)]
    both = [jnp.concatenate([both[0][j], both[1][j]], axis=0) for j in range(2)]
    arrived = [
        route(
            lax.select_n(micro ^ d, *both),
            lambda s, c, t, d=d: (s - s % 2 + t % 2, c, 2 * ((t // 2) ^ d) + s % 2),
        )
        for d in range(2)
    ]
    twos = scatter_finish(twos, twos_got, "x", 1)
    thirds = scatter_finish(thirds, thirds_got, "y", 1)
    pieces = jnp.concatenate([twos, thirds], axis=-1).reshape(2, 2, rows, -1)
    theirs = swap(lax.dynamic_index_in_dim(pieces, 1 - core, 1, False), "shard", 1)
    ours = lax.dynamic_index_in_dim(pieces, core, 1, False)
    pieces = by_core(ours, theirs, 0)
    wgrad_sum, pieces = tie(wgrad_sum, pieces)
    parts = [lax.dynamic_index_in_dim(pieces, group ^ d, 0, False) for d in range(4)]
    parts = parts[:1] + [swap(parts[d], "tp", d) for d in range(1, 4)]
    *parts, arrived[0], arrived[1] = tie(*parts, *arrived)
    outer_grad = wgrad_sum[:rows].astype(f32).T
    inner_grad = wgrad_sum[rows : 2 * rows].astype(f32)
    small = wgrad_sum[2 * rows :].reshape(rows, -1)
    embeddings = jnp.stack([lax.select_n((group % 2) ^ m, *emb_got) for m in range(2)])
    embeddings = embeddings.reshape(2, 1, quarter, -1)
    grad_tokens = jnp.stack([lax.select_n(m ^ micro, *arrived) for m in range(2)])
    grad_tokens = grad_tokens.reshape(2, 1, length, own_cols).astype(f32)
    query_grad, key_grad, value_grad, output_grad, proj_grad, norm_grads = finish(parts, small)
    return (
        embeddings,
        grad_tokens,
        query_grad,
        key_grad,
        value_grad,
        output_grad,
        norm_grads[0],
        norm_grads[1],
        inner_grad,
        outer_grad,
        norm_grads[2],
        norm_grads[3],
        proj_grad,
    )


def solution(mesh):
    rows = ("shard", "ctx")
    placed = (
        P(None, "shard", "ctx", None),
        P(None, "shard", "ctx"),
        P(rows, "tp"),
        P(rows, "tp"),
        P(rows, "tp"),
        P("tp", rows),
        P(rows),
        P(rows),
        P(rows, "tp"),
        P("tp", rows),
        P(rows),
        P(rows),
        P(rows, None),
        P(None, "shard", "ctx", None),
    )
    return jax.shard_map(
        per_device,
        mesh=mesh,
        in_specs=placed,
        out_specs=(
            P(None, "shard", ("ctx", "tp"), None),
            P(None, "shard", "ctx", "tp"),
            P(rows, "tp"),
            P(rows, "tp"),
            P(rows, "tp"),
            P("tp", rows),
            P(rows),
            P(rows),
            P(rows, "tp"),
            P("tp", rows),
            P(rows),
            P(rows),
            P(rows, None),
        ),
        check_vma=False,
    )
```

```python
import functools

import jax
import jax.numpy as jnp
from jax import lax
from jax.experimental import pallas as pl
from jax.experimental.pallas import tpu as pltpu
from jax.sharding import PartitionSpec as P

DH = 64
SEG_COUNT = 6
SEG_MOST = 800
BQ = 256
BK_FWD = 512
BK_BWD = 256
VMEM_MIB = 34

eps_norm = 1e-12
eps_unit = 1e-06
mask_fill = -1e30

NN = (((1,), (0,)), ((), ()))
NT = (((1,), (1,)), ((), ()))
TN = (((0,), (0,)), ((), ()))


def dot(first_op, second_op, dims=NN):
    return lax.dot_general(first_op, second_op, dims, preferred_element_type=jnp.float32)


def tie(*values):
    return lax.optimization_barrier(values)


def after(value, *others):
    return lax.optimization_barrier((value, *others))[0]


def after_all(done, *values):
    return lax.optimization_barrier((done, *values))[1:]


def swap(v, axis, bit):
    count = lax.axis_size(axis)
    return lax.ppermute(v, axis, [(i, i ^ bit) for i in range(count)])


def route(v, target):
    shards, halves, groups = (lax.axis_size(a) for a in ("shard", "ctx", "tp"))

    def flat(s, c, t):
        return (s * halves + c) * groups + t

    pairs = []
    for s in range(shards):
        for c in range(halves):
            for t in range(groups):
                to = target(s, c, t)
                if to is not None:
                    pairs.append((flat(s, c, t), flat(*to)))
    return lax.ppermute(v, ("shard", "ctx", "tp"), pairs)


def shard_bits():
    return lax.axis_size("shard").bit_length() - 1


def steps_of(name):
    bits = shard_bits()
    if name == "x":
        return [("ctx", 1, bits)]
    return [("shard", 1 << i, bits - 1 - i) for i in range(bits - 1, 0, -1)]


def my_bit(axis, bit):
    return (lax.axis_index(axis) // bit) % 2


def gather_tp_start(own):
    return [
        route(
            own,
            lambda s, c, t, d=d: (s - s % 2 + t // 2, c, (2 * (s % 2) + t % 2) ^ d),
        )
        for d in range(4)
    ]


def gather_tp_finish(parts):
    t = lax.axis_index("tp")
    dim = shard_bits() - 1
    shape = (1,) * dim + (1, 1) + parts[0].shape
    return [
        jnp.concatenate(
            [lax.select_n(t ^ (2 * j + s), *parts).reshape(shape) for j in range(2)], axis=dim
        )
        for s in range(2)
    ]


def join(cur, other, axis, bit, dim):
    first = my_bit(axis, bit) == 0
    return jnp.concatenate([jnp.where(first, cur, other), jnp.where(first, other, cur)], axis=dim)


def gather_start(cur, name):
    axis, bit, _ = steps_of(name)[0]
    return swap(cur, axis, bit)


def gather_finish(cur, other, name):
    first, *rest = steps_of(name)
    cur = join(cur, other, *first)
    for axis, bit, dim in rest:
        cur = join(cur, swap(cur, axis, bit), axis, bit, dim)
    return cur


def flat_rows(cur):
    return cur.reshape(-1, cur.shape[-1])


def split_rows(full):
    rows = full.shape[-2] // (lax.axis_size("shard") * lax.axis_size("ctx"))
    return full.reshape(full.shape[:-2] + (2,) * (shard_bits() + 1) + (rows, full.shape[-1]))


def scatter_start(cur, name, lead=0):
    axis, bit, dim = steps_of(name)[0]
    return swap(lax.dynamic_slice_in_dim(cur, 1 - my_bit(axis, bit), 1, dim + lead), axis, bit)


def scatter_finish(cur, other, name, lead=0):
    first, *rest = steps_of(name)
    kept = lax.dynamic_slice_in_dim(cur, my_bit(*first[:2]), 1, first[2] + lead)
    cur = (kept.astype(jnp.float32) + other.astype(jnp.float32)).astype(jnp.bfloat16)
    for axis, bit, dim in rest:
        mine = my_bit(axis, bit)
        other = swap(lax.dynamic_slice_in_dim(cur, 1 - mine, 1, dim + lead), axis, bit)
        kept = lax.dynamic_slice_in_dim(cur, mine, 1, dim + lead)
        cur = (kept.astype(jnp.float32) + other.astype(jnp.float32)).astype(jnp.bfloat16)
    return cur


def scatter_rest(cur, name, lead=0):
    for axis, bit, dim in steps_of(name)[1:]:
        mine = my_bit(axis, bit)
        other = swap(lax.dynamic_slice_in_dim(cur, 1 - mine, 1, dim + lead), axis, bit)
        kept = lax.dynamic_slice_in_dim(cur, mine, 1, dim + lead)
        cur = (kept.astype(jnp.float32) + other.astype(jnp.float32)).astype(jnp.bfloat16)
    return cur


def scatter_tp_start(first, second):
    z = lax.axis_index("tp")
    blocks = [lax.index_in_dim(s, j, s.ndim - 4, False) for j in range(2) for s in (first, second)]
    return [
        route(
            lax.select_n(z ^ d, *blocks),
            lambda s, c, t, d=d: (s - s % 2 + ((t ^ d) >> 1), c, 2 * (s % 2) + ((t ^ d) & 1)),
        )
        for d in range(4)
    ]


def sum_all(parts):
    total = parts[0].astype(jnp.float32)
    for part in parts[1:]:
        total = total + part.astype(jnp.float32)
    return total


def two_heads(pair):
    lane = lax.broadcasted_iota(jnp.int32, pair.shape, 1)
    zero = jnp.zeros_like(pair)
    return jnp.concatenate(
        [jnp.where(lane < DH, pair, zero), jnp.where(lane < DH, zero, pair)], axis=0
    )


def fold_heads(wide):
    rows = wide.shape[1] // 2
    both = jnp.concatenate([wide[:DH, :rows], wide[DH:, rows:]], axis=0)
    return both.T


def document(ends, start, stop, most):
    low, high = start * 0, start * 0 + most
    for d in range(SEG_COUNT):
        low = jnp.maximum(low, jnp.where(ends[d] <= start, ends[d], 0))
        high = jnp.minimum(high, jnp.where(ends[d] > stop, ends[d], most))
    return low, high


def key_blocks(ends, qb, span, size):
    length = span // 2
    here = ends[SEG_COUNT]
    far = length - here
    start = here + qb * BQ
    low, high = document(ends, start, start + BQ - 1, span)
    first = jnp.clip(low - here, 0, length) // size
    count = (jnp.clip(high - here, 0, length) + (size - 1)) // size - first
    first_far = jnp.clip(low - far, 0, length) // size
    count_far = (jnp.clip(high - far, 0, length) + (size - 1)) // size - first_far
    count_far = jnp.maximum(count_far, 0)

    def block(i):
        is_here = i < count
        kb = jnp.where(is_here, first + i, length // size + first_far + (i - count))
        return kb, kb * size + jnp.where(is_here, here, far - length)

    return count + count_far, block


def query_bounds(ends, qb, span):
    pos = ends[SEG_COUNT] + qb * BQ + lax.broadcasted_iota(jnp.int32, (1, BQ), 1)
    return document(ends, pos, pos, span)


def key_mask(bounds, base, size):
    key_pos = lax.broadcasted_iota(jnp.int32, (size, BQ), 0) + base
    same = (key_pos >= bounds[0]) & (key_pos < bounds[1])
    return jnp.concatenate([same, same], axis=1)


def attn_fwd_kernel(first_block, ends, q_ref, k_ref, v_ref, o_ref, lse_ref, acc, top, den):
    span = k_ref.shape[0]
    qb = pl.program_id(0) + first_block
    pairs = q_ref.shape[1] // 128
    acc[...] = jnp.zeros_like(acc)
    top[...] = jnp.full_like(top, mask_fill)
    den[...] = jnp.zeros_like(den)
    queries = [two_heads(q_ref[:, 128 * p : 128 * p + 128]) for p in range(pairs)]
    bounds = query_bounds(ends, qb, span)
    count, block = key_blocks(ends, qb, span, BK_FWD)

    @pl.loop(0, count)
    def _(i):
        kb, base = block(i)
        rows = pl.ds(pl.multiple_of(kb * BK_FWD, BK_FWD), BK_FWD)
        same = key_mask(bounds, base, BK_FWD)
        for p in range(pairs):
            cols = slice(128 * p, 128 * p + 128)
            s = dot(k_ref[rows, cols], queries[p], NT)
            s = jnp.where(same, s, mask_fill)
            old = top[p]
            new = jnp.maximum(old, jnp.max(s, axis=0, keepdims=True))
            e = jnp.exp(s - new)
            shrink = jnp.exp(old - new)
            den[p] = den[p] * shrink + jnp.sum(e, axis=0, keepdims=True)
            top[p] = new
            acc[p] = acc[p] * shrink + dot(v_ref[rows, cols], e.astype(jnp.bfloat16), TN)

    for p in range(pairs):
        out = fold_heads(acc[p] / den[p])
        o_ref[:, 128 * p : 128 * p + 128] = out.astype(o_ref.dtype)
        lse_ref[p] = top[p] + jnp.log(den[p])


def row_sums(grads, outs):
    prod = (grads.astype(jnp.float32) * outs.astype(jnp.float32)).T
    return jnp.concatenate(
        [jnp.sum(prod[:DH], axis=0, keepdims=True), jnp.sum(prod[DH:], axis=0, keepdims=True)],
        axis=1,
    )


def attn_bwd_kernel(
    ends,
    q_ref,
    do_ref,
    o_low,
    o_high,
    lse_low,
    lse_high,
    k_ref,
    v_ref,
    dq_ref,
    dk_ref,
    dv_ref,
    dk_acc,
    dv_acc,
    dq_acc,
):
    span = k_ref.shape[0]
    qb = pl.program_id(0)
    is_low = qb < pl.num_programs(0) // 2
    pairs = q_ref.shape[1] // 128
    cols = [slice(128 * p, 128 * p + 128) for p in range(pairs)]

    @pl.when(qb == 0)
    def _():
        dk_acc[...] = jnp.zeros_like(dk_acc)
        dv_acc[...] = jnp.zeros_like(dv_acc)

    dq_acc[...] = jnp.zeros_like(dq_acc)
    outs = jnp.where(is_low, o_low[...], o_high[...])
    lses = jnp.where(is_low, lse_low[...], lse_high[...])
    queries = [two_heads(q_ref[:, c]) for c in cols]
    grads = [two_heads(do_ref[:, c]) for c in cols]
    deltas = [row_sums(do_ref[:, c], outs[:, c]) for c in cols]
    bounds = query_bounds(ends, qb, span)
    count, block = key_blocks(ends, qb, span, BK_BWD)

    @pl.loop(0, count)
    def _(i):
        kb, base = block(i)
        rows = pl.ds(pl.multiple_of(kb * BK_BWD, BK_BWD), BK_BWD)
        same = key_mask(bounds, base, BK_BWD)
        for p, c in enumerate(cols):
            keys = k_ref[rows, c]
            s = dot(keys, queries[p], NT)
            probs = jnp.exp(jnp.where(same, s, mask_fill) - lses[p])
            dp = dot(v_ref[rows, c], grads[p], NT)
            ds = (probs * (dp - deltas[p])).astype(jnp.bfloat16)
            dv_acc[rows, c] += dot(probs.astype(jnp.bfloat16), grads[p])
            dk_acc[rows, c] += dot(ds, queries[p])
            dq_acc[p] += dot(keys, ds, TN)

    for p, c in enumerate(cols):
        dq_ref[:, c] = (fold_heads(dq_acc[p]) * (DH**-0.5)).astype(dq_ref.dtype)

    @pl.when(qb == pl.num_programs(0) - 1)
    def _():
        dk_ref[...] = dk_acc[...].astype(dk_ref.dtype)
        dv_ref[...] = dv_acc[...].astype(dv_ref.dtype)


def in_hbm(*arrays):
    return [pltpu.with_memory_space_constraint(a, pltpu.HBM) for a in arrays]


def params(mib):
    return pltpu.CompilerParams(vmem_limit_bytes=mib * 2**20)


def cost(seconds):
    return pl.CostEstimate(flops=int(seconds * 1.15e15), bytes_accessed=2**20, transcendentals=0)


def attn_forward(ends, first_block, queries, keys, values):
    rows, width = queries.shape
    span = keys.shape[0]
    pairs = width // 128
    every = pl.BlockSpec((span, width), lambda i, e: (0, 0))
    return pl.pallas_call(
        functools.partial(attn_fwd_kernel, first_block),
        grid_spec=pltpu.PrefetchScalarGridSpec(
            num_scalar_prefetch=1,
            grid=(rows // BQ // 2,),
            in_specs=[
                pl.BlockSpec((BQ, width), lambda i, e: (i + first_block, 0)),
                every,
                every,
            ],
            out_specs=[
                pl.BlockSpec((BQ, width), lambda i, e: (i, 0)),
                pl.BlockSpec((pairs, 1, 2 * BQ), lambda i, e: (0, 0, i)),
            ],
            scratch_shapes=[
                pltpu.VMEM((pairs, 128, 2 * BQ), jnp.float32),
                pltpu.VMEM((pairs, 1, 2 * BQ), jnp.float32),
                pltpu.VMEM((pairs, 1, 2 * BQ), jnp.float32),
            ],
        ),
        out_shape=[
            jax.ShapeDtypeStruct((rows // 2, width), jnp.bfloat16),
            jax.ShapeDtypeStruct((pairs, 1, rows), jnp.float32),
        ],
        compiler_params=params(VMEM_MIB),
        cost_estimate=cost(10e-6),
        name="attn_fwd",
    )(ends, queries, keys, values)


def attn_backward(ends, start, pairs, queries, grads, mixed, lse, keys, values):
    rows = queries.shape[0]
    span = keys.shape[0]
    half = rows // BQ // 2
    width = 128 * pairs
    col = start // pairs
    tile = pl.BlockSpec((BQ, width), lambda i, e: (i, col))
    low = pl.BlockSpec((BQ, width), lambda i, e: (jnp.minimum(i, half - 1), col))
    high = pl.BlockSpec((BQ, width), lambda i, e: (jnp.maximum(i - half, 0), col))
    low_line = pl.BlockSpec((pairs, 1, 2 * BQ), lambda i, e: (col, 0, jnp.minimum(i, half - 1)))
    high_line = pl.BlockSpec((pairs, 1, 2 * BQ), lambda i, e: (col, 0, jnp.maximum(i - half, 0)))
    every = pl.BlockSpec((span, width), lambda i, e: (0, col))
    out = pl.BlockSpec((span, width), lambda i, e: (0, 0))
    shape = jax.ShapeDtypeStruct((span, width), jnp.bfloat16)
    return pl.pallas_call(
        attn_bwd_kernel,
        grid_spec=pltpu.PrefetchScalarGridSpec(
            num_scalar_prefetch=1,
            grid=(rows // BQ,),
            in_specs=[tile, tile, low, high, low_line, high_line, every, every],
            out_specs=[pl.BlockSpec((BQ, width), lambda i, e: (i, 0)), out, out],
            scratch_shapes=[
                pltpu.VMEM((span, width), jnp.float32),
                pltpu.VMEM((span, width), jnp.float32),
                pltpu.VMEM((pairs, 128, 2 * BQ), jnp.float32),
            ],
        ),
        out_shape=[jax.ShapeDtypeStruct((rows, width), jnp.bfloat16), shape, shape],
        compiler_params=params(VMEM_MIB),
        cost_estimate=cost(1e-6 * pairs),
        name="attn_bwd",
    )(ends, queries, grads, *mixed, *lse, keys, values)


def full_spec(shape):
    return pl.BlockSpec(shape, lambda i: (0,) * len(shape))


def rows_spec(rows, cols):
    return pl.BlockSpec((rows, cols), lambda i: (i, 0))


def pack_kernel(q_ref, k_ref, v_ref, out_ref):
    parts = [q_ref[...], k_ref[...], v_ref[...]]
    for i, part in enumerate(parts):
        out_ref[:, 128 * i : 128 * i + 128] = part[:, :128]
    thirds = [p[:, 128:] for p in parts]
    thirds.append(jnp.zeros_like(thirds[0]))
    out_ref[:, 384:512] = jnp.concatenate(thirds[:2], axis=1)
    out_ref[:, 512:640] = jnp.concatenate(thirds[2:], axis=1)


def pack_heads(*parts):
    return pl.pallas_call(
        pack_kernel,
        out_shape=jax.ShapeDtypeStruct((parts[0].shape[0], 640), parts[0].dtype),
        compiler_params=params(8),
        cost_estimate=cost(1e-6),
        name="pack_heads",
    )(*parts)


def build_heads(outs, a_ref, b_ref):
    for i, out in enumerate(outs):
        lo = 384 + DH * i
        out[:, :128] = a_ref[:, 128 * i : 128 * i + 128]
        out[:, 128:256] = b_ref[:, 128 * i : 128 * i + 128]
        out[:, 256:] = jnp.concatenate([a_ref[:, lo : lo + DH], b_ref[:, lo : lo + DH]], axis=1)


def qkv_kernel(x_ref, a_ref, b_ref, q_ref, k_ref, v_ref, wq, wk, wv):
    step = pl.program_id(0)

    @pl.when(step == 0)
    def _():
        build_heads((wq, wk, wv), a_ref, b_ref)

    x = x_ref[...]
    k_ref[...] = dot(x, wk[...]).astype(k_ref.dtype)
    v_ref[...] = dot(x, wv[...]).astype(v_ref.dtype)

    @pl.when(step < pl.num_programs(0) // 2)
    def _():
        q = dot(x, wq[...]).astype(jnp.bfloat16).astype(jnp.float32)
        q_ref[...] = (q * DH**-0.5).astype(q_ref.dtype)


def project(tok_all, w_a, w_b):
    span, width = tok_all.shape
    block = 512
    steps = span // block
    cols = 384
    low = jnp.bfloat16
    return pl.pallas_call(
        qkv_kernel,
        grid=(steps,),
        in_specs=[rows_spec(block, width), full_spec(w_a.shape), full_spec(w_b.shape)],
        out_specs=[
            pl.BlockSpec((block, cols), lambda i: (jnp.minimum(i, steps // 2 - 1), 0)),
            rows_spec(block, cols),
            rows_spec(block, cols),
        ],
        out_shape=[
            jax.ShapeDtypeStruct((span // 2, cols), low),
            jax.ShapeDtypeStruct((span, cols), low),
            jax.ShapeDtypeStruct((span, cols), low),
        ],
        scratch_shapes=[pltpu.VMEM((width, cols), low)] * 3,
        compiler_params=params(VMEM_MIB),
        cost_estimate=cost(6e-6),
        name="qkv",
    )(tok_all, w_a, w_b)


def attn_out_kernel(low_ref, high_ref, a_ref, b_ref, part_ref, ow_ref, proj_ref, norms_ref):
    step = pl.program_id(0)

    @pl.when(step == 0)
    def _():
        ow_ref[:, :128] = a_ref[:, :128]
        ow_ref[:, 128:256] = b_ref[:, :128]
        ow_ref[:, 256:] = jnp.concatenate([a_ref[:, 128:192], b_ref[:, 128:192]], axis=1)
        proj_ref[...] = a_ref[:, 192:320]
        turned = a_ref[:, 256:384].astype(jnp.float32).T
        norms_ref[...] = turned[64:72]

    mixed = jnp.where(step < pl.num_programs(0) // 2, low_ref[...], high_ref[...])
    part_ref[...] = dot(mixed, ow_ref[...], NT).astype(part_ref.dtype)


def attn_out(mixed, w_a, w_b):
    half, cols = mixed[0].shape
    width = w_a.shape[0]
    block = 256
    per = half // block
    low = jnp.bfloat16
    third = pl.BlockSpec((width, 384), lambda i: (0, w_a.shape[1] // 384 - 1))
    return pl.pallas_call(
        attn_out_kernel,
        grid=(2 * per,),
        in_specs=[
            pl.BlockSpec((block, cols), lambda i: (jnp.minimum(i, per - 1), 0)),
            pl.BlockSpec((block, cols), lambda i: (jnp.maximum(i - per, 0), 0)),
            third,
            third,
        ],
        out_specs=[
            rows_spec(block, width),
            full_spec((width, cols)),
            full_spec((width, 128)),
            full_spec((8, width)),
        ],
        out_shape=[
            jax.ShapeDtypeStruct((2 * half, width), low),
            jax.ShapeDtypeStruct((width, cols), low),
            jax.ShapeDtypeStruct((width, 128), low),
            jax.ShapeDtypeStruct((8, width), jnp.float32),
        ],
        compiler_params=params(VMEM_MIB),
        cost_estimate=cost(3e-6),
        name="attn_out",
    )(*mixed, w_a, w_b)


def normalize(hidden):
    row_mean = jnp.mean(hidden, axis=-1, keepdims=True)
    centred = hidden - row_mean
    variance = jnp.mean(centred * centred, axis=-1, keepdims=True)
    inv_std = lax.rsqrt(variance + eps_norm)
    return centred * inv_std, inv_std


def norm_backward(grad_out, normed, inv_std, gain):
    scaled = grad_out * gain
    return inv_std * (
        scaled
        - jnp.mean(scaled, axis=-1, keepdims=True)
        - normed * jnp.mean(scaled * normed, axis=-1, keepdims=True)
    )


def wide(ref):
    return ref[...].astype(jnp.float32)


def gelu_parts(v):
    e = jnp.exp(v * v * -0.5)
    t = 1.0 / (1.0 + (0.3275911 * 0.5**0.5) * jnp.abs(v))
    poly = 0.5 * 1.061405429
    for c in (-1.453152027, 1.421413741, -0.284496736, 0.254829592):
        poly = poly * t + 0.5 * c
    upper = poly * t * e
    cdf = jnp.where(v >= 0, 1.0 - upper, upper)
    return v * cdf, cdf + v * e * 0.3989422804014327


def ffn_kernel(
    x_ref, mine_ref, got_ref, norms, ia, ib, normed_ref, inv_ref, low_ref, act_ref, slope_ref
):
    step = pl.program_id(0)
    steps = pl.num_programs(0)
    parts = [slice(r, r + 256) for r in range(0, x_ref.shape[0], 256)]

    @pl.when(step == 0)
    def _():
        for rows in parts:
            hidden = x_ref[rows, :].astype(jnp.float32) + (
                mine_ref[rows, :].astype(jnp.float32) + got_ref[rows, :].astype(jnp.float32)
            )
            normed, inv = normalize(hidden)
            normed_ref[rows, :] = normed.astype(normed_ref.dtype)
            inv_ref[rows, :] = jnp.broadcast_to(inv, (256, 128))
            low_ref[rows, :] = (normed * norms[0:1, :] + norms[1:2, :]).astype(low_ref.dtype)

    def work(i_ref):
        for rows in parts:
            act, slope = gelu_parts(dot(low_ref[rows, :], i_ref[...]))
            act_ref[rows, :] = act.astype(act_ref.dtype)
            slope_ref[rows, :] = slope.astype(slope_ref.dtype)

    first = step < steps // 2
    pl.when(first)(lambda: work(ia))
    pl.when(jnp.logical_not(first))(lambda: work(ib))


def slice_specs(width, cols, per):
    return [
        pl.BlockSpec((width, cols), lambda i: (0, jnp.minimum(i, per - 1))),
        pl.BlockSpec((width, cols), lambda i: (0, jnp.maximum(i - per, 0))),
    ]


FFN_COLS = 256
GROUPS = 1


def feed_forward(tok, mine, got, norms, inner, hidden):
    rows, width = tok.shape
    cols = FFN_COLS
    per = hidden // cols
    tile = full_spec((rows, width))
    chunk = pl.BlockSpec((rows, cols), lambda i: (0, i))
    low = jax.ShapeDtypeStruct((rows, width), jnp.bfloat16)
    units = jax.ShapeDtypeStruct((rows, 2 * hidden), jnp.bfloat16)
    return pl.pallas_call(
        ffn_kernel,
        grid=(2 * per,),
        in_specs=[tile, tile, tile, full_spec(norms.shape)]
        + slice_specs(width, cols, per),
        out_specs=[tile, full_spec((rows, 128)), tile, chunk, chunk],
        out_shape=[low, jax.ShapeDtypeStruct((rows, 128), jnp.float32), low, units, units],
        compiler_params=params(VMEM_MIB),
        cost_estimate=cost(14e-6),
        name="feed_forward",
    )(tok, mine, got, norms, *inner)


def ffn_out_kernel(act_ref, a_ref, b_ref, out_ref):
    hidden = a_ref.shape[1]
    part = dot(act_ref[:, :hidden], a_ref[...], NT) + dot(act_ref[:, hidden:], b_ref[...], NT)
    out_ref[...] = part.astype(out_ref.dtype)


def ffn_out(act, w_a, w_b):
    rows = act.shape[0]
    width = w_a.shape[0]
    block = 256
    return pl.pallas_call(
        ffn_out_kernel,
        grid=(rows // block,),
        in_specs=[rows_spec(block, act.shape[1]), full_spec(w_a.shape), full_spec(w_b.shape)],
        out_specs=rows_spec(block, width),
        out_shape=jax.ShapeDtypeStruct((rows, width), jnp.bfloat16),
        compiler_params=params(VMEM_MIB),
        cost_estimate=cost(3e-6),
        name="ffn_out",
    )(act, w_a, w_b)


def middle_kernel(
    normed_ref, mine_ref, got_ref, norms, proj_ref, cot_ref, emb_ref, gh2_ref, low_ref, pg_ref, vec_ref
):
    step = pl.program_id(0)
    first = wide(normed_ref) * norms[0:1, :] + norms[1:2, :]
    normed, inv = normalize(first + (wide(mine_ref) + wide(got_ref)))
    second = (normed * norms[2:3, :] + norms[3:4, :]).astype(jnp.bfloat16)
    projected = dot(second, proj_ref[...])
    inv_norm = lax.rsqrt(jnp.sum(projected * projected, axis=-1, keepdims=True) + eps_unit)
    embedding = projected * inv_norm
    emb_ref[...] = embedding
    cot = wide(cot_ref)
    radial = jnp.sum(cot * embedding, axis=-1, keepdims=True)
    grad_projected = (inv_norm * (cot - embedding * radial)).astype(jnp.bfloat16)
    grad_second = dot(grad_projected, proj_ref[...], NT)
    grad = norm_backward(grad_second, normed, inv, norms[2:3, :])
    gh2_ref[...] = grad
    low_ref[...] = grad.astype(low_ref.dtype)

    @pl.when(step == 0)
    def _():
        pg_ref[...] = jnp.zeros_like(pg_ref)
        vec_ref[...] = jnp.zeros_like(vec_ref)

    pg_ref[...] += dot(second, grad_projected, TN)
    vec_ref[0:1, :] += jnp.sum(grad_second * normed, axis=0, keepdims=True)
    vec_ref[1:2, :] += jnp.sum(grad_second, axis=0, keepdims=True)


def middle(normed, mine, got, norms, proj, cot):
    rows, width = normed.shape
    p_width = proj.shape[1]
    block = 256
    tile = rows_spec(block, width)
    return pl.pallas_call(
        middle_kernel,
        grid=(rows // block,),
        in_specs=[
            tile,
            tile,
            tile,
            full_spec(norms.shape),
            full_spec(proj.shape),
            rows_spec(block, p_width),
        ],
        out_specs=[
            rows_spec(block, p_width),
            tile,
            tile,
            full_spec((width, p_width)),
            full_spec((8, width)),
        ],
        out_shape=[
            jax.ShapeDtypeStruct((rows, p_width), jnp.float32),
            jax.ShapeDtypeStruct((rows, width), jnp.float32),
            jax.ShapeDtypeStruct((rows, width), jnp.bfloat16),
            jax.ShapeDtypeStruct((width, p_width), jnp.float32),
            jax.ShapeDtypeStruct((8, width), jnp.float32),
        ],
        compiler_params=params(VMEM_MIB),
        cost_estimate=cost(5e-6),
        name="middle",
    )(normed, mine, got, norms, proj, cot)


def ffn_back_kernel(
    turns, bits, g_ref, x_ref, act_ref, slope_ref, ia, ib, oa, ob, keep_a, send_a, keep_b, send_b, out_ref, acc, g_t, x_t, wgrad
):
    step = pl.program_id(0)
    steps = pl.num_programs(0)

    @pl.when(step == 0)
    def _():
        g_t[...] = g_ref[...].T
        x_t[...] = x_ref[...].T
        acc[...] = jnp.zeros_like(acc)

    def put(which, run, keep, send, bit):
        for j in range(keep.shape[1] // run):
            for out, side in ((keep, bit), (send, 1 - bit)):
                rows = pl.ds(pl.multiple_of((2 * j + side) * run, run), run)
                out[which, j * run : (j + 1) * run, :] = wgrad[rows, :].astype(out.dtype)

    def work(i_ref, o_ref, run, keep, send, bit):
        wgrad[...] = dot(g_t[...], act_ref[...])
        put(0, run, keep, send, bit)
        grad = dot(g_ref[...], o_ref[...]) * slope_ref[...].astype(jnp.float32)
        grad = grad.astype(jnp.bfloat16)
        wgrad[...] = dot(x_t[...], grad)
        put(1, run, keep, send, bit)
        acc[...] += dot(grad, i_ref[...], NT)

    first = step < steps // 2
    pl.when(first)(lambda: work(ia, oa, turns[0], keep_a, send_a, bits[0]))
    pl.when(jnp.logical_not(first))(lambda: work(ib, ob, turns[1], keep_b, send_b, bits[1]))

    @pl.when(step == steps - 1)
    def _():
        out_ref[...] = acc[...].astype(out_ref.dtype)


def ffn_back(bits, turns, grad, x, act, slope, inner, outer, hidden):
    rows, width = grad.shape
    cols = FFN_COLS
    per = hidden // cols

    def left(i):
        return jnp.minimum(i, per - 1)

    def right(i):
        return jnp.maximum(i - per, 0)

    tile = pl.BlockSpec((rows, width), lambda i, e: (0, 0))
    chunk = pl.BlockSpec((rows, cols), lambda i, e: (0, i))
    mats = [
        pl.BlockSpec((width, cols), lambda i, e: (0, left(i))),
        pl.BlockSpec((width, cols), lambda i, e: (0, right(i))),
    ]
    outs = [
        pl.BlockSpec((2, width // 2, cols), lambda i, e: (0, 0, left(i))),
        pl.BlockSpec((2, width // 2, cols), lambda i, e: (0, 0, right(i))),
    ]
    low = jnp.bfloat16
    shape = jax.ShapeDtypeStruct((2, width // 2, hidden), low)
    return pl.pallas_call(
        functools.partial(ffn_back_kernel, turns),
        grid_spec=pltpu.PrefetchScalarGridSpec(
            num_scalar_prefetch=1,
            grid=(2 * per,),
            in_specs=[tile, tile, chunk, chunk] + mats * 2,
            out_specs=[outs[0], outs[0], outs[1], outs[1], tile],
            scratch_shapes=[
                pltpu.VMEM((rows, width), jnp.float32),
                pltpu.VMEM((width, rows), low),
                pltpu.VMEM((width, rows), low),
                pltpu.VMEM((width, cols), jnp.float32),
            ],
        ),
        out_shape=[pltpu.HBM(shape.shape, low)] * 4 + [jax.ShapeDtypeStruct((rows, width), low)],
        compiler_params=params(VMEM_MIB),
        cost_estimate=cost(17e-6),
        name="ffn_back",
    )(bits, grad, *in_hbm(x, act, slope, *inner, *outer))


def first_back_kernel(
    mine_ref,
    got_ref,
    gh2_ref,
    normed_ref,
    inv_ref,
    norms,
    ow_ref,
    low_ref,
    high_ref,
    pg_ref,
    vec2_ref,
    gh1_ref,
    gmix_ref,
    og_ref,
    small_ref,
    og_acc,
    vec,
):
    step = pl.program_id(0)
    steps = pl.num_programs(0)

    @pl.when(step == 0)
    def _():
        og_acc[...] = jnp.zeros_like(og_acc)
        vec[...] = jnp.zeros_like(vec)
        vec[2:4, :] = vec2_ref[0:2, :]

    grad = gh2_ref[...] + (wide(mine_ref) + wide(got_ref))
    normed = wide(normed_ref)
    vec[0:1, :] += jnp.sum(grad * normed, axis=0, keepdims=True)
    vec[1:2, :] += jnp.sum(grad, axis=0, keepdims=True)
    grad_h1 = norm_backward(grad, normed, inv_ref[:, 0:1], norms[0:1, :])
    gh1_ref[...] = grad_h1
    low = grad_h1.astype(jnp.bfloat16)
    gmix_ref[...] = dot(low, ow_ref[...]).astype(gmix_ref.dtype)
    mixed = jnp.where(step < steps // 2, low_ref[...], high_ref[...])
    og_acc[...] += dot(low, mixed, TN)

    @pl.when(step == steps - 1)
    def _():
        og_ref[...] = og_acc[...].astype(og_ref.dtype)
        p_width = pg_ref.shape[1]
        small_ref[:, :p_width] = pg_ref[...].astype(small_ref.dtype)
        small_ref[:, p_width:] = vec[...].T.astype(small_ref.dtype)


def first_back(mine, got, grad_h2, normed, inv, norms, output_w, mixed, proj_part, vec2):
    rows, width = grad_h2.shape
    cols = output_w.shape[1]
    block = 256
    per = rows // block // 2
    tile = rows_spec(block, width)
    low = jnp.bfloat16
    p_width = proj_part.shape[1]
    return pl.pallas_call(
        first_back_kernel,
        grid=(2 * per,),
        in_specs=[
            tile,
            tile,
            tile,
            tile,
            rows_spec(block, 128),
            full_spec(norms.shape),
            full_spec(output_w.shape),
            pl.BlockSpec((block, cols), lambda i: (jnp.minimum(i, per - 1), 0)),
            pl.BlockSpec((block, cols), lambda i: (jnp.maximum(i - per, 0), 0)),
            full_spec(proj_part.shape),
            full_spec(vec2.shape),
        ],
        out_specs=[
            tile,
            rows_spec(block, cols),
            full_spec((width, cols)),
            full_spec((width, p_width + 128)),
        ],
        out_shape=[
            pltpu.HBM((rows, width), jnp.float32),
            jax.ShapeDtypeStruct((rows, cols), low),
            jax.ShapeDtypeStruct((width, cols), low),
            jax.ShapeDtypeStruct((width, p_width + 128), low),
        ],
        scratch_shapes=[pltpu.VMEM((width, cols), jnp.float32), pltpu.VMEM((128, width), jnp.float32)],
        compiler_params=params(VMEM_MIB),
        cost_estimate=cost(1e-6),
        name="first_back",
    )(mine, got, *in_hbm(grad_h2, normed, inv), norms, *in_hbm(output_w, *mixed, proj_part), vec2)


def token_grads_kernel(core, *refs):
    *parts, a_ref, b_ref, theirs, mine, wq, wk, wv = refs
    step = pl.program_id(0)
    weights = (wq, wk, wv)[-(len(parts) // GROUPS) :]

    @pl.when(step == 0)
    def _():
        build_heads((wq, wk, wv), a_ref, b_ref)

    total = 0.0
    for i, w in enumerate(weights):
        grads = [parts[p * len(weights) + i][...] for p in range(GROUPS)]
        total = total + dot(jnp.concatenate(grads, axis=1), w[...], NT)

    @pl.when(step == 0)
    def _():
        theirs[...] = total.astype(theirs.dtype)

    @pl.when(step == 1)
    def _():
        mine[...] = total.astype(mine.dtype)


def token_grads(core, far, grads, w_a, w_b):
    half = grads[0][0].shape[0] // 2
    width = w_a.shape[0]
    skip = 2 if far else 0
    used = [arrays[1:] if far else arrays for arrays in grads]
    rows = lambda i, core: (skip + jnp.where(i < 1, 1 - core[0], core[0]), 0)
    specs = [pl.BlockSpec((half, x.shape[1]), rows) for arrays in used for x in arrays]
    mat = pl.BlockSpec(w_a.shape, lambda i, core: (0, 0))
    shape = jax.ShapeDtypeStruct((half, width), jnp.bfloat16)
    whole = pl.BlockSpec((half, width), lambda i, core: (0, 0))
    return pl.pallas_call(
        token_grads_kernel,
        grid_spec=pltpu.PrefetchScalarGridSpec(
            num_scalar_prefetch=1,
            grid=(2,),
            in_specs=specs + [mat, mat],
            out_specs=[whole, whole],
            scratch_shapes=[pltpu.VMEM((width, 384), jnp.bfloat16)] * 3,
        ),
        out_shape=[shape, shape],
        compiler_params=params(VMEM_MIB),
        cost_estimate=cost(0.5e-6),
        name="token_grads",
    )(core.reshape(1), *[x for arrays in used for x in arrays], w_a, w_b)


def head_grads_kernel(x_ref, *refs):
    *parts, og_ref, twos, thirds, acc = refs
    step = pl.program_id(0)
    steps = pl.num_programs(0)

    @pl.when(step == 0)
    def _():
        acc[...] = jnp.zeros_like(acc)

    x_t = x_ref[...].T

    def add(i):
        grads = [parts[3 * p + i][...] for p in range(GROUPS)]
        acc[i] += dot(x_t, jnp.concatenate(grads, axis=1))

    add(1)
    add(2)
    pl.when(step < steps // 2)(lambda: add(0))

    @pl.when(step == steps - 1)
    def _():
        for s in range(2):
            for i in range(4):
                part = og_ref if i == 3 else acc.at[i]
                lo = 128 * s
                twos[s, :, 128 * i : 128 * i + 128] = part[:, lo : lo + 128].astype(twos.dtype)
            for i in (0, 2):
                lo = 256 + DH * s
                both = [
                    (og_ref if j == 3 else acc.at[j])[:, lo : lo + DH].astype(thirds.dtype)
                    for j in (i, i + 1)
                ]
                thirds[s, :, DH * i : DH * i + 128] = jnp.concatenate(both, axis=1)


def head_grads(tok_all, grads, output_part):
    span, width = tok_all.shape
    block = 512
    steps = span // block
    near = lambda i: (jnp.minimum(i, steps // 2 - 1), 0)
    specs = []
    for dq, _, _ in grads:
        cols = dq.shape[1]
        specs += [pl.BlockSpec((block, cols), near), rows_spec(block, cols), rows_spec(block, cols)]
    return pl.pallas_call(
        head_grads_kernel,
        grid=(steps,),
        in_specs=[rows_spec(block, width)] + specs + [full_spec(output_part.shape)],
        out_specs=[full_spec((2, width, 512)), full_spec((2, width, 256))],
        out_shape=[
            jax.ShapeDtypeStruct((2, width, 512), jnp.bfloat16),
            jax.ShapeDtypeStruct((2, width, 256), jnp.bfloat16),
        ],
        scratch_shapes=[pltpu.VMEM((3, width, 384), jnp.float32)],
        compiler_params=params(VMEM_MIB),
        cost_estimate=cost(0.5e-6),
        name="head_grads",
    )(*in_hbm(tok_all), *[x for arrays in grads for x in arrays], output_part)


def finish_kernel(p0, p1, p2, p3, small, q_ref, k_ref, v_ref, o_ref, proj_ref, vec_ref):
    total = (wide(p0) + wide(p1)) + (wide(p2) + wide(p3))
    rows = total.shape[0]

    def part(i):
        third = total[:, 512 + DH * i : 512 + DH * i + DH]
        return jnp.concatenate([total[:, 128 * i : 128 * i + 128], third], axis=1)

    def turned(block):
        pad = jnp.zeros((128 - rows, block.shape[1]), block.dtype)
        return jnp.concatenate([block, pad], axis=0).T[:, :rows]

    for i, out in enumerate((q_ref, k_ref, v_ref)):
        out[...] = part(i)
    o_ref[:128, :] = turned(total[:, 384:512])
    o_ref[128:, :] = turned(total[:, 640:768])[DH:, :]
    sums = wide(small)
    proj_ref[...] = sums[:, :128]
    vec_ref[...] = turned(sums[:, 128:])[:8, :]


def finish(parts, small):
    rows = parts[0].shape[0]
    shapes = [(rows, 192)] * 3 + [(192, rows), (rows, 128), (8, rows)]
    return pl.pallas_call(
        finish_kernel,
        out_shape=[jax.ShapeDtypeStruct(s, jnp.float32) for s in shapes],
        compiler_params=params(16),
        cost_estimate=cost(2e-6),
        name="finish",
    )(*parts, small)


def per_device(
    tokens,
    segments,
    query_weight,
    key_weight,
    value_weight,
    output_weight,
    attn_gain,
    attn_shift,
    inner_weight,
    outer_weight,
    ffn_gain,
    ffn_shift,
    proj_weight,
    grad_embed,
):
    length, model_width = tokens.shape[2:]
    half = length // 2
    core = lax.axis_index("shard") % 2
    ctx = lax.axis_index("ctx")
    group = lax.axis_index("tp")
    micro, seat = group // 2, group % 2
    owner = core == seat
    edge = min(SEG_MOST, length)
    bf16, f32 = jnp.bfloat16, jnp.float32

    def by_core(mine, theirs, axis):
        return jnp.concatenate(
            [jnp.where(core == 0, mine, theirs), jnp.where(core == 0, theirs, mine)], axis=axis
        )

    tok_m = lax.dynamic_index_in_dim(tokens, micro, 0, False)[0]
    sent = lax.dynamic_slice_in_dim(tok_m, (1 - ctx) * (length - edge), edge, 0)
    got = route(sent, lambda s, c, t: (s, 1 - c, t) if s % 2 == t % 2 else None)
    heads_own = pack_heads(query_weight, key_weight, value_weight)
    heads_parts = gather_tp_start(heads_own)
    tokens_in, segments_in, outer_in, output_in, cot_in = after_all(
        heads_own, tokens, segments, outer_weight, output_weight, grad_embed
    )
    vectors = jnp.stack([attn_gain, attn_shift, ffn_gain, ffn_shift])
    vectors = dot(vectors, jnp.eye(4, 64, dtype=bf16), TN).astype(bf16)
    ffn_own = jnp.concatenate([inner_weight, output_in.T, proj_weight, vectors, outer_in.T], axis=1)
    ffn_all = lax.all_gather(ffn_own, "tp", axis=0)
    tok_m = lax.dynamic_index_in_dim(tokens_in, micro, 0, False)[0]

    *heads_parts, got, ffn_own, tok_m, segments_in, cot_in = tie(
        *heads_parts, got, ffn_own, tok_m, segments_in, cot_in
    )
    heads_a, heads_b = gather_tp_finish(heads_parts)
    other_a, other_b = gather_start(heads_a, "y"), gather_start(heads_b, "x")
    tok_got = swap(tok_m, "shard", 1)
    seg_m = lax.dynamic_index_in_dim(segments_in, micro, 0, False)
    seg_m = seg_m.reshape(1, -1, 128)
    upto = jnp.arange(8, dtype=jnp.int32).reshape(8, 1, 1)
    counts_own = jnp.sum((seg_m <= upto).astype(jnp.int32), axis=(1, 2))
    counts_got = swap(counts_own, "shard", 1)
    cot_m = lax.dynamic_index_in_dim(cot_in, micro, 0, False)[0]
    other_a, other_b, tok_got, counts_got, cot_m = tie(other_a, other_b, tok_got, counts_got, cot_m)
    heads_a, heads_b = gather_finish(heads_a, other_a, "y"), gather_finish(heads_b, other_b, "x")
    other_a, other_b = gather_start(heads_a, "x"), gather_start(heads_b, "y")
    got_core = swap(got, "shard", 1)
    cot_got = swap(cot_m, "shard", 1)
    counts = jnp.where(owner, counts_own, counts_got)
    counts = counts + swap(counts, "ctx", 1)
    place_of = jnp.arange(8)
    ends = jnp.where(place_of == SEG_COUNT, ctx * length, counts).astype(jnp.int32)
    tok_here = jnp.where(owner, tok_m, tok_got)
    tok_far = lax.dynamic_update_slice_in_dim(
        jnp.zeros_like(tok_here), jnp.where(owner, got, got_core), ctx * (length - edge), 0
    )
    tok_all = jnp.concatenate([tok_here, tok_far], axis=0)
    cot = jnp.where(owner, cot_m, cot_got)
    other_a, other_b, tok_all, cot, ends = tie(other_a, other_b, tok_all, cot, ends)
    heads_a, heads_b = gather_finish(heads_a, other_a, "x"), gather_finish(heads_b, other_b, "y")
    heads_a, heads_b = flat_rows(heads_a), flat_rows(heads_b)

    core_dim = shard_bits() - 1
    queries, keys, values = project(tok_all, heads_a, heads_b)
    ffn_all = after(ffn_all, keys)
    kept = lax.dynamic_slice_in_dim(ffn_all, 2 * core, 2, 0)
    other = swap(lax.dynamic_slice_in_dim(ffn_all, 2 - 2 * core, 2, 0), "shard", 1)
    shape = (1,) * core_dim + (1, 1) + ffn_own.shape
    split = inner_weight.shape[1] + 384
    inner, outer = [], []
    for s in range(2):
        both = join(kept[s].reshape(shape), other[s].reshape(shape), "shard", 1, core_dim)
        inner.append(both[..., :split])
        outer.append(both[..., split:])
    inner_got = [gather_start(inner[0], "x"), gather_start(inner[1], "y")]
    outer_got = [gather_start(outer[0], "x"), gather_start(outer[1], "y")]
    mixed_low, lse_low = attn_forward(after(ends, *inner, *outer), 0, queries, keys, values)
    mixed_low, *inner_got = tie(mixed_low, *inner_got)
    inner = [gather_finish(inner[0], inner_got[0], "x"), gather_finish(inner[1], inner_got[1], "y")]
    inner_got = [gather_start(inner[0], "y"), gather_start(inner[1], "x")]
    mixed_high, lse_high = attn_forward(
        after(ends, mixed_low, *inner), half // BQ, queries, keys, values
    )
    mixed_high, *got_all = tie(mixed_high, *inner_got, *outer_got)
    outer = [gather_finish(outer[0], got_all[2], "x"), gather_finish(outer[1], got_all[3], "y")]
    outer_got = [gather_start(outer[0], "y"), gather_start(outer[1], "x")]
    inner = [
        flat_rows(gather_finish(inner[0], got_all[0], "y")),
        flat_rows(gather_finish(inner[1], got_all[1], "x")),
    ]
    mixed = (mixed_low, mixed_high)
    part, output_w, proj, norms = attn_out(mixed, *inner)

    hidden_cols = outer_weight.shape[0]
    normed, inv, first_low, act, slope = feed_forward(
        tok_here, part, swap(part, "shard", 1), norms, inner, hidden_cols
    )
    act, *outer_got = tie(act, *outer_got)
    outer = [
        flat_rows(gather_finish(outer[0], outer_got[0], "y")),
        flat_rows(gather_finish(outer[1], outer_got[1], "x")),
    ]
    part = ffn_out(act, *outer)
    embedding, grad_h2, grad_ffn, proj_part, vec2 = middle(
        normed, part, swap(part, "shard", 1), norms, proj, cot
    )

    rows = model_width // (lax.axis_size("shard") * lax.axis_size("ctx"))
    y_axis, y_bit, _ = steps_of("y")[0]
    y_mine = my_bit(y_axis, y_bit)
    x_first = rows % 16 == 0
    bits = jnp.stack([ctx if x_first else y_mine, y_mine]).astype(jnp.int32)
    turns = (rows if x_first else model_width // 2, model_width // 2)
    keep_a, send_a, keep_b, send_b, part = ffn_back(
        bits, turns, grad_ffn, first_low, act, slope, inner, outer, hidden_cols
    )
    wgrad_got = [
        swap(send_a, "ctx", 1) if x_first else swap(send_a, y_axis, y_bit),
        swap(send_b, y_axis, y_bit),
    ]
    part_got = swap(part, "shard", 1)
    grad_h1, grad_mixed, output_part, small = first_back(
        part, part_got, grad_h2, normed, inv, norms, output_w, mixed, proj_part, vec2
    )

    small = split_rows(small)
    small_got = scatter_start(small, "y")
    quarter = half // 2
    emb_half = lax.dynamic_slice_in_dim(after(embedding, grad_mixed), core * half, half, 0)
    emb_got = [
        route(
            lax.select_n(micro ^ d, emb_half[:quarter], emb_half[quarter:]),
            lambda s, c, t, d=d: (s - s % 2 + t % 2, c, 2 * (s % 2) + ((t // 2) ^ d)),
        )
        for d in range(2)
    ]
    flow = (queries, grad_mixed, mixed, (lse_low, lse_high), keys, values)
    grads = attn_backward(after(ends, small, emb_half), 0, 3, *flow)
    *grads, wgrad_got[0], wgrad_got[1], small_got, emb_got[0], emb_got[1] = tie(
        *grads, *wgrad_got, small_got, *emb_got
    )
    grads = [grads]

    def added(kept, got):
        return (kept.astype(f32) + got.astype(f32)).astype(bf16)

    lead = (2,) * (shard_bits() - 1)
    last = (rows, hidden_cols)
    shapes = [(2, *lead, 2, 1, *last), (2, 1, *lead[1:], 2, 2, *last)]
    second_steps = ("y" if x_first else "x", "x")
    wgrad = [
        added(keep_a, wgrad_got[0]).reshape(shapes[0 if x_first else 1]),
        added(keep_b, wgrad_got[1]).reshape(shapes[1]),
    ]
    wgrad = [scatter_rest(w, "y", 1) if n == "x" else w for w, n in zip(wgrad, second_steps)]
    small = scatter_finish(small, small_got, "y")
    *wgrad, small, dq, dk, dv = tie(*wgrad, small, *grads[0])
    grads = [[dq, dk, dv]]
    wgrad_got = [scatter_start(w, n, 1) for w, n in zip(wgrad, second_steps)]
    small_got = scatter_start(small, "x")

    far_theirs, far_mine = token_grads(core, True, grads, heads_a, heads_b)
    near_theirs, near_mine = token_grads(core, False, grads, heads_a, heads_b)
    far_theirs, near_theirs, tok_in = tie(far_theirs, near_theirs, tok_all)
    far_got = swap(far_theirs, "shard", 1)
    near_got = swap(near_theirs, "shard", 1)
    twos, thirds = head_grads(tok_in, grads, output_part)
    twos, thirds, far_got, near_got, small_got, *wgrad_got = tie(
        twos, thirds, far_got, near_got, small_got, *wgrad_got
    )
    far_sum = added(far_mine, far_got)
    from_far = swap(far_sum, "ctx", 1)
    wgrad = [scatter_finish(w, g, n, 1) for w, g, n in zip(wgrad, wgrad_got, second_steps)]
    blocks = jnp.stack([w.reshape(2, 2, rows, hidden_cols) for w in wgrad], axis=0)
    wgrad_theirs = swap(lax.dynamic_index_in_dim(blocks, 1 - core, 2, False), "shard", 1)
    twos, thirds = split_rows(twos), split_rows(thirds)
    twos_got, thirds_got = scatter_start(twos, "y", 1), scatter_start(thirds, "x", 1)
    mine = lax.dynamic_slice_in_dim(grad_h1, core * half, half, 0)
    near_sum = near_mine.astype(f32) + near_got.astype(f32) + mine
    small = scatter_finish(small, small_got, "x")
    near_sum, wgrad_theirs, small = tie(near_sum, wgrad_theirs, small)
    ours = lax.dynamic_index_in_dim(blocks, core, 2, False)
    blocks = by_core(ours, wgrad_theirs, 0).reshape(4, 2 * rows, hidden_cols)
    small = lax.dynamic_index_in_dim(small.reshape(2, rows, -1), core, 0, False)
    extra = small.reshape(1, -1, hidden_cols)
    blocks = jnp.concatenate([blocks, jnp.concatenate([extra] * 4, axis=0)], axis=1)
    wgrad_sum = lax.psum_scatter(blocks, "tp", scatter_dimension=0)
    near_sum, from_far, twos_got, thirds_got = tie(near_sum, from_far, twos_got, thirds_got)
    grad_tok = (near_sum + from_far.astype(f32)).astype(bf16)

    own_cols = model_width // lax.axis_size("tp")
    cols = [grad_tok[:, own_cols * j : own_cols * (j + 1)] for j in range(4)]
    even, odd = jnp.stack(cols[0::2]), jnp.stack(cols[1::2])
    kept = jnp.where(core == 0, even, odd)
    other = swap(jnp.where(core == 0, odd, even), "shard", 1)
    twos = scatter_finish(twos, twos_got, "y", 1)
    thirds = scatter_finish(thirds, thirds_got, "x", 1)
    twos_got, thirds_got = scatter_start(twos, "x", 1), scatter_start(thirds, "y", 1)
    both = [jnp.where(core == 0, kept, other), jnp.where(core == 0, other, kept)]
    both = [jnp.concatenate([both[0][j], both[1][j]], axis=0) for j in range(2)]
    arrived = [
        route(
            lax.select_n(micro ^ d, *both),
            lambda s, c, t, d=d: (s - s % 2 + t % 2, c, 2 * ((t // 2) ^ d) + s % 2),
        )
        for d in range(2)
    ]
    twos = scatter_finish(twos, twos_got, "x", 1)
    thirds = scatter_finish(thirds, thirds_got, "y", 1)
    pieces = jnp.concatenate([twos, thirds], axis=-1).reshape(2, 2, rows, -1)
    theirs = swap(lax.dynamic_index_in_dim(pieces, 1 - core, 1, False), "shard", 1)
    ours = lax.dynamic_index_in_dim(pieces, core, 1, False)
    pieces = by_core(ours, theirs, 0)
    wgrad_sum, pieces = tie(wgrad_sum, pieces)
    parts = [lax.dynamic_index_in_dim(pieces, group ^ d, 0, False) for d in range(4)]
    parts = parts[:1] + [swap(parts[d], "tp", d) for d in range(1, 4)]
    *parts, arrived[0], arrived[1] = tie(*parts, *arrived)
    outer_grad = wgrad_sum[:rows].astype(f32).T
    inner_grad = wgrad_sum[rows : 2 * rows].astype(f32)
    small = wgrad_sum[2 * rows :].reshape(rows, -1)
    embeddings = jnp.stack([lax.select_n((group % 2) ^ m, *emb_got) for m in range(2)])
    embeddings = embeddings.reshape(2, 1, quarter, -1)
    grad_tokens = jnp.stack([lax.select_n(m ^ micro, *arrived) for m in range(2)])
    grad_tokens = grad_tokens.reshape(2, 1, length, own_cols).astype(f32)
    query_grad, key_grad, value_grad, output_grad, proj_grad, norm_grads = finish(parts, small)
    return (
        embeddings,
        grad_tokens,
        query_grad,
        key_grad,
        value_grad,
        output_grad,
        norm_grads[0],
        norm_grads[1],
        inner_grad,
        outer_grad,
        norm_grads[2],
        norm_grads[3],
        proj_grad,
    )


def solution(mesh):
    rows = ("shard", "ctx")
    placed = (
        P(None, "shard", "ctx", None),
        P(None, "shard", "ctx"),
        P(rows, "tp"),
        P(rows, "tp"),
        P(rows, "tp"),
        P("tp", rows),
        P(rows),
        P(rows),
        P(rows, "tp"),
        P("tp", rows),
        P(rows),
        P(rows),
        P(rows, None),
        P(None, "shard", "ctx", None),
    )
    return jax.shard_map(
        per_device,
        mesh=mesh,
        in_specs=placed,
        out_specs=(
            P(None, "shard", ("ctx", "tp"), None),
            P(None, "shard", "ctx", "tp"),
            P(rows, "tp"),
            P(rows, "tp"),
            P(rows, "tp"),
            P("tp", rows),
            P(rows),
            P(rows),
            P(rows, "tp"),
            P("tp", rows),
            P(rows),
            P(rows),
            P(rows, None),
        ),
        check_vma=False,
    )
```
